32 devices in a mesh: rows: 8 (over z, x), tp: 4 (over y, core).
Axes of the slice: x: 2, y: 2, z: 4, core: 2. Of those that a mesh axis runs over, the one named last changes fastest.
Arguments:
- layer_input: bfloat16 [128, 256, 512], P('rows', 'tp'), may hold values from -6 to 6
- segment_labels: int32 [128, 256], P('rows'), may hold values from 0 to 31, never falling along the last dimension, each value on 1 to 24 neighbouring positions
- attend_weight: bfloat16 [3, 512, 512], P(None, None, 'tp'), may hold values from -0.25 to 0.25
- attend_bias: float32 [2, 512], P(None, 'tp'), may hold values from -3 to 3
- out_weight: bfloat16 [512, 512], P('tp'), may hold values from -0.75 to 0.75
- out_bias: float32 [512], replicated, may hold values from -2 to 2
- gain_attention: float32 [512], replicated, may hold values from 0.5 to 1.5
- shift_attention: float32 [512], replicated, may hold values from -2 to 2
- gain_feed: float32 [512], replicated, may hold values from 0.5 to 1.5
- shift_feed: float32 [512], replicated, may hold values from -2 to 2
- up_weight: bfloat16 [512, 2048], P(None, 'tp'), may hold values from -0.25 to 0.25
- up_bias: float32 [2048], P('tp'), may hold values from -3 to 3
- down_weight: bfloat16 [2048, 512], P('tp'), may hold values from -0.1875 to 0.1875
- down_bias: float32 [512], replicated, may hold values from -2 to 2
- pool_weight: bfloat16 [512, 2048], P(None, 'tp'), may hold values from -0.25 to 0.25
- pool_bias: float32 [2048], P('tp'), may hold values from -3 to 3
- hidden_grad: bfloat16 [128, 256, 512], P('rows', 'tp'), may hold values from -6 to 6
- embedding_grad: bfloat16 [128, 32, 2048], P('rows', None, 'tp'), may hold values from -6 to 6
Outputs:
- hidden: bfloat16 [128, 256, 512], P('rows', 'tp')
- embedding: bfloat16 [128, 32, 2048], P('rows', None, 'tp')
- input_grad: bfloat16 [128, 256, 512], P('rows', 'tp')
- attend_weight_grad: float32 [3, 512, 512], P(None, None, 'tp')
- attend_bias_grad: float32 [2, 512], P(None, 'tp')
- out_weight_grad: float32 [512, 512], P('tp')
- out_bias_grad: float32 [512], replicated
- gain_attention_grad: float32 [512], replicated
- shift_attention_grad: float32 [512], replicated
- gain_feed_grad: float32 [512], replicated
- shift_feed_grad: float32 [512], replicated
- up_weight_grad: float32 [512, 2048], P(None, 'tp')
- up_bias_grad: float32 [2048], P('tp')
- down_weight_grad: float32 [2048, 512], P('tp')
- down_bias_grad: float32 [512], replicated
- pool_weight_grad: float32 [512, 2048], P(None, 'tp')
- pool_bias_grad: float32 [2048], P('tp')
The draws below stay inside these ranges and needn't reach their ends.
Inputs may be any that keep to these rules, and one draw needn't show every extreme that they name: `segment_labels`: in each row labels never fall, start at 0, end at 31, and each label covers 1 to 24 consecutive slots; some segment covers exactly 24.
All inputs are finite; a program needn't handle non-finite values.
Results may differ from the reference program's by a relative error of at most 0.02.
Values may be sent and summed in bfloat16 or wider, within the bound.
A program may use at most 128 MiB of HBM per device.

```python
import math
import jax
import jax.numpy as jnp
import numpy as np
from jax import lax

D = 512
HEADS = 8
HEAD_DIM = 64
FF = 2048
OUT = 2048
SLOTS = 256
SEGS = 32
MOST = 24
ROWS = 128


def level_of(own_key, dims, split, least, largest):
    factor_of, own = 1.0, jax.random.fold_in(own_key, 6)
    for axis_at, shards_of in split:
        steps = jnp.exp(jax.random.uniform(jax.random.fold_in(own, axis_at), (shards_of,), jnp.float32, least / len(split), largest / len(split)))
        factor_of = factor_of * jnp.repeat(steps, dims[axis_at] // shards_of).reshape([-1 if axis == axis_at else 1 for axis in range(len(dims))])
    return factor_of


def profile(number_of, total, reach, lean):
    portions = [(1 << 20) // math.isqrt(grade ** lean) + 1 for grade in range(2, number_of + 1)]
    surplus, given = total - reach - (number_of - 1), [1] * (number_of - 1)
    while surplus > 0:
        free = [i for i in range(number_of - 1) if given[i] < reach]
        whole, remaining = sum([portions[i] for i in free]), surplus
        for i in free:
            extra = min(reach - given[i], max(1, remaining * portions[i] // whole), surplus)
            given[i] = given[i] + extra
            surplus = surplus - extra
    return np.array([reach] + given)


def uneven_parts(rng, number_of, total, reach, skew):
    if number_of == 2:
        one = jax.random.randint(rng, (), max(1, total - reach), min(reach, total - 1) + 1)
        return jnp.stack([one, total - one])
    lengths = jnp.asarray(profile(number_of, total, reach, skew), jnp.int32)
    couples = (number_of - 1) // 2
    source_of, taker = lengths[1:1 + 2 * couples:2], lengths[2:2 + 2 * couples:2]
    slack = jnp.minimum(source_of - 1, reach - taker)
    passed = jax.random.randint(jax.random.fold_in(rng, 1), (couples,), 0, 1 << 20) % (slack + 1)
    lengths = lengths.at[1:1 + 2 * couples:2].set(source_of - passed).at[2:2 + 2 * couples:2].set(taker + passed)
    return lengths[jax.random.permutation(jax.random.fold_in(rng, 2), number_of)]


def bell_draw(rng, extent, width, reach, cuts=(), kind=jnp.bfloat16):
    entries = width * jax.random.normal(rng, extent, jnp.float32)
    if cuts:
        entries = entries * level_of(rng, extent, cuts, -0.22, 0.18)
    return jnp.clip(entries, -reach, reach).astype(kind)


def setup_inputs(seed: int = 0) -> dict:
    seeds = jax.random.split(jax.random.key(seed), 19)
    return {
        "layer_input": bell_draw(seeds[0], (ROWS, SLOTS, D), 1.0, 6.0, ((0, 8), (1, 4))),
        "segment_labels": jax.vmap(lambda own: jnp.searchsorted(jnp.cumsum(uneven_parts(own, SEGS, SLOTS, MOST, 2)), jnp.arange(SLOTS), side="right"))(jax.random.split(seeds[1], ROWS)).reshape((ROWS, SLOTS)).astype(jnp.int32),
        "attend_weight": bell_draw(seeds[2], (3, D, D), D ** -0.5, 0.25, ((2, 4),)),
        "attend_bias": bell_draw(seeds[3], (2, D), 0.5, 3.0, ((1, 4),), jnp.float32),
        "out_weight": bell_draw(seeds[4], (D, D), (D // 8) ** -0.5, 0.75, ((0, 4),)),
        "out_bias": bell_draw(seeds[5], (D,), 0.3, 2.0, (), jnp.float32),
        "gain_attention": jnp.clip(1.0 + 0.1 * jax.random.normal(seeds[6], (D,), jnp.float32), 0.5, 1.5),
        "shift_attention": bell_draw(seeds[7], (D,), 0.3, 2.0, (), jnp.float32),
        "gain_feed": jnp.clip(1.0 + 0.1 * jax.random.normal(seeds[8], (D,), jnp.float32), 0.5, 1.5),
        "shift_feed": bell_draw(seeds[9], (D,), 0.3, 2.0, (), jnp.float32),
        "up_weight": bell_draw(seeds[10], (D, FF), D ** -0.5, 0.25, ((1, 4),)),
        "up_bias": bell_draw(seeds[11], (FF,), 0.5, 3.0, ((0, 4),), jnp.float32),
        "down_weight": bell_draw(seeds[12], (FF, D), (FF // 2) ** -0.5, 0.1875, ((0, 4),)),
        "down_bias": bell_draw(seeds[13], (D,), 0.3, 2.0, (), jnp.float32),
        "pool_weight": bell_draw(seeds[14], (D, OUT), D ** -0.5, 0.25, ((1, 4),)),
        "pool_bias": bell_draw(seeds[15], (OUT,), 0.5, 3.0, ((0, 4),), jnp.float32),
        "hidden_grad": bell_draw(seeds[16], (ROWS, SLOTS, D), 1.0, 6.0, ((0, 8), (1, 4))),
        "embedding_grad": bell_draw(seeds[17], (ROWS, SEGS, OUT), 1.0, 6.0, ((0, 8), (2, 4))),
    }


epsilon = 1e-05
highest = lax.Precision.HIGHEST

@jax.custom_vjp
def low(v):
    return lax.optimization_barrier(v.astype(jnp.bfloat16)).astype(jnp.float32)

@jax.custom_vjp
def low_back(v):
    return v

def low_keep(v):
    return (low(v), None)

def low_pass(kept, grad):
    return (grad,)

def back_keep(v):
    return (v, None)

def back_low(kept, grad):
    return (low(grad),)
low.defvjp(low_keep, low_pass)
low_back.defvjp(back_keep, back_low)

def round_both(values):
    return low(low_back(values))

def layer_norm(values, gain, shift):
    centred = values - lax.optimization_barrier(jnp.mean(values, axis=-1, keepdims=True))
    spread_sq = lax.optimization_barrier(jnp.mean(centred * centred, axis=-1, keepdims=True))
    return centred * lax.rsqrt(spread_sq + epsilon) * gain + shift

def layer_group(residual_in, labels, attend_weight, attend_bias, out_weight, out_bias, gain_attention, shift_attention, gain_feed, shift_feed, up_weight, up_bias, down_weight, down_bias, pool_weight, pool_bias):
    rows_here = residual_in.shape[0]
    norm_a = low(layer_norm(residual_in, gain_attention, shift_attention))
    projected = jnp.einsum('gsd,cde->cgse', norm_a, attend_weight, precision=highest)
    shape_heads = (rows_here, SLOTS, HEADS, HEAD_DIM)
    queries = round_both(projected[0] + attend_bias[0]).reshape(shape_heads)
    key_rows = round_both(projected[1]).reshape(shape_heads)
    value_rows = round_both(projected[2] + attend_bias[1]).reshape(shape_heads)
    scores = low_back(jnp.einsum('gqhd,gkhd->ghqk', queries, key_rows, precision=highest) * HEAD_DIM ** (-0.5))
    allowed = labels[:, None, :, None] == labels[:, None, None, :]
    weights = low(jax.nn.softmax(jnp.where(allowed, scores, -1e+30), axis=-1))
    attended = round_both(jnp.einsum('ghqk,gkhd->gqhd', weights, value_rows, precision=highest).reshape(rows_here, SLOTS, D))
    middle = residual_in + low_back(jnp.einsum('gse,ed->gsd', attended, out_weight, precision=highest) + out_bias)
    norm_f = low(layer_norm(middle, gain_feed, shift_feed))
    preact = low_back(jnp.einsum('gsd,df->gsf', norm_f, up_weight, precision=highest) + up_bias)
    activated = low(jax.nn.gelu(preact, approximate=True))
    residual_out = middle + low_back(jnp.einsum('gsf,fd->gsd', activated, down_weight, precision=highest) + down_bias)
    earlier = jnp.concatenate([labels[:, :1] - 1, labels[:, :-1]], axis=1)
    segment_range = jnp.arange(SEGS).astype(jnp.int32)
    select_first = ((labels[:, None, :] == segment_range[None, :, None]) & (labels != earlier)[:, None, :]).astype(jnp.float32)
    pooled = round_both(jnp.einsum('gcs,gsd->gcd', select_first, residual_out, precision=highest))
    embedding = jnp.einsum('gcd,do->gco', pooled, pool_weight, precision=highest) + pool_bias
    return (residual_out, embedding)

def reference(layer_input, segment_labels, attend_weight, attend_bias, out_weight, out_bias, gain_attention, shift_attention, gain_feed, shift_feed, up_weight, up_bias, down_weight, down_bias, pool_weight, pool_bias, hidden_grad, embedding_grad):
    params = tuple((tensor.astype(jnp.float32) for tensor in (attend_weight, attend_bias, out_weight, out_bias, gain_attention, shift_attention, gain_feed, shift_feed, up_weight, up_bias, down_weight, down_bias, pool_weight, pool_bias)))
    group_rows = 16
    group_count = layer_input.shape[0] // group_rows

    def regroup(tensor):
        return tensor.reshape((group_count, group_rows) + tensor.shape[1:])

    def accumulate(running, inputs):
        input_block, label_block, hidden_block, embed_block = inputs

        def forward(residual_in, *weights_all):
            return layer_group(residual_in, label_block, *weights_all)
        outputs, pullback = jax.vjp(forward, input_block, *params)
        gradients = pullback((hidden_block, embed_block))
        running = tuple((former + update for former, update in zip(running, gradients[1:])))
        return (running, (outputs[0].astype(jnp.bfloat16), outputs[1].astype(jnp.bfloat16), gradients[0].astype(jnp.bfloat16)))
    initial = tuple((jnp.zeros_like(tensor) for tensor in params))
    totals, (hidden, embedding, input_grad) = lax.scan(accumulate, initial, (regroup(layer_input.astype(jnp.float32)), regroup(segment_labels), regroup(hidden_grad.astype(jnp.float32)), regroup(embedding_grad.astype(jnp.float32))))
    return (hidden.reshape(-1, SLOTS, D), embedding.reshape(-1, SEGS, OUT), input_grad.reshape(-1, SLOTS, D), totals[0], totals[1], totals[2], totals[3], totals[4], totals[5], totals[6], totals[7], totals[8], totals[9], totals[10], totals[11], totals[12], totals[13])
```

```python
import functools
import math

import jax
import jax.numpy as jnp
from jax import lax
from jax.experimental import pallas as pl
from jax.experimental.pallas import tpu as pltpu
from jax.sharding import PartitionSpec as P

MESH = pl.DeviceIdType.MESH
HEAD_DIM = 64
HALO = 32
EPS = 1e-5
BF = jnp.bfloat16
F32 = jnp.float32
ROOT = math.sqrt(2.0 / math.pi)
CUBE = 0.044715
NAMES = ("dna", "dnb", "upa", "upb", "o", "q", "k", "v", "pl")
X_FIRST = ("dna", "upa")
PLAN = (
    (),
    (),
    (),
    (),
    (),
    (),
    (),
    (),
    (),
    (),
    ("qkv.step1", "gpool.step2", "wo.step1"),
    ("up.step1", "qkv.rx", "qkv.rz", "dn.step1", "wo.rx", "qkv.rxz"),
    ("wo.rz",),
    ("wo.rxz",),
    (),
    ("up.rx",),
    (),
    ("up.rz",),
    (),
    (),
    (),
    (),
    ("dn.rx", "up.rxz"),
    ("gpool.step3",),
    (),
    ("dn.rz",),
    (),
    (),
    ("dn.rxz",),
    (),
    (),
    (),
    (),
    (),
    (),
    (),
    (),
    (),
    ("pooled.step2",),
    (),
    (),
    ("dnb.y",),
    ("dna.x",),
    (),
    ("pooled.step3",),
    (),
    (),
    ("pl.x",),
    ("dna.y",),
    ("dnb.x",),
    (),
    ("upb.y",),
    ("upa.x",),
    (),
    (),
    ("dna.z", "o.y"),
    (),
    ("pl.z",),
    (),
    (),
    (),
    ("dnb.z", "upb.x"),
    ("dna.gz", "v.y", "o.x"),
    ("k.y",),
    ("upa.y",),
    ("q.y", "pl.gz"),
    ("upb.z", "v.x"),
    ("dnb.gz", "o.z"),
    ("dna.gx", "upa.z", "v.z", "k.x", "sm.s0", "pl.gx"),
    (),
    ("upb.gz", "q.x"),
    ("dnb.gx", "sm.s1", "k.z"),
    ("dna.end", "o.gz", "late.tp", "upa.gz", "v.gz", "pl.end", "q.z", "upb.gx", "k.gz", "dnb.end", "sm.s2", "o.gx", "late.rows", "upb.end", "upa.gx", "o.end", "v.gx", "q.gz", "k.gx", "upa.end", "v.end", "sm.s3", "k.end", "q.gx", "q.end"),
)


def mm(a, b):
    return jnp.dot(a, b, preferred_element_type=F32)


def mm_t(a, b):
    return lax.dot_general(a, b, (((1,), (1,)), ((), ())), preferred_element_type=F32)


def t_mm(a, b):
    return lax.dot_general(a, b, (((0,), (0,)), ((), ())), preferred_element_type=F32)


def normalize(values):
    mean = jnp.mean(values, axis=-1, keepdims=True)
    centred = values - mean
    spread = jnp.mean(centred * centred, axis=-1, keepdims=True)
    factor = lax.rsqrt(spread + EPS)
    return centred * factor, factor


def norm_back(grad, unit, factor, gain):
    scaled = grad * gain
    first = jnp.mean(scaled, axis=-1, keepdims=True)
    second = jnp.mean(scaled * unit, axis=-1, keepdims=True)
    return factor * (scaled - first - unit * second)


def total(values):
    return jnp.sum(values, axis=0, keepdims=True)


def layer_kernel(dims, *refs):
    (groups, RH, LS, D, FF, SEGS) = dims
    W = LS + 2 * HALO
    (x_in, lab_in, wqkv_in, ab_in, wo_in, v0_in, v1_in, v2_in, v3_in, v4_in, wup_in, bup_in, wdn_in, v5_in, wp_in, bp_in, hg_in, eg_in,
     hid_out, emb_out, ig_out, gdn_out, gup_out, go_out, gq_out, gk_out, gv_out, gpl_out, sm_out, late_out,
     x, hg, eg, mask, codes, wqkv, wo, wup, wdn, wp, shared, vec, bup,
     nw, q, k, v, p, at, mid, nf, act, dact, gma, gat, hid, gnc,
     halo_l, halo_r, halo_fl, halo_fr,
     gpt, gpr1, gpr2, gps, pt, pr1, pr2, ps, emb,
     smalls, sm_r, late, late_tp, late_rows,
     *tail) = refs
    tail = list(tail)
    sets = {}
    for name in NAMES:
        sets[name] = [tail.pop(0) for _ in range(4 if name == "pl" else 6)]
    if groups > 1:
        r5 = {name: tail.pop(0) for name in NAMES + ("sm", "late")}
    send_sems, recv_sems, local_sems = tail
    T = RH * LS
    BR = 4
    NB = RH // BR
    BT = BR * LS
    H2 = 4 * HEAD_DIM

    r, t = lax.axis_index("rows"), lax.axis_index("tp")
    core, ypos = t % 2, t // 2
    tc = t + 1 - 2 * core
    ty = (t + 2) % 4
    tdiag = 3 - t
    xpos = r % 2
    rx = r + 1 - 2 * xpos
    zpos = (r // 2) % 4
    base = (r // 8) * 8
    zpeers = [base + ((zpos + dz) % 4) * 2 + xpos for dz in (1, 2, 3)]
    quad = r % 4
    rz = r + 2 - 4 * (quad // 2)
    rxz = rz + 1 - 2 * xpos
    xzpeers = [base + ((zpos + dz) % 4) * 2 + 1 - xpos for dz in (1, 2, 3)]
    gpeers = [((r // 8 + dg) % groups) * 8 + r % 8 for dg in range(1, groups)]

    counter = [0]

    def remote(src, dst, dev):
        i = counter[0]
        counter[0] += 1
        return pltpu.make_async_remote_copy(
            src_ref=src, dst_ref=dst, send_sem=send_sems.at[i], recv_sem=recv_sems.at[i],
            device_id=dev, device_id_type=MESH)

    local_count = [0]

    def local(src, dst):
        i = local_count[0]
        local_count[0] += 1
        c = pltpu.make_async_copy(src, dst, local_sems.at[i])
        c.start()
        return c

    spot, steps = [0], {}

    def chain(name, *links):
        for label, fn, _ in links:
            steps[name + "." + label] = fn

    def live(*names):
        pass

    def take(i):
        for name in PLAN[i] if i < len(PLAN) else ():
            steps[name]()

    def point():
        spot[0] += 1
        take(spot[0] - 1)

    def must(*names):
        point()

    def run(name, count, body, polls=None):
        first = spot[0]
        spot[0] += count

        def step(b, carry):
            body(b)
            for i in range(count):
                if i in (polls or {}) or (first + i < len(PLAN) and PLAN[first + i]):
                    @pl.when(b == i)
                    def _():
                        if i in (polls or {}):
                            polls[i]()
                        take(first + i)
            return carry

        lax.fori_loop(0, count, step, 0)

    def once(name, fn):
        fn()
        point()

    pending = []

    def go(copy):
        copy.start()
        pending.append(copy)
        return copy

    load_x = local(x_in, x)
    load_wp = local(wp_in, wp)
    load_eg = local(eg_in, eg)
    barrier = pltpu.get_barrier_semaphore()
    friends = [(r, tc), (r, ty), (r, tdiag), (rx, t)] + [(zp, t) for zp in zpeers + xzpeers] + [(gp_, t) for gp_ in gpeers]
    for dev in friends:
        pl.semaphore_signal(barrier, inc=1, device_id=dev, device_id_type=MESH)
    pl.semaphore_wait(barrier, len(friends))

    shared[t, 0:2, :] = ab_in[...]
    shared[t, 2:6, :] = bup_in[...]
    bias_moves = [go(remote(shared.at[t], shared.at[t], (r, dev))) for dev in (tc, ty, tdiag)]
    full = {"qkv": wqkv, "wo": wo, "up": wup, "dn": wdn}
    given = {"qkv": wqkv_in, "wo": wo_in, "up": wup_in, "dn": wdn_in}

    def shard(name, s, piece=None):
        ref = full[name]
        if name in ("qkv", "up"):
            rows_ = pl.ds(0, D) if piece is None else pl.ds(piece * (D // 4), D // 4)
            if name == "qkv":
                return ref.at[:, rows_, pl.ds(pl.multiple_of(s * 128, 128), 128)]
            return ref.at[rows_, pl.ds(pl.multiple_of(s * (FF // 4), 128), FF // 4)]
        n = (D if name == "wo" else FF) // 4
        if piece is None:
            return ref.at[pl.ds(s * n, n)]
        return ref.at[pl.ds(s * n + piece * (n // 4), n // 4)]

    def own_piece(name, piece):
        ref = given[name]
        if name == "qkv":
            return ref.at[:, pl.ds(piece * (D // 4), D // 4)]
        n = ref.shape[0] // 4
        return ref.at[pl.ds(piece * n, n)]

    class Gather:
        def __init__(self, name):
            self.name = name
            self.y = go(remote(own_piece(name, quad), shard(name, t, quad), (r, ty)))
            self.c = go(remote(given[name], shard(name, t), (r, tc)))
            self.loc = local(given[name], shard(name, t))
            mine = shard(name, ty, quad)
            self.x = [remote(mine, mine, (dev, t)) for dev in (rx, rz, rxz)]
            self.f = [remote(mine, mine, (r, tc))]
            for dev in (rx, rz, rxz):
                got = shard(name, ty, dev % 4)
                self.f.append(remote(got, got, (r, tc)))
            chain(name, ("step1", self.step1, [self.y]), ("rx", lambda: self.step2(0), [self.x[0]]),
                  ("rz", lambda: self.step2(1), [self.x[1]]), ("rxz", lambda: self.step2(2), [self.x[2]]))

        def step1(self):
            self.y.wait_recv()
            for c in self.x:
                go(c)
            go(self.f[0])

        def step2(self, i):
            self.x[i].wait_recv()
            go(self.f[i + 1])

        def near(self):
            self.loc.wait()
            self.c.wait_recv()

        def ready(self):
            for c in self.f:
                c.wait_recv()

    w_qkv = Gather("qkv")
    w_o = Gather("wo")
    w_up = Gather("up")
    w_dn = Gather("dn")
    live("qkv", "wo", "up", "dn")

    for i, ref in enumerate((v0_in, v1_in, v2_in, v3_in, v4_in, v5_in)):
        vec[i:i + 1, :] = ref[...].reshape(1, D)

    def row(i):
        return vec[i:i + 1, :]

    load_x.wait()

    class Halo:
        def __init__(self, pairs):
            self.left = [remote(a, b, (r, (t + 3) % 4)) for a, b, _, _ in pairs]
            self.right = [remote(c, d, (r, (t + 1) % 4)) for _, _, c, d in pairs]

        def send(self, i):
            pl.when(t > 0)(self.left[i].start)
            pl.when(t < 3)(self.right[i].start)

        def wait(self, i):
            pl.when(t > 0)(self.right[i].wait_recv)
            pl.when(t < 3)(self.left[i].wait_recv)

        def sent(self):
            for i in range(2):
                pl.when(t > 0)(self.left[i].wait_send)
                pl.when(t < 3)(self.right[i].wait_send)

    HR = RH // 2

    def edges(i, first):
        return nw.at[pl.ds(i * HR, HR), pl.ds(first, HALO)]

    halo = Halo([(edges(i, HALO), edges(i, HALO + LS), edges(i, LS), edges(i, 0)) for i in range(2)])

    def ln1(b):
        xs = x[pl.ds(b * BT, BT), :].astype(F32)
        unit, _ = normalize(xs)
        out = (unit * row(1) + row(2)).astype(BF)
        nw[pl.ds(b * BR, BR), HALO:HALO + LS, :] = out.reshape(BR, LS, D)

    run("ln1", NB, ln1, {NB // 2 - 1: lambda: halo.send(0), NB - 1: lambda: halo.send(1)})

    @pl.when(t == 0)
    def _():
        nw[:, 0:HALO, :] = jnp.zeros((RH, HALO, D), BF)

    @pl.when(t == 3)
    def _():
        nw[:, HALO + LS:W, :] = jnp.zeros((RH, HALO, D), BF)

    PH = RH * SEGS // 2
    load_wp.wait()
    load_eg.wait()

    class PoolSum:
        def __init__(self, name, terms, r1, r2, out):
            self.terms, self.r1, self.r2, self.out = terms, r1, r2, out
            mine, theirs = pl.ds(core * PH, PH), pl.ds((1 - core) * PH, PH)
            self.mine = mine
            self.a = remote(terms.at[theirs], r1, (r, tc))
            self.b = remote(terms.at[mine], r2, (r, ty))
            self.c = remote(out.at[mine], out.at[mine], (r, tc))
            chain(name, ("step2", self.step2, [self.a]), ("step3", self.step3, [self.b]))

        def step1(self):
            go(self.a)

        def step2(self):
            self.a.wait_recv()
            self.terms[self.mine, :] = (self.terms[self.mine, :].astype(F32) + self.r1[...].astype(F32)).astype(BF)
            go(self.b)

        def step3(self):
            self.b.wait_recv()
            self.out[self.mine, :] = (self.terms[self.mine, :].astype(F32) + self.r2[...].astype(F32)).astype(BF)
            go(self.c)

        def ready(self):
            self.c.wait_recv()

    gpool = PoolSum("gpool", gpt, gpr1, gpr2, gps)
    pooled = PoolSum("pooled", pt, pr1, pr2, ps)
    smalls[...] = jnp.zeros(smalls.shape, F32)

    def pool_back():
        smalls[pl.ds(12 + t, 1), :] = total(eg[...].astype(F32))
        gpt[...] = mm_t(eg[...], wp[...]).astype(BF)

    once("pool_back", pool_back)
    gpool.step1()

    load_hg = local(hg_in, hg)
    w_qkv.near()
    live("gpool")
    point()

    labels = lab_in[...]
    SL = labels.shape[1]
    window = pltpu.roll(labels, (SL + HALO - t * LS) % SL, 1)[:, 0:W].astype(F32)
    own_lab = pltpu.roll(labels, (SL - t * LS) % SL, 1)[:, 0:W].astype(F32)
    before = pltpu.roll(labels, (SL + 1 - t * LS) % SL, 1)[:, 0:W].astype(F32)
    codes[...] = jnp.where(own_lab == before, -1.0, own_lab)
    columns = jnp.transpose(own_lab)
    for i in range(RH):
        mask[i * LS:(i + 1) * LS, :] = jnp.where(columns[0:LS, i:i + 1] == window[i:i + 1, :], 0.0, -1e30)

    for copy in bias_moves:
        copy.wait_recv()
    for s in range(4):
        for i in range(2):
            vec[6 + i:7 + i, s * 128:(s + 1) * 128] = shared[s, i:i + 1, :]
        for i in range(4):
            bup[s:s + 1, i * 128:(i + 1) * 128] = shared[s, 2 + i:3 + i, :]

    point()

    near = pl.ds(pl.multiple_of(ypos * H2, H2), H2)
    far = pl.ds(pl.multiple_of((1 - ypos) * H2, H2), H2)

    def project_own(cols, b):
        own = nw[pl.ds(b * BR, BR), HALO:HALO + LS, :].reshape(BT, D)
        q[pl.ds(b * BT, BT), cols] = ((mm(own, wqkv[0, :, cols]) + vec[6:7, cols]) * (HEAD_DIM ** -0.5)).astype(BF)
        ks = mm(own, wqkv[1, :, cols]).astype(BF)
        vs = (mm(own, wqkv[2, :, cols]) + vec[7:8, cols]).astype(BF)
        k[pl.ds(b * BR, BR), HALO:HALO + LS, cols] = ks.reshape(BR, LS, H2)
        v[pl.ds(b * BR, BR), HALO:HALO + LS, cols] = vs.reshape(BR, LS, H2)

    def project_halo(b):
        rows_ = pl.ds(b * BR, BR)
        both = jnp.concatenate([nw[rows_, 0:HALO, :], nw[rows_, HALO + LS:W, :]], axis=0).reshape(BR * 2 * HALO, D)
        ks = mm(both, wqkv[1]).astype(BF).reshape(2, BR, HALO, D)
        vs = (mm(both, wqkv[2]) + row(7)).astype(BF).reshape(2, BR, HALO, D)
        k[rows_, 0:HALO, :] = ks[0]
        k[rows_, HALO + LS:W, :] = ks[1]
        v[rows_, 0:HALO, :] = vs[0]
        v[rows_, HALO + LS:W, :] = vs[1]

    lane = lax.broadcasted_iota(jnp.int32, (1, H2), 1) // HEAD_DIM
    heads = [(lane == h).astype(F32).astype(BF) for h in range(4)]

    def spread_heads(block):
        return jnp.concatenate([block * heads[h] for h in range(4)], axis=0)

    def merge_heads(stack):
        parts = [stack[h * LS:(h + 1) * LS, :] for h in range(4)]
        out = jnp.where(lane == 0, parts[0], parts[1])
        out = jnp.where(lane == 2, parts[2], out)
        return jnp.where(lane == 3, parts[3], out)

    def attend(i):
        work = [(i * 2 + n, half) for n in range(2) for half in range(2)]
        sides = [slice(half * H2, (half + 1) * H2) for _, half in work]
        scores = []
        for (n, _), c in zip(work, sides):
            m1 = mask[pl.ds(n * LS, LS), :]
            qs = spread_heads(q[pl.ds(n * LS, LS), c])
            scores.append(mm_t(qs, k[n, :, c]) + jnp.concatenate([m1] * 4, axis=0))
        tops = [jnp.max(sc, axis=-1, keepdims=True) for sc in scores]
        es = [jnp.exp(sc - top) for sc, top in zip(scores, tops)]
        inv = [1.0 / jnp.sum(e, axis=-1, keepdims=True) for e in es]
        ws = [(e * f).astype(BF) for e, f in zip(es, inv)]
        outs = []
        for (n, half), c, w in zip(work, sides, ws):
            p[pl.ds((n * 2 + half) * 4 * LS, 4 * LS), :] = w
            outs.append(mm(w, v[n, :, c]))
        for (n, _), c, o in zip(work, sides, outs):
            at[pl.ds(n * LS, LS), c] = merge_heads(o).astype(BF)

    HB = NB // 2
    AB = RH // 4
    run("own_near", NB, lambda b: project_own(near, b))
    must("qkv")
    w_qkv.ready()
    run("own_far", NB, lambda b: project_own(far, b))
    halo.wait(0)
    run("halo_all", HB, project_halo)
    run("attend", AB, attend)
    halo.wait(1)
    run("halo_all", HB, lambda b: project_halo(b + HB))
    run("attend", AB, lambda i: attend(i + AB))
    must("wo", "up", "dn")
    for w in (w_o, w_up, w_dn):
        w.near()
        w.ready()

    FC = FF // 4
    ids = lax.broadcasted_iota(jnp.int32, (SEGS, LS), 0).astype(F32)

    def chosen(n):
        return (ids == codes[pl.ds(n, 1), 0:LS]).astype(F32).astype(BF)

    def feed(b):
        rows_ = pl.ds(b * BT, BT)
        middle = x[rows_, :].astype(F32) + (mm(at[rows_, :], wo[...]) + row(0))
        mid[rows_, :] = middle
        unit, _ = normalize(middle)
        normed = (unit * row(3) + row(4)).astype(BF)
        nf[rows_, :] = normed
        acc = middle + row(5)
        for j in range(4):
            cols = slice(j * FC, (j + 1) * FC)
            u = mm(normed, wup[:, cols]) + bup[j:j + 1, :]
            u2 = u * u
            th = jnp.tanh(ROOT * u * (1.0 + CUBE * u2))
            half_up = 0.5 * (1.0 + th)
            a = (u * half_up).astype(BF)
            act[rows_, cols] = a
            dact[rows_, cols] = (half_up + u * half_up * (1.0 - th) * (ROOT + (3.0 * CUBE * ROOT) * u2)).astype(BF)
            acc = acc + mm(a, wdn[cols, :])
        low = acc.astype(BF)
        hid[rows_, :] = low
        for n in range(BR):
            first = chosen(b * BR + n)
            pt[pl.ds((b * BR + n) * SEGS, SEGS), :] = mm(first, low[n * LS:(n + 1) * LS, :]).astype(BF)

    run("feed", NB, feed)
    store_hid = local(hid, hid_out)
    pooled.step1()
    live("pooled")
    must("gpool")
    gpool.ready()
    load_hg.wait()

    def place(b):
        rows_ = pl.ds(b * BT, BT)
        put = [t_mm(chosen(b * BR + n), gps[pl.ds((b * BR + n) * SEGS, SEGS), :]) for n in range(BR)]
        g = hg[rows_, :].astype(F32) + jnp.concatenate(put, axis=0)
        low = g.astype(BF)
        hg[rows_, :] = low
        smalls[5:6, :] += total(low.astype(F32))

    run("place", NB, place)
    gb = hg

    class Reduce:
        def __init__(self, name, g, r1, r2, r3, r4, o):
            self.name, self.g, self.r1, self.r2, self.r3, self.r4, self.o = name, g, r1, r2, r3, r4, o
            own = g
            if r1 is not None:
                self.a1 = remote(g.at[1 - core, 1 - ypos], r1.at[1 - ypos], (r, tc))
                self.a2 = remote(g.at[1 - core, ypos], r1.at[ypos], (r, tc))
                own = g.at[core, ypos]
            self.own = own
            self.middle()
            self.d = [remote(own.at[(zpos + dz) % 4, xpos], r4.at[dz - 1], (zpeers[dz - 1], t)) for dz in (1, 2, 3)]
            if groups > 1:
                self.m = [remote(o.at[zpos, xpos], r5[name].at[i], (gpeers[i], t)) for i in range(groups - 1)]
            self.e = [remote(o.at[zpos, xpos], o.at[zpos, xpos], (zpeers[dz - 1], t)) for dz in (1, 2, 3)]
            self.f = remote(o.at[:, xpos], o.at[:, xpos], (rx, t))
            ends = [("gz", self.gather_z, self.d), ("gx", self.gather_x, self.e), ("end", self.finish, [self.f])]
            chain(name, *self.links(), *ends)

        def links(self):
            if self.r1 is None:
                return [("x", self.x, []), ("z", self.z, [self.c])]
            return [("y", self.y, [self.a1]), ("x", self.x, [self.a2, self.b]), ("z", self.z, [self.c])]

        def middle(self):
            if self.r1 is not None:
                self.b = remote(self.g.at[core, 1 - ypos], self.r2, (r, ty))
            self.c = remote(self.own.at[:, 1 - xpos], self.r3, (rx, t))

        def core1(self):
            go(self.a1)

        def core2(self):
            go(self.a2)

        def y(self):
            self.a1.wait_recv()
            self.g[core, 1 - ypos] = (self.g[core, 1 - ypos].astype(F32) + self.r1[1 - ypos].astype(F32)).astype(BF)
            go(self.b)

        def part(self, i):
            acc = self.own[:, i].astype(F32)
            if self.r1 is not None:
                acc = acc + self.r1[ypos, :, i].astype(F32) + self.r2[:, i].astype(F32)
            return acc

        def x(self):
            if self.r1 is not None:
                self.a2.wait_recv()
                self.b.wait_recv()
                self.own[:, 1 - xpos] = self.part(1 - xpos).astype(BF)
            go(self.c)

        def z(self):
            self.c.wait_recv()
            self.own[:, xpos] = (self.part(xpos) + self.r3[...].astype(F32)).astype(BF)
            for c in self.d:
                go(c)

        def gather_z(self):
            for c in self.d:
                c.wait_recv()
            acc = self.own[zpos, xpos].astype(F32)
            for i in range(3):
                acc = acc + self.r4[i].astype(F32)
            self.o[zpos, xpos] = acc.astype(BF)
            if groups > 1:
                for c in self.m:
                    c.start()
                for c in self.m:
                    c.wait()
                acc = self.o[zpos, xpos].astype(F32)
                for i in range(groups - 1):
                    acc = acc + r5[self.name][i].astype(F32)
                self.o[zpos, xpos] = acc.astype(BF)
            for c in self.e:
                go(c)

        def gather_x(self):
            for c in self.e:
                c.wait_recv()
            go(self.f)

        def finish(self):
            self.f.wait_recv()
            stores.append(local(self.o, final[self.name]))

    class ReduceX(Reduce):
        def links(self):
            return [("x", self.x, [self.a1, self.a2]), ("y", self.y, [self.c]), ("z", self.z, [self.b])]

        def middle(self):
            self.c = remote(self.g.at[core, :, :, 1 - xpos], self.r3, (rx, t))
            self.b = remote(self.g.at[core, 1 - ypos, :, xpos], self.r2, (r, ty))

        def x(self):
            self.a1.wait_recv()
            self.a2.wait_recv()
            both = self.g[core, :, :, 1 - xpos].astype(F32) + self.r1[:, :, 1 - xpos].astype(F32)
            self.g[core, :, :, 1 - xpos] = both.astype(BF)
            go(self.c)

        def half(self, i):
            return self.g[core, i, :, xpos].astype(F32) + self.r1[i, :, xpos].astype(F32) + self.r3[i].astype(F32)

        def y(self):
            self.c.wait_recv()
            self.g[core, 1 - ypos, :, xpos] = self.half(1 - ypos).astype(BF)
            go(self.b)

        def z(self):
            self.b.wait_recv()
            self.g[core, ypos, :, xpos] = (self.half(ypos) + self.r2[...].astype(F32)).astype(BF)
            for c in self.d:
                go(c)

    HC = D // 2

    def halves(out, i):
        return out.at[:, :, :, pl.ds(i * HC, HC)]

    final = {"dna": halves(gdn_out, 0), "dnb": halves(gdn_out, 1), "upa": halves(gup_out, 0), "upb": halves(gup_out, 1),
             "o": go_out, "q": gq_out, "k": gk_out, "v": gv_out, "pl": gpl_out}
    stores = []
    red = {}
    for name in NAMES:
        held = sets[name]
        if name == "pl":
            held = [held[0], None, None] + held[1:]
        red[name] = (ReduceX if name in X_FIRST else Reduce)(name, *held)

    def split(names, cs, ys, val):
        for i, name in enumerate(names):
            g = sets[name][0]
            g[cs, ys] = val[:, i * HC:(i + 1) * HC].astype(BF).reshape(g.shape[2:])

    def place_of(i):
        return (core + 1 + i // 2) % 2, (ypos + 1 + i) % 2

    def down_grad(i):
        cs, ys = place_of(i)
        val = t_mm(act[:, pl.ds(pl.multiple_of((ys * 2 + cs) * FC, FC), FC)], gb[...])
        split(("dna", "dnb"), cs, ys, val)

    def near_cores(*names):
        return lambda: [red[n].core1() for n in names], lambda: [red[n].core2() for n in names]

    send1, send2 = near_cores("dna", "dnb")
    run("down_grad", 4, down_grad, {0: send1, 1: send2, 2: lambda: live("dnb"), 3: lambda: live("dna")})

    def feed_back(b):
        rows_ = pl.ds(b * BT, BT)
        g = gb[rows_, :]
        acc = jnp.zeros((BT, D), F32)
        for j in range(4):
            cols = slice(j * FC, (j + 1) * FC)
            ga = mm_t(g, wdn[cols, :])
            gp = (ga * dact[rows_, cols].astype(F32)).astype(BF)
            dact[rows_, cols] = gp
            smalls[8 + j:9 + j, :] += total(gp.astype(F32))
            acc = acc + mm_t(gp, wup[:, cols])
        unit, factor = normalize(mid[rows_, :])
        smalls[3:4, :] += total(acc * unit)
        smalls[4:5, :] += total(acc)
        gm = g.astype(F32) + norm_back(acc, unit, factor, row(3))
        mid[rows_, :] = gm
        low = gm.astype(BF)
        gma[rows_, :] = low
        smalls[0:1, :] += total(low.astype(F32))
        gat[rows_, :] = mm_t(low, wo[...]).astype(BF)

    run("feed_back", NB, feed_back)
    must("pooled")
    pooled.ready()

    def embed():
        emb[...] = (mm(ps[...], wp[...]) + bp_in[...].reshape(1, D)).astype(BF)
        sets["pl"][0][...] = t_mm(ps[...], eg[...]).astype(BF).reshape(sets["pl"][0].shape)
        live("pl")

    once("embed", embed)
    store_emb = local(emb, emb_out)

    def up_grad(i):
        cs, ys = place_of(i)
        val = t_mm(nf[...], dact[:, pl.ds(pl.multiple_of((ys * 2 + cs) * FC, FC), FC)])
        split(("upa", "upb"), cs, ys, val)

    send3, send4 = near_cores("upa", "upb")
    run("up_grad", 4, up_grad, {0: send3, 1: send4, 2: lambda: live("upb"), 3: lambda: live("upa")})

    def out_grad():
        val = t_mm(at[...], gma[...]).astype(BF)
        for s in range(4):
            g = sets["o"][0]
            g[s % 2, s // 2] = val[s * (D // 4):(s + 1) * (D // 4), :].reshape(g.shape[2:])
        red["o"].core1()
        red["o"].core2()
        live("o")

    once("out_grad", out_grad)

    def attend_back(i):
        work = [(i * 2 + n, half) for n in range(2) for half in range(2)]
        sides = [slice(half * H2, (half + 1) * H2) for _, half in work]
        qss = [spread_heads(q[pl.ds(n * LS, LS), c]) for (n, _), c in zip(work, sides)]
        gss = [spread_heads(gat[pl.ds(n * LS, LS), c]) for (n, _), c in zip(work, sides)]
        ws = [p[pl.ds((n * 2 + half) * 4 * LS, 4 * LS), :] for n, half in work]
        gws = [mm_t(g, v[n, :, c]) for g, (n, _), c in zip(gss, work, sides)]
        wfs = [w.astype(F32) for w in ws]
        prods = [w * g for w, g in zip(wfs, gws)]
        sums = [jnp.sum(pr, axis=-1, keepdims=True) for pr in prods]
        dss = [(pr - w * sm).astype(BF) for pr, w, sm in zip(prods, wfs, sums)]
        dvs = [t_mm(w, g).astype(BF) for w, g in zip(ws, gss)]
        dqs = [mm(ds, k[n, :, c]) for ds, (n, _), c in zip(dss, work, sides)]
        dks = [t_mm(ds, qq).astype(BF) for ds, qq in zip(dss, qss)]
        for (n, _), c, dq, dk, dv in zip(work, sides, dqs, dks, dvs):
            q[pl.ds(n * LS, LS), c] = (merge_heads(dq) * (HEAD_DIM ** -0.5)).astype(BF)
            k[n, :, c] = dk
            v[n, :, c] = dv

    run("attend_back", RH // 2, attend_back)

    back = Halo([tuple(ref.at[pl.ds(i * HR, HR)] for ref in (halo_l, halo_fr, halo_r, halo_fl)) for i in range(2)])

    def norm_grad(b):
        keys = pl.ds(b * BR, BR)
        dqs = q[pl.ds(b * BT, BT), :]
        dks, dvs = k[keys].reshape(BR * W, D), v[keys].reshape(BR * W, D)
        smalls[6:7, :] += total(dqs.astype(F32))
        smalls[7:8, :] += total(dvs.astype(F32))
        win = (mm_t(dks, wqkv[1]) + mm_t(dvs, wqkv[2])).reshape(BR, W, D)
        own = win[:, HALO:HALO + LS, :].reshape(BT, D) + mm_t(dqs, wqkv[0])
        gnc[pl.ds(b * BT, BT), :] = own
        halo_l[keys] = win[:, 0:HALO, :].astype(BF)
        halo_r[keys] = win[:, HALO + LS:W, :].astype(BF)

    def put_at(g, val):
        low = val.astype(BF)
        for s in range(4):
            g[s % 2, s // 2] = low[:, s * 128:(s + 1) * 128].reshape(g.shape[2:])

    def put_value():
        put_at(sets["v"][0], t_mm(nw[...].reshape(RH * W, D), v[...].reshape(RH * W, D)))
        red["v"].core1()
        red["v"].core2()
        live("v")

    def put_key():
        put_at(sets["k"][0], t_mm(nw[...].reshape(RH * W, D), k[...].reshape(RH * W, D)))
        red["k"].core1()
        red["k"].core2()
        live("k")

    def put_query():
        put_at(sets["q"][0], t_mm(nw[:, HALO:HALO + LS, :].reshape(T, D), q[...]))
        red["q"].core1()
        red["q"].core2()
        live("q")

    once("put_v", put_value)
    once("put_k", put_key)
    once("put_q", put_query)
    run("norm_grad", NB, norm_grad, {HB - 1: lambda: back.send(0), NB - 1: lambda: back.send(1)})

    @pl.when(t == 0)
    def _():
        halo_fl[...] = jnp.zeros(halo_fl.shape, BF)

    @pl.when(t == 3)
    def _():
        halo_fr[...] = jnp.zeros(halo_fr.shape, BF)

    class Small:
        name = "sm"

        def __init__(self):
            self.copies = [[remote(smalls, sm_r.at[0], (r, tc))], [remote(smalls, sm_r.at[1], (r, ty))],
                           [remote(smalls, sm_r.at[2], (rx, t))],
                           [remote(smalls, sm_r.at[2 + dz], (zpeers[dz - 1], t)) for dz in (1, 2, 3)]]
            chain("sm", *[("s" + str(i), functools.partial(self.step, i), self.copies[i]) for i in range(4)])

        def send(self, i):
            for c in self.copies[i]:
                c.start()

        def step(self, i):
            for c in self.copies[i]:
                c.wait()
            if i < 3:
                smalls[...] += sm_r[i]
                self.send(i + 1)
            else:
                smalls[...] += sm_r[3] + sm_r[4] + sm_r[5]
                across(smalls, "sm")
                stores.append(local(smalls, sm_out))

    class Late:
        name = "late"

        def __init__(self):
            self.a = [remote(late, late_tp.at[i], (r, dev)) for i, dev in enumerate((tc, ty, tdiag))]
            self.b = [remote(late, late_rows.at[i], (dev, t)) for i, dev in enumerate([rx] + zpeers + xzpeers)]
            chain("late", ("tp", self.over_tp, self.a), ("rows", self.over_rows, self.b))

        def over_tp(self):
            for c in self.a:
                c.wait()
            late[...] += late_tp[0] + late_tp[1] + late_tp[2]
            for c in self.b:
                c.start()

        def over_rows(self):
            for c in self.b:
                c.wait()
            for i in range(7):
                late[...] += late_rows[i]
            across(late, "late")
            stores.append(local(late, late_out))

    def across(ref, name):
        moves = [remote(ref, r5[name].at[i], (gpeers[i], t)) for i in range(groups - 1)]
        for c in moves:
            c.start()
        for c in moves:
            c.wait()
        for i in range(groups - 1):
            ref[...] += r5[name][i]

    small, lates = Small(), Late()
    small.send(0)
    live("sm")
    late[...] = jnp.zeros(late.shape, F32)

    def ln1_back(b):
        rows_ = pl.ds(b * BT, BT)
        grp = pl.ds(b * BR, BR)
        g = gnc[rows_, :].reshape(BR, LS, D)
        g = jnp.concatenate([g[:, 0:HALO, :] + halo_fl[grp].astype(F32), g[:, HALO:LS, :] + halo_fr[grp].astype(F32)], axis=1)
        g = g.reshape(BT, D)
        unit, factor = normalize(x[rows_, :].astype(F32))
        late[0:1, :] += total(g * unit)
        late[1:2, :] += total(g)
        nf[rows_, :] = (mid[rows_, :] + norm_back(g, unit, factor, row(1))).astype(BF)

    back.wait(0)
    run("ln1_back", HB, ln1_back)
    back.wait(1)
    run("ln1_back", HB, lambda b: ln1_back(b + HB))
    store_ig = local(nf, ig_out)
    for c in lates.a:
        c.start()
    live("late")
    must(*NAMES, "sm", "late")
    for c in pending:
        c.wait_send()
    halo.sent()
    back.sent()
    for c in stores + [store_hid, store_emb, store_ig]:
        c.wait()


def per_device(rows_size, layer_input, segment_labels, attend_weight, attend_bias, out_weight, out_bias, gain_attention,
               shift_attention, gain_feed, shift_feed, up_weight, up_bias, down_weight, down_bias, pool_weight, pool_bias,
               hidden_grad, embedding_grad):
    RH, LS, D = layer_input.shape
    SEGS = embedding_grad.shape[1]
    OC = pool_weight.shape[1]
    FS = up_weight.shape[1]
    FF = FS * 4
    W = LS + 2 * HALO
    T = RH * LS
    NB = RH // 4
    groups = rows_size // 8
    t = lax.axis_index("tp")
    part = (D // 8, D // 4)
    chunk = {"dna": (FS // 8, D // 2), "dnb": (FS // 8, D // 2), "upa": (D // 8, FS // 2), "upb": (D // 8, FS // 2), "o": (D // 32, D), "q": part, "k": part, "v": part, "pl": (D // 8, OC)}
    any_, vmem = pl.BlockSpec(memory_space=pl.ANY), pl.BlockSpec(memory_space=pltpu.VMEM)

    def buf(*shape, dtype=BF):
        return pltpu.VMEM(shape, dtype)

    scratch = [
        buf(T, D), buf(T, D), buf(RH * SEGS, OC), buf(T, W, dtype=F32), buf(RH, W, dtype=F32),
        buf(3, D, D), buf(D, D), buf(D, FF), buf(FF, D), buf(D, OC), buf(4, 8, 128, dtype=F32), buf(8, D, dtype=F32), buf(4, FS, dtype=F32),
        buf(RH, W, D), buf(T, D), buf(RH, W, D), buf(RH, W, D), buf(RH * 2 * 4 * LS, W), buf(T, D), buf(T, D, dtype=F32),
        buf(T, D), buf(T, FF), buf(T, FF), buf(T, D), buf(T, D), buf(T, D), buf(T, D, dtype=F32),
        buf(RH, HALO, D), buf(RH, HALO, D), buf(RH, HALO, D), buf(RH, HALO, D),
    ]
    for _ in range(2):
        scratch += [buf(RH * SEGS, D), buf(RH * SEGS // 2, D), buf(RH * SEGS // 2, D), buf(RH * SEGS, D)]
    scratch += [buf(RH * SEGS, OC), buf(16, D, dtype=F32), buf(6, 16, D, dtype=F32), buf(2, D, dtype=F32), buf(3, 2, D, dtype=F32), buf(7, 2, D, dtype=F32)]
    for name in NAMES[:-1]:
        c = chunk[name]
        steps = [buf(4, *c), buf(2, 4, *c)] if name in X_FIRST else [buf(4, 2, *c), buf(4, *c)]
        scratch += [buf(2, 2, 4, 2, *c), buf(2, 4, 2, *c)] + steps + [buf(3, *c), buf(4, 2, *c)]
    c = chunk["pl"]
    scratch += [buf(4, 2, *c), buf(4, *c), buf(3, *c), buf(4, 2, *c)]
    if groups > 1:
        scratch += [buf(groups - 1, *chunk[name]) for name in NAMES]
        scratch += [buf(groups - 1, 16, D, dtype=F32), buf(groups - 1, 2, D, dtype=F32)]
    n_remote = 4 * 9 + 3 + 8 + 6 + 9 * 11 + 6 + 10 + 11 * (groups - 1)
    scratch += [pltpu.SemaphoreType.DMA((n_remote,)), pltpu.SemaphoreType.DMA((n_remote,)), pltpu.SemaphoreType.DMA((24,))]

    def out(*shape, dtype=BF):
        return jax.ShapeDtypeStruct(shape, dtype)

    flops = 30 * T * D * FF
    hid, emb, ig, gdn, gup, go_, gq, gk, gv, gpl, sm, late = pl.pallas_call(
        functools.partial(layer_kernel, (groups, RH, LS, D, FF, SEGS)),
        out_shape=[out(T, D), out(RH * SEGS, OC), out(T, D)]
        + [out(4, 2, FS // 8, D), out(4, 2, D // 8, FS)] + [out(4, 2, *chunk[name]) for name in ("o", "q", "k", "v", "pl")]
        + [out(16, D, dtype=F32), out(2, D, dtype=F32)],
        in_specs=[any_, vmem, any_, vmem, any_] + [vmem] * 5 + [any_, vmem, any_, vmem, any_, vmem, any_, any_],
        out_specs=[any_] * 12,
        scratch_shapes=scratch,
        compiler_params=pltpu.CompilerParams(collective_id=0, has_side_effects=True, vmem_limit_bytes=63 * 2 ** 20),
        cost_estimate=pl.CostEstimate(flops=flops, bytes_accessed=20 * 2 ** 20, transcendentals=T * FF),
        name="layer",
    )(layer_input.reshape(T, D), segment_labels, attend_weight, attend_bias, out_weight, out_bias, gain_attention,
      shift_attention, gain_feed, shift_feed, up_weight, up_bias.reshape(4, FS // 4), down_weight, down_bias,
      pool_weight, pool_bias, hidden_grad.reshape(T, D), embedding_grad.reshape(RH * SEGS, OC))

    d8 = D // 4
    return (
        hid.reshape(RH, LS, D),
        emb.reshape(RH, SEGS, OC),
        ig.reshape(RH, LS, D),
        jnp.stack([gq, gk, gv]).reshape(3, D, D // 4).astype(F32),
        lax.dynamic_slice_in_dim(sm[6:8], t * d8, d8, 1),
        go_.reshape(D // 4, D).astype(F32),
        sm[0], late[0], late[1], sm[3], sm[4],
        gup.reshape(D, FS).astype(F32),
        lax.dynamic_slice_in_dim(sm, 8 + t, 1, 0)[0],
        gdn.reshape(FS, D).astype(F32),
        sm[5],
        gpl.reshape(D, OC).astype(F32),
        lax.dynamic_slice_in_dim(sm, 12 + t, 1, 0)[0],
    )


def solution(mesh):
    placed = (
        P("rows", "tp", None), P("rows", None), P(None, None, "tp"), P(None, "tp"), P("tp", None), P(), P(), P(), P(), P(),
        P(None, "tp"), P("tp"), P("tp", None), P(), P(None, "tp"), P("tp"), P("rows", "tp", None), P("rows", None, "tp"),
    )
    return jax.shard_map(
        functools.partial(per_device, mesh.shape["rows"]),
        mesh=mesh,
        in_specs=placed,
        out_specs=(
            P("rows", "tp", None), P("rows", None, "tp"), P("rows", "tp", None), P(None, None, "tp"), P(None, "tp"),
            P("tp", None), P(), P(), P(), P(), P(), P(None, "tp"), P("tp"), P("tp", None), P(), P(None, "tp"), P("tp"),
        ),
        check_vma=False,
    )
```

```python
import functools
import math

import jax
import jax.numpy as jnp
from jax import lax
from jax.experimental import pallas as pl
from jax.experimental.pallas import tpu as pltpu
from jax.sharding import PartitionSpec as P

MESH = pl.DeviceIdType.MESH
HEAD_DIM = 64
HALO = 32
EPS = 1e-5
BF = jnp.bfloat16
F32 = jnp.float32
ROOT = math.sqrt(2.0 / math.pi)
CUBE = 0.044715
NAMES = ("dna", "dnb", "upa", "upb", "o", "q", "k", "v", "pl")
ORDERS = {'dna': ('lxhy', 'hlx'), 'dnb': ('yxlh', 'Zx'), 'upa': ('xylh', 'hlx'), 'upb': ('yxlh', 'hlx'), 'o': ('yhlx', 'hlx'), 'q': ('ylxh', 'xZ'), 'k': ('yxZ', 'lhx'), 'v': ('yxZ', 'lhx'), 'pl': ('lxh', 'xhl')}
PLAN = (
    (),
    (),
    (),
    (),
    (),
    (),
    (),
    (),
    (),
    ("qkv.step1", "gpool.step2", "wo.step1"),
    (),
    ("up.step1", "qkv.rx", "qkv.rz", "dn.step1", "wo.rx", "wo.rz", "qkv.rxz"),
    ("fore0.in", "wo.rxz"),
    (),
    (),
    ("up.rx", "up.rz"),
    (),
    (),
    ("fore1.in",),
    (),
    (),
    ("up.rxz",),
    (),
    (),
    (),
    ("dn.rx", "dn.rz"),
    ("gpool.step3",),
    (),
    (),
    ("dn.rxz",),
    (),
    (),
    (),
    (),
    (),
    (),
    (),
    (),
    (),
    (),
    (),
    (),
    (),
    ("dnb.r0", "dna.r0"),
    (),
    (),
    (),
    (),
    (),
    ("pooled.step2",),
    ("dnb.r1", "dna.r1"),
    (),
    (),
    ("pooled.step3", "dnb.r2"),
    (),
    ("upb.r0",),
    ("upa.r0", "dna.r2"),
    ("dnb.r3",),
    (),
    ("pl.r0", "o.r0"),
    (),
    (),
    (),
    (),
    ("dna.r3",),
    (),
    ("upb.r1", "dnb.sum", "upa.r1"),
    (),
    ("o.r1",),
    ("pl.r1", "v.r0", "dna.sum"),
    ("upb.r2", "upa.r2", "dnb.g1", "k.r0"),
    ("q.r0",),
    ("o.r2",),
    ("pl.r2", "upb.r3", "v.r1", "dna.g1"),
    ("upa.r3", "o.r3"),
    ("dnb.end", "k.r1", "sm.s0", "v.r2", "o.sum", "q.r1", "pl.sum", "dna.g2", "k.r2", "upb.sum", "back0.in"),
    ("upa.sum",),
    ("pl.g1", "q.r2"),
    ("v.sum", "o.g1", "back1.in"),
    (),
    ("sm.s1", "k.sum"),
    ("dna.end", "q.r3", "upb.g1", "upa.g1", "late.tp", "v.g1", "sm.s2", "o.g2", "k.g1", "upb.g2", "upa.g2", "o.end", "pl.g2", "q.sum", "late.rows", "upb.end", "v.g2", "upa.end", "q.g1", "sm.s3", "v.end", "k.g2", "pl.end", "k.end", "q.end"),
)


def mm(a, b):
    return jnp.dot(a, b, preferred_element_type=F32)


def mm_t(a, b):
    return lax.dot_general(a, b, (((1,), (1,)), ((), ())), preferred_element_type=F32)


def t_mm(a, b):
    return lax.dot_general(a, b, (((0,), (0,)), ((), ())), preferred_element_type=F32)


def normalize(values):
    mean = jnp.mean(values, axis=-1, keepdims=True)
    centred = values - mean
    spread = jnp.mean(centred * centred, axis=-1, keepdims=True)
    factor = lax.rsqrt(spread + EPS)
    return centred * factor, factor


def norm_back(grad, unit, factor, gain):
    scaled = grad * gain
    first = jnp.mean(scaled, axis=-1, keepdims=True)
    second = jnp.mean(scaled * unit, axis=-1, keepdims=True)
    return factor * (scaled - first - unit * second)


def total(values):
    return jnp.sum(values, axis=0, keepdims=True)


def layer_kernel(dims, *refs):
    (groups, RH, LS, D, FF, SEGS) = dims
    W = LS + 2 * HALO
    (x_in, lab_in, wqkv_in, ab_in, wo_in, v0_in, v1_in, v2_in, v3_in, v4_in, wup_in, bup_in, wdn_in, v5_in, wp_in, bp_in, hg_in, eg_in,
     hid_out, emb_out, ig_out, gdn_out, gup_out, go_out, gq_out, gk_out, gv_out, gpl_out, sm_out, late_out,
     x, hg, eg, mask, codes, wqkv, wo, wup, wdn, wp, shared, vec, bup,
     nw, q, k, v, p, at, mid, nf, act, dact, gma, gat, hid, gnc,
     halo_l, halo_r, halo_fl, halo_fr,
     gpt, gpr1, gpr2, gps, pt, pr1, pr2, ps, emb,
     smalls, sm_r, late, late_tp, late_rows,
     *tail) = refs
    tail = list(tail)
    sets = {}
    for name in NAMES:
        sets[name] = [tail.pop(0) for _ in range(len(ORDERS[name][0]) + (2 if name == "pl" else 3))]
    if groups > 1:
        r5 = {name: tail.pop(0) for name in NAMES + ("sm", "late")}
    send_sems, recv_sems, local_sems = tail
    T = RH * LS
    BR = 4
    NB = RH // BR
    BT = BR * LS
    H2 = 4 * HEAD_DIM

    r, t = lax.axis_index("rows"), lax.axis_index("tp")
    core, ypos = t % 2, t // 2
    tc = t + 1 - 2 * core
    ty = (t + 2) % 4
    tdiag = 3 - t
    xpos = r % 2
    rx = r + 1 - 2 * xpos
    zpos = (r // 2) % 4
    base = (r // 8) * 8
    zpeers = [base + ((zpos + dz) % 4) * 2 + xpos for dz in (1, 2, 3)]
    quad = r % 4
    rz = r + 2 - 4 * (quad // 2)
    rxz = rz + 1 - 2 * xpos
    zh, zl = zpos // 2, zpos % 2
    z1 = base + (zpos + 1 - 2 * zl) * 2 + xpos
    z2 = base + ((zpos + 2) % 4) * 2 + xpos
    xzpeers = [base + ((zpos + dz) % 4) * 2 + 1 - xpos for dz in (1, 2, 3)]
    gpeers = [((r // 8 + dg) % groups) * 8 + r % 8 for dg in range(1, groups)]

    counter = [0]

    def remote(src, dst, dev):
        i = counter[0]
        counter[0] += 1
        return pltpu.make_async_remote_copy(
            src_ref=src, dst_ref=dst, send_sem=send_sems.at[i], recv_sem=recv_sems.at[i],
            device_id=dev, device_id_type=MESH)

    local_count = [0]

    def local(src, dst):
        i = local_count[0]
        local_count[0] += 1
        c = pltpu.make_async_copy(src, dst, local_sems.at[i])
        c.start()
        return c

    spot, steps = [0], {}

    def chain(name, *links):
        for label, fn, _ in links:
            steps[name + "." + label] = fn

    def live(*names):
        pass

    def take(i):
        for name in PLAN[i] if i < len(PLAN) else ():
            steps[name]()

    def point():
        spot[0] += 1
        take(spot[0] - 1)

    def must(*names):
        point()

    def run(name, count, body, polls=None):
        first = spot[0]
        spot[0] += count

        def step(b, carry):
            body(b)
            for i in range(count):
                if i in (polls or {}) or (first + i < len(PLAN) and PLAN[first + i]):
                    @pl.when(b == i)
                    def _():
                        if i in (polls or {}):
                            polls[i]()
                        take(first + i)
            return carry

        lax.fori_loop(0, count, step, 0)

    def once(name, fn):
        fn()
        point()

    pending = []

    def go(copy):
        copy.start()
        pending.append(copy)
        return copy

    load_x = local(x_in, x)
    load_wp = local(wp_in, wp)
    load_eg = local(eg_in, eg)
    barrier = pltpu.get_barrier_semaphore()
    friends = [(r, tc), (r, ty), (r, tdiag), (rx, t)] + [(zp, t) for zp in zpeers + xzpeers] + [(gp_, t) for gp_ in gpeers]
    for dev in friends:
        pl.semaphore_signal(barrier, inc=1, device_id=dev, device_id_type=MESH)
    pl.semaphore_wait(barrier, len(friends))

    shared[t, 0:2, :] = ab_in[...]
    shared[t, 2:6, :] = bup_in[...]
    bias_moves = [go(remote(shared.at[t], shared.at[t], (r, dev))) for dev in (tc, ty, tdiag)]
    full = {"qkv": wqkv, "wo": wo, "up": wup, "dn": wdn}
    given = {"qkv": wqkv_in, "wo": wo_in, "up": wup_in, "dn": wdn_in}

    def shard(name, s, piece=None):
        ref = full[name]
        if name in ("qkv", "up"):
            rows_ = pl.ds(0, D) if piece is None else pl.ds(piece * (D // 4), D // 4)
            if name == "qkv":
                return ref.at[:, rows_, pl.ds(pl.multiple_of(s * 128, 128), 128)]
            return ref.at[rows_, pl.ds(pl.multiple_of(s * (FF // 4), 128), FF // 4)]
        n = (D if name == "wo" else FF) // 4
        if piece is None:
            return ref.at[pl.ds(s * n, n)]
        return ref.at[pl.ds(s * n + piece * (n // 4), n // 4)]

    def own_piece(name, piece):
        ref = given[name]
        if name == "qkv":
            return ref.at[:, pl.ds(piece * (D // 4), D // 4)]
        n = ref.shape[0] // 4
        return ref.at[pl.ds(piece * n, n)]

    class Gather:
        def __init__(self, name):
            self.name = name
            self.y = go(remote(own_piece(name, quad), shard(name, t, quad), (r, ty)))
            self.c = go(remote(given[name], shard(name, t), (r, tc)))
            self.loc = local(given[name], shard(name, t))
            mine = shard(name, ty, quad)
            self.x = [remote(mine, mine, (dev, t)) for dev in (rx, rz, rxz)]
            self.f = [remote(mine, mine, (r, tc))]
            for dev in (rx, rz, rxz):
                got = shard(name, ty, dev % 4)
                self.f.append(remote(got, got, (r, tc)))
            chain(name, ("step1", self.step1, [self.y]), ("rx", lambda: self.step2(0), [self.x[0]]),
                  ("rz", lambda: self.step2(1), [self.x[1]]), ("rxz", lambda: self.step2(2), [self.x[2]]))

        def step1(self):
            self.y.wait_recv()
            for c in self.x:
                go(c)
            go(self.f[0])

        def step2(self, i):
            self.x[i].wait_recv()
            go(self.f[i + 1])

        def near(self):
            self.loc.wait()
            self.c.wait_recv()

        def ready(self):
            for c in self.f:
                c.wait_recv()

    w_qkv = Gather("qkv")
    w_o = Gather("wo")
    w_up = Gather("up")
    w_dn = Gather("dn")
    live("qkv", "wo", "up", "dn")

    for i, ref in enumerate((v0_in, v1_in, v2_in, v3_in, v4_in, v5_in)):
        vec[i:i + 1, :] = ref[...].reshape(1, D)

    def row(i):
        return vec[i:i + 1, :]

    load_x.wait()

    class Halo:
        def __init__(self, pairs):
            self.left = [remote(a, b, (r, (t + 3) % 4)) for a, b, _, _ in pairs]
            self.right = [remote(c, d, (r, (t + 1) % 4)) for _, _, c, d in pairs]

        def send(self, i):
            pl.when(t > 0)(self.left[i].start)
            pl.when(t < 3)(self.right[i].start)

        def wait(self, i):
            pl.when(t > 0)(self.right[i].wait_recv)
            pl.when(t < 3)(self.left[i].wait_recv)

        def arrivals(self, name):
            for i in range(2):
                chain(name + str(i), ("in", functools.partial(self.wait, i), [self.left[i], self.right[i]]))

        def sent(self):
            for i in range(2):
                pl.when(t > 0)(self.left[i].wait_send)
                pl.when(t < 3)(self.right[i].wait_send)

    HR = RH // 2

    def edges(i, first):
        return nw.at[pl.ds(i * HR, HR), pl.ds(first, HALO)]

    halo = Halo([(edges(i, HALO), edges(i, HALO + LS), edges(i, LS), edges(i, 0)) for i in range(2)])

    halo.arrivals("fore")

    def ln1(b):
        xs = x[pl.ds(b * BT, BT), :].astype(F32)
        unit, _ = normalize(xs)
        out = (unit * row(1) + row(2)).astype(BF)
        nw[pl.ds(b * BR, BR), HALO:HALO + LS, :] = out.reshape(BR, LS, D)

    run("ln1", NB, ln1, {NB // 2 - 1: lambda: halo.send(0), NB - 1: lambda: (halo.send(1), live("fore0", "fore1"))})

    @pl.when(t == 0)
    def _():
        nw[:, 0:HALO, :] = jnp.zeros((RH, HALO, D), BF)

    @pl.when(t == 3)
    def _():
        nw[:, HALO + LS:W, :] = jnp.zeros((RH, HALO, D), BF)

    PH = RH * SEGS // 2
    load_wp.wait()
    load_eg.wait()

    class PoolSum:
        def __init__(self, name, terms, r1, r2, out):
            self.terms, self.r1, self.r2, self.out = terms, r1, r2, out
            mine, theirs = pl.ds(core * PH, PH), pl.ds((1 - core) * PH, PH)
            self.mine = mine
            self.a = remote(terms.at[theirs], r1, (r, tc))
            self.b = remote(terms.at[mine], r2, (r, ty))
            self.c = remote(out.at[mine], out.at[mine], (r, tc))
            chain(name, ("step2", self.step2, [self.a]), ("step3", self.step3, [self.b]))

        def step1(self):
            go(self.a)

        def step2(self):
            self.a.wait_recv()
            self.terms[self.mine, :] = (self.terms[self.mine, :].astype(F32) + self.r1[...].astype(F32)).astype(BF)
            go(self.b)

        def step3(self):
            self.b.wait_recv()
            self.out[self.mine, :] = (self.terms[self.mine, :].astype(F32) + self.r2[...].astype(F32)).astype(BF)
            go(self.c)

        def ready(self):
            self.c.wait_recv()

    gpool = PoolSum("gpool", gpt, gpr1, gpr2, gps)
    pooled = PoolSum("pooled", pt, pr1, pr2, ps)
    smalls[...] = jnp.zeros(smalls.shape, F32)

    def pool_back():
        smalls[pl.ds(12 + t, 1), :] = total(eg[...].astype(F32))
        gpt[...] = mm_t(eg[...], wp[...]).astype(BF)

    once("pool_back", pool_back)
    gpool.step1()

    load_hg = local(hg_in, hg)
    w_qkv.near()
    live("gpool")
    point()

    labels = lab_in[...]
    SL = labels.shape[1]
    window = pltpu.roll(labels, (SL + HALO - t * LS) % SL, 1)[:, 0:W].astype(F32)
    own_lab = pltpu.roll(labels, (SL - t * LS) % SL, 1)[:, 0:W].astype(F32)
    before = pltpu.roll(labels, (SL + 1 - t * LS) % SL, 1)[:, 0:W].astype(F32)
    codes[...] = jnp.where(own_lab == before, -1.0, own_lab)
    columns = jnp.transpose(own_lab)
    for i in range(RH):
        mask[i * LS:(i + 1) * LS, :] = jnp.where(columns[0:LS, i:i + 1] == window[i:i + 1, :], 0.0, -1e30)

    for copy in bias_moves:
        copy.wait_recv()
    for s in range(4):
        for i in range(2):
            vec[6 + i:7 + i, s * 128:(s + 1) * 128] = shared[s, i:i + 1, :]
        for i in range(4):
            bup[s:s + 1, i * 128:(i + 1) * 128] = shared[s, 2 + i:3 + i, :]

    point()

    near = pl.ds(pl.multiple_of(ypos * H2, H2), H2)
    far = pl.ds(pl.multiple_of((1 - ypos) * H2, H2), H2)

    def project_own(cols, b):
        own = nw[pl.ds(b * BR, BR), HALO:HALO + LS, :].reshape(BT, D)
        q[pl.ds(b * BT, BT), cols] = ((mm(own, wqkv[0, :, cols]) + vec[6:7, cols]) * (HEAD_DIM ** -0.5)).astype(BF)
        ks = mm(own, wqkv[1, :, cols]).astype(BF)
        vs = (mm(own, wqkv[2, :, cols]) + vec[7:8, cols]).astype(BF)
        k[pl.ds(b * BR, BR), HALO:HALO + LS, cols] = ks.reshape(BR, LS, H2)
        v[pl.ds(b * BR, BR), HALO:HALO + LS, cols] = vs.reshape(BR, LS, H2)

    def project_halo(b):
        rows_ = pl.ds(b * BR, BR)
        both = jnp.concatenate([nw[rows_, 0:HALO, :], nw[rows_, HALO + LS:W, :]], axis=0).reshape(BR * 2 * HALO, D)
        ks = mm(both, wqkv[1]).astype(BF).reshape(2, BR, HALO, D)
        vs = (mm(both, wqkv[2]) + row(7)).astype(BF).reshape(2, BR, HALO, D)
        k[rows_, 0:HALO, :] = ks[0]
        k[rows_, HALO + LS:W, :] = ks[1]
        v[rows_, 0:HALO, :] = vs[0]
        v[rows_, HALO + LS:W, :] = vs[1]

    lane = lax.broadcasted_iota(jnp.int32, (1, H2), 1) // HEAD_DIM
    heads = [(lane == h).astype(F32).astype(BF) for h in range(4)]

    def spread_heads(block):
        return jnp.concatenate([block * heads[h] for h in range(4)], axis=0)

    def merge_heads(stack):
        parts = [stack[h * LS:(h + 1) * LS, :] for h in range(4)]
        out = jnp.where(lane == 0, parts[0], parts[1])
        out = jnp.where(lane == 2, parts[2], out)
        return jnp.where(lane == 3, parts[3], out)

    def attend(i):
        work = [(i * 2 + n, half) for n in range(2) for half in range(2)]
        sides = [slice(half * H2, (half + 1) * H2) for _, half in work]
        scores = []
        for (n, _), c in zip(work, sides):
            m1 = mask[pl.ds(n * LS, LS), :]
            qs = spread_heads(q[pl.ds(n * LS, LS), c])
            scores.append(mm_t(qs, k[n, :, c]) + jnp.concatenate([m1] * 4, axis=0))
        tops = [jnp.max(sc, axis=-1, keepdims=True) for sc in scores]
        es = [jnp.exp(sc - top) for sc, top in zip(scores, tops)]
        inv = [1.0 / jnp.sum(e, axis=-1, keepdims=True) for e in es]
        ws = [(e * f).astype(BF) for e, f in zip(es, inv)]
        outs = []
        for (n, half), c, w in zip(work, sides, ws):
            p[pl.ds((n * 2 + half) * 4 * LS, 4 * LS), :] = w
            outs.append(mm(w, v[n, :, c]))
        for (n, _), c, o in zip(work, sides, outs):
            at[pl.ds(n * LS, LS), c] = merge_heads(o).astype(BF)

    HB = NB // 2
    AB = RH // 4
    run("own_near", NB, lambda b: project_own(near, b))
    must("qkv")
    w_qkv.ready()
    run("own_far", NB, lambda b: project_own(far, b))
    must("fore0")
    run("halo_all", HB, project_halo)
    run("attend", AB, attend)
    must("fore1")
    run("halo_all", HB, lambda b: project_halo(b + HB))
    run("attend", AB, lambda i: attend(i + AB))
    ids = lax.broadcasted_iota(jnp.int32, (SEGS, LS), 0).astype(F32)

    def chosen(n):
        return (ids == codes[pl.ds(n, 1), 0:LS]).astype(F32).astype(BF)

    must("gpool")
    gpool.ready()
    load_hg.wait()

    def place(b):
        rows_ = pl.ds(b * BT, BT)
        put = [t_mm(chosen(b * BR + n), gps[pl.ds((b * BR + n) * SEGS, SEGS), :]) for n in range(BR)]
        g = hg[rows_, :].astype(F32) + jnp.concatenate(put, axis=0)
        low = g.astype(BF)
        hg[rows_, :] = low
        smalls[5:6, :] += total(low.astype(F32))

    run("place", NB, place)

    must("wo", "up")
    for w in (w_o, w_up):
        w.near()
        w.ready()

    FC = FF // 4
    def feed_up(b):
        rows_ = pl.ds(b * BT, BT)
        middle = x[rows_, :].astype(F32) + (mm(at[rows_, :], wo[...]) + row(0))
        mid[rows_, :] = middle
        unit, _ = normalize(middle)
        normed = (unit * row(3) + row(4)).astype(BF)
        nf[rows_, :] = normed
        for j in range(4):
            cols = slice(j * FC, (j + 1) * FC)
            u = mm(normed, wup[:, cols]) + bup[j:j + 1, :]
            u2 = u * u
            th = jnp.tanh(u * (ROOT + (ROOT * CUBE) * u2))
            half_up = 0.5 + 0.5 * th
            a = u * half_up
            act[rows_, cols] = a.astype(BF)
            dact[rows_, cols] = (half_up + (a - a * half_up) * (2.0 * ROOT + (6.0 * CUBE * ROOT) * u2)).astype(BF)

    def feed_down(b):
        rows_ = pl.ds(b * BT, BT)
        low = (mid[rows_, :] + (mm(act[rows_, :], wdn[...]) + row(5))).astype(BF)
        hid[rows_, :] = low
        for n in range(BR):
            first = chosen(b * BR + n)
            pt[pl.ds((b * BR + n) * SEGS, SEGS), :] = mm(first, low[n * LS:(n + 1) * LS, :]).astype(BF)

    run("feed_up", NB, feed_up)
    gb = hg

    mine = {"y": ypos, "h": zh, "l": zl, "x": xpos}
    partner = {"y": (r, ty), "h": (z2, t), "l": (z1, t), "x": (rx, t)}
    own_part = (zh, zl, xpos)

    class Reduce:
        def __init__(self, name, g, r1, bufs, o):
            self.name, self.g, self.r1, self.bufs, self.o = name, g, r1, bufs, o
            axes = "hlx" if r1 is None else "yhlx"
            lead = () if r1 is None else (core,)
            over, gather = ORDERS[name]

            def at(fixed, flip=""):
                return tuple(1 - mine[a] if a == flip else mine[a] if a in fixed else slice(None) for a in axes)

            def peer(dz):
                z = (zpos + dz) % 4
                return (z // 2, z % 2, xpos)

            near_copies = []
            if r1 is not None:
                self.a1 = remote(g.at[1 - core, 1 - ypos], r1.at[1 - ypos], (r, tc))
                self.a2 = remote(g.at[1 - core, ypos], r1.at[ypos], (r, tc))
                near_copies = [self.a1] if over[0] == "y" else [self.a1, self.a2]
            moves, fixed, regions = [], "", []
            for i, d in enumerate(over):
                if d == "Z":
                    tail_at = at(fixed)[:-3] + ()
                    moves.append([remote(g.at[lead + tail_at + peer(dz)], bufs[i].at[dz - 1], (zpeers[dz - 1], t)) for dz in (1, 2, 3)])
                    fixed += "hl"
                else:
                    moves.append([remote(g.at[lead + at(fixed, d)], bufs[i], partner[d])])
                    fixed += d
                regions.append(at(fixed))
            links = [("r0", functools.partial(self.first, lead, at("", over[0]), near_copies, moves[0]), near_copies)]
            for i in range(1, len(over)):
                wait_for = moves[i - 1] + ([self.a2] if r1 is not None and i == 1 and over[0] == "y" else [])
                links.append(("r" + str(i), functools.partial(self.middle, lead, regions[i - 1], i, wait_for, moves[i]), wait_for))
            gathers, got = [], ""
            for d in gather:
                place_at = tuple(slice(None) if a in got else mine[a] for a in "hlx")
                if d == "Z":
                    gathers.append([remote(o.at[place_at], o.at[place_at], (zpeers[dz - 1], t)) for dz in (1, 2, 3)])
                    got += "hl"
                else:
                    gathers.append([remote(o.at[place_at], o.at[place_at], partner[d])])
                    got += d
            if groups > 1:
                self.m = [remote(o.at[own_part], r5[name].at[i], (gpeers[i], t)) for i in range(groups - 1)]
            links.append(("sum", functools.partial(self.last, lead, regions[-1], over[-1] == "Z", moves[-1], gathers[0]), moves[-1]))
            for i in range(1, len(gather)):
                links.append(("g" + str(i), functools.partial(self.gather, gathers[i - 1], gathers[i]), gathers[i - 1]))
            links.append(("end", functools.partial(self.finish, gathers[-1]), gathers[-1]))
            chain(name, *links)

        def core1(self):
            go(self.a1)

        def core2(self):
            go(self.a2)

        def first(self, lead, region, awaited, moves):
            for c in awaited:
                c.wait_recv()
            if self.r1 is not None:
                self.g[lead + region] = (self.g[lead + region].astype(F32) + self.r1[region].astype(F32)).astype(BF)
            go(moves[0])

        def middle(self, lead, region, i, awaited, moves):
            for c in awaited:
                c.wait_recv()
            acc = self.g[lead + region].astype(F32) + self.bufs[i - 1][...].astype(F32)
            if self.r1 is not None and i == 1:
                acc = acc + self.r1[region].astype(F32)
            self.g[lead + region] = acc.astype(BF)
            for c in moves:
                go(c)

        def last(self, lead, region, direct, awaited, moves):
            acc = self.g[lead + region].astype(F32)
            for i, c in enumerate(awaited):
                c.wait_recv()
                acc = acc + (self.bufs[-1][i] if direct else self.bufs[-1][...]).astype(F32)
            self.o[own_part] = acc.astype(BF)
            if groups > 1:
                for c in self.m:
                    c.start()
                for c in self.m:
                    c.wait()
                acc = self.o[own_part].astype(F32)
                for i in range(groups - 1):
                    acc = acc + r5[self.name][i].astype(F32)
                self.o[own_part] = acc.astype(BF)
            for c in moves:
                go(c)

        def gather(self, awaited, moves):
            for c in awaited:
                c.wait_recv()
            for c in moves:
                go(c)

        def finish(self, awaited):
            for c in awaited:
                c.wait_recv()
            stores.append(local(self.o, final[self.name]))

    HC = D // 2

    def halves(out, i):
        return out.at[:, :, :, :, pl.ds(i * HC, HC)]

    final = {"dna": halves(gdn_out, 0), "dnb": halves(gdn_out, 1), "upa": halves(gup_out, 0), "upb": halves(gup_out, 1),
             "o": go_out, "q": gq_out, "k": gk_out, "v": gv_out, "pl": gpl_out}
    stores = []
    red = {}
    for name in NAMES:
        held = sets[name]
        if name == "pl":
            held = [held[0], None] + held[1:]
        red[name] = Reduce(name, held[0], held[1], held[2:-1], held[-1])

    def split(names, cs, ys, val):
        for i, name in enumerate(names):
            g = sets[name][0]
            g[cs, ys] = val[:, i * HC:(i + 1) * HC].astype(BF).reshape(g.shape[2:])

    def place_of(i):
        return (core + 1 + i // 2) % 2, (ypos + 1 + i) % 2

    def down_grad(i):
        cs, ys = place_of(i)
        val = t_mm(act[:, pl.ds(pl.multiple_of((ys * 2 + cs) * FC, FC), FC)], gb[...])
        split(("dna", "dnb"), cs, ys, val)

    def near_cores(*names):
        return lambda: [red[n].core1() for n in names], lambda: [red[n].core2() for n in names]

    send1, send2 = near_cores("dna", "dnb")
    run("down_grad", 4, down_grad, {0: send1, 1: send2, 2: lambda: live("dnb"), 3: lambda: live("dna")})
    must("dn")
    w_dn.near()
    w_dn.ready()
    run("feed_down", NB, feed_down)
    store_hid = local(hid, hid_out)
    pooled.step1()
    live("pooled")

    def feed_back(b):
        rows_ = pl.ds(b * BT, BT)
        g = gb[rows_, :]
        acc = jnp.zeros((BT, D), F32)
        for j in range(4):
            cols = slice(j * FC, (j + 1) * FC)
            ga = mm_t(g, wdn[cols, :])
            gp = (ga * dact[rows_, cols].astype(F32)).astype(BF)
            dact[rows_, cols] = gp
            smalls[8 + j:9 + j, :] += total(gp.astype(F32))
            acc = acc + mm_t(gp, wup[:, cols])
        unit, factor = normalize(mid[rows_, :])
        smalls[3:4, :] += total(acc * unit)
        smalls[4:5, :] += total(acc)
        gm = g.astype(F32) + norm_back(acc, unit, factor, row(3))
        mid[rows_, :] = gm
        low = gm.astype(BF)
        gma[rows_, :] = low
        smalls[0:1, :] += total(low.astype(F32))
        gat[rows_, :] = mm_t(low, wo[...]).astype(BF)

    run("feed_back", NB, feed_back)
    def up_grad(i):
        cs, ys = place_of(i)
        val = t_mm(nf[...], dact[:, pl.ds(pl.multiple_of((ys * 2 + cs) * FC, FC), FC)])
        split(("upa", "upb"), cs, ys, val)

    send3, send4 = near_cores("upa", "upb")
    run("up_grad", 4, up_grad, {0: send3, 1: send4, 2: lambda: live("upb"), 3: lambda: live("upa")})

    def out_grad():
        val = t_mm(at[...], gma[...]).astype(BF)
        for s in range(4):
            g = sets["o"][0]
            g[s % 2, s // 2] = val[s * (D // 4):(s + 1) * (D // 4), :].reshape(g.shape[2:])
        red["o"].core1()
        red["o"].core2()
        live("o")

    once("out_grad", out_grad)

    must("pooled")
    pooled.ready()

    def embed():
        emb[...] = (mm(ps[...], wp[...]) + bp_in[...].reshape(1, D)).astype(BF)
        sets["pl"][0][...] = t_mm(ps[...], eg[...]).astype(BF).reshape(sets["pl"][0].shape)
        live("pl")

    once("embed", embed)
    store_emb = local(emb, emb_out)

    def attend_back(i):
        work = [(i * 2 + n, half) for n in range(2) for half in range(2)]
        sides = [slice(half * H2, (half + 1) * H2) for _, half in work]
        qss = [spread_heads(q[pl.ds(n * LS, LS), c]) for (n, _), c in zip(work, sides)]
        gss = [spread_heads(gat[pl.ds(n * LS, LS), c]) for (n, _), c in zip(work, sides)]
        ws = [p[pl.ds((n * 2 + half) * 4 * LS, 4 * LS), :] for n, half in work]
        gws = [mm_t(g, v[n, :, c]) for g, (n, _), c in zip(gss, work, sides)]
        wfs = [w.astype(F32) for w in ws]
        prods = [w * g for w, g in zip(wfs, gws)]
        sums = [jnp.sum(pr, axis=-1, keepdims=True) for pr in prods]
        dss = [(pr - w * sm).astype(BF) for pr, w, sm in zip(prods, wfs, sums)]
        dvs = [t_mm(w, g).astype(BF) for w, g in zip(ws, gss)]
        dqs = [mm(ds, k[n, :, c]) for ds, (n, _), c in zip(dss, work, sides)]
        dks = [t_mm(ds, qq).astype(BF) for ds, qq in zip(dss, qss)]
        for (n, _), c, dq, dk, dv in zip(work, sides, dqs, dks, dvs):
            q[pl.ds(n * LS, LS), c] = (merge_heads(dq) * (HEAD_DIM ** -0.5)).astype(BF)
            k[n, :, c] = dk
            v[n, :, c] = dv

    run("attend_back", RH // 2, attend_back)

    back = Halo([tuple(ref.at[pl.ds(i * HR, HR)] for ref in (halo_l, halo_fr, halo_r, halo_fl)) for i in range(2)])
    back.arrivals("back")

    def norm_grad(b):
        keys = pl.ds(b * BR, BR)
        dqs = q[pl.ds(b * BT, BT), :]
        dks, dvs = k[keys].reshape(BR * W, D), v[keys].reshape(BR * W, D)
        smalls[6:7, :] += total(dqs.astype(F32))
        smalls[7:8, :] += total(dvs.astype(F32))
        win = (mm_t(dks, wqkv[1]) + mm_t(dvs, wqkv[2])).reshape(BR, W, D)
        own = win[:, HALO:HALO + LS, :].reshape(BT, D) + mm_t(dqs, wqkv[0])
        gnc[pl.ds(b * BT, BT), :] = own
        halo_l[keys] = win[:, 0:HALO, :].astype(BF)
        halo_r[keys] = win[:, HALO + LS:W, :].astype(BF)

    def put_at(g, val):
        low = val.astype(BF)
        for s in range(4):
            g[s % 2, s // 2] = low[:, s * 128:(s + 1) * 128].reshape(g.shape[2:])

    def put_value():
        put_at(sets["v"][0], t_mm(nw[...].reshape(RH * W, D), v[...].reshape(RH * W, D)))
        red["v"].core1()
        red["v"].core2()
        live("v")

    def put_key():
        put_at(sets["k"][0], t_mm(nw[...].reshape(RH * W, D), k[...].reshape(RH * W, D)))
        red["k"].core1()
        red["k"].core2()
        live("k")

    def put_query():
        put_at(sets["q"][0], t_mm(nw[:, HALO:HALO + LS, :].reshape(T, D), q[...]))
        red["q"].core1()
        red["q"].core2()
        live("q")

    once("put_v", put_value)
    once("put_k", put_key)
    once("put_q", put_query)
    run("norm_grad", NB, norm_grad, {HB - 1: lambda: back.send(0), NB - 1: lambda: (back.send(1), live("back0", "back1"))})

    @pl.when(t == 0)
    def _():
        halo_fl[...] = jnp.zeros(halo_fl.shape, BF)

    @pl.when(t == 3)
    def _():
        halo_fr[...] = jnp.zeros(halo_fr.shape, BF)

    class Small:
        name = "sm"

        def __init__(self):
            self.copies = [[remote(smalls, sm_r.at[0], (r, tc))], [remote(smalls, sm_r.at[1], (r, ty))],
                           [remote(smalls, sm_r.at[2], (rx, t))],
                           [remote(smalls, sm_r.at[2 + dz], (zpeers[dz - 1], t)) for dz in (1, 2, 3)]]
            chain("sm", *[("s" + str(i), functools.partial(self.step, i), self.copies[i]) for i in range(4)])

        def send(self, i):
            for c in self.copies[i]:
                c.start()

        def step(self, i):
            for c in self.copies[i]:
                c.wait()
            if i < 3:
                smalls[...] += sm_r[i]
                self.send(i + 1)
            else:
                smalls[...] += sm_r[3] + sm_r[4] + sm_r[5]
                across(smalls, "sm")
                stores.append(local(smalls, sm_out))

    class Late:
        name = "late"

        def __init__(self):
            self.a = [remote(late, late_tp.at[i], (r, dev)) for i, dev in enumerate((tc, ty, tdiag))]
            self.b = [remote(late, late_rows.at[i], (dev, t)) for i, dev in enumerate([rx] + zpeers + xzpeers)]
            chain("late", ("tp", self.over_tp, self.a), ("rows", self.over_rows, self.b))

        def over_tp(self):
            for c in self.a:
                c.wait()
            late[...] += late_tp[0] + late_tp[1] + late_tp[2]
            for c in self.b:
                c.start()

        def over_rows(self):
            for c in self.b:
                c.wait()
            for i in range(7):
                late[...] += late_rows[i]
            across(late, "late")
            stores.append(local(late, late_out))

    def across(ref, name):
        moves = [remote(ref, r5[name].at[i], (gpeers[i], t)) for i in range(groups - 1)]
        for c in moves:
            c.start()
        for c in moves:
            c.wait()
        for i in range(groups - 1):
            ref[...] += r5[name][i]

    small, lates = Small(), Late()
    small.send(0)
    live("sm")
    late[...] = jnp.zeros(late.shape, F32)

    def ln1_back(b):
        rows_ = pl.ds(b * BT, BT)
        grp = pl.ds(b * BR, BR)
        g = gnc[rows_, :].reshape(BR, LS, D)
        g = jnp.concatenate([g[:, 0:HALO, :] + halo_fl[grp].astype(F32), g[:, HALO:LS, :] + halo_fr[grp].astype(F32)], axis=1)
        g = g.reshape(BT, D)
        unit, factor = normalize(x[rows_, :].astype(F32))
        late[0:1, :] += total(g * unit)
        late[1:2, :] += total(g)
        nf[rows_, :] = (mid[rows_, :] + norm_back(g, unit, factor, row(1))).astype(BF)

    must("back0")
    run("ln1_back", HB, ln1_back)
    must("back1")
    run("ln1_back", HB, lambda b: ln1_back(b + HB))
    store_ig = local(nf, ig_out)
    for c in lates.a:
        c.start()
    live("late")
    must(*NAMES, "sm", "late")
    for c in pending:
        c.wait_send()
    halo.sent()
    back.sent()
    for c in stores + [store_hid, store_emb, store_ig]:
        c.wait()


def per_device(rows_size, layer_input, segment_labels, attend_weight, attend_bias, out_weight, out_bias, gain_attention,
               shift_attention, gain_feed, shift_feed, up_weight, up_bias, down_weight, down_bias, pool_weight, pool_bias,
               hidden_grad, embedding_grad):
    RH, LS, D = layer_input.shape
    SEGS = embedding_grad.shape[1]
    OC = pool_weight.shape[1]
    FS = up_weight.shape[1]
    FF = FS * 4
    W = LS + 2 * HALO
    T = RH * LS
    NB = RH // 4
    groups = rows_size // 8
    t = lax.axis_index("tp")
    part = (D // 8, D // 4)
    chunk = {"dna": (FS // 8, D // 2), "dnb": (FS // 8, D // 2), "upa": (D // 8, FS // 2), "upb": (D // 8, FS // 2), "o": (D // 32, D), "q": part, "k": part, "v": part, "pl": (D // 8, OC)}
    any_, vmem = pl.BlockSpec(memory_space=pl.ANY), pl.BlockSpec(memory_space=pltpu.VMEM)

    def buf(*shape, dtype=BF):
        return pltpu.VMEM(shape, dtype)

    scratch = [
        buf(T, D), buf(T, D), buf(RH * SEGS, OC), buf(T, W, dtype=F32), buf(RH, W, dtype=F32),
        buf(3, D, D), buf(D, D), buf(D, FF), buf(FF, D), buf(D, OC), buf(4, 8, 128, dtype=F32), buf(8, D, dtype=F32), buf(4, FS, dtype=F32),
        buf(RH, W, D), buf(T, D), buf(RH, W, D), buf(RH, W, D), buf(RH * 2 * 4 * LS, W), buf(T, D), buf(T, D, dtype=F32),
        buf(T, D), buf(T, FF), buf(T, FF), buf(T, D), buf(T, D), buf(T, D), buf(T, D, dtype=F32),
        buf(RH, HALO, D), buf(RH, HALO, D), buf(RH, HALO, D), buf(RH, HALO, D),
    ]
    for _ in range(2):
        scratch += [buf(RH * SEGS, D), buf(RH * SEGS // 2, D), buf(RH * SEGS // 2, D), buf(RH * SEGS, D)]
    scratch += [buf(RH * SEGS, OC), buf(16, D, dtype=F32), buf(6, 16, D, dtype=F32), buf(2, D, dtype=F32), buf(3, 2, D, dtype=F32), buf(7, 2, D, dtype=F32)]
    for name in NAMES:
        c, over = chunk[name], ORDERS[name][0]
        left = 3 if name == "pl" else 4
        scratch += [buf(*[2] * 3, *c)] if name == "pl" else [buf(2, *[2] * 4, *c), buf(*[2] * 4, *c)]
        for i, d in enumerate(over):
            scratch.append(buf(3, *c) if d == "Z" else buf(*[2] * (left - 1 - i), *c))
        scratch.append(buf(2, 2, 2, *c))
    if groups > 1:
        scratch += [buf(groups - 1, *chunk[name]) for name in NAMES]
        scratch += [buf(groups - 1, 16, D, dtype=F32), buf(groups - 1, 2, D, dtype=F32)]
    n_remote = 4 * 9 + 3 + 8 + 6 + 9 * 11 + 6 + 10 + 11 * (groups - 1)
    scratch += [pltpu.SemaphoreType.DMA((n_remote,)), pltpu.SemaphoreType.DMA((n_remote,)), pltpu.SemaphoreType.DMA((24,))]

    def out(*shape, dtype=BF):
        return jax.ShapeDtypeStruct(shape, dtype)

    flops = 30 * T * D * FF
    hid, emb, ig, gdn, gup, go_, gq, gk, gv, gpl, sm, late = pl.pallas_call(
        functools.partial(layer_kernel, (groups, RH, LS, D, FF, SEGS)),
        out_shape=[out(T, D), out(RH * SEGS, OC), out(T, D)]
        + [out(2, 2, 2, FS // 8, D), out(2, 2, 2, D // 8, FS)] + [out(2, 2, 2, *chunk[name]) for name in ("o", "q", "k", "v", "pl")]
        + [out(16, D, dtype=F32), out(2, D, dtype=F32)],
        in_specs=[any_, vmem, any_, vmem, any_] + [vmem] * 5 + [any_, vmem, any_, vmem, any_, vmem, any_, any_],
        out_specs=[any_] * 12,
        scratch_shapes=scratch,
        compiler_params=pltpu.CompilerParams(collective_id=0, has_side_effects=True, vmem_limit_bytes=63 * 2 ** 20),
        cost_estimate=pl.CostEstimate(flops=flops, bytes_accessed=20 * 2 ** 20, transcendentals=T * FF),
        name="layer",
    )(layer_input.reshape(T, D), segment_labels, attend_weight, attend_bias, out_weight, out_bias, gain_attention,
      shift_attention, gain_feed, shift_feed, up_weight, up_bias.reshape(4, FS // 4), down_weight, down_bias,
      pool_weight, pool_bias, hidden_grad.reshape(T, D), embedding_grad.reshape(RH * SEGS, OC))

    grads = [gq, gk, gv, go_, gup, gdn, gpl]
    flat = [(D, D // 4)] * 3 + [(D // 4, D), (D, FS), (FS, D), (D, OC)]
    grads = [g.reshape(shape) for g, shape in zip(grads, flat)]
    whole = [hid.reshape(RH, LS, D), emb.reshape(RH, SEGS, OC), ig.reshape(RH, LS, D)]
    vecs = [D] * 6 + [FS, OC]
    made = pl.pallas_call(
        last_kernel,
        out_shape=[out(*w.shape) for w in whole] + [out(3, D, D // 4, dtype=F32)] + [out(*shape, dtype=F32) for shape in flat[3:]]
        + [out(2, D // 4, dtype=F32)] + [out(n, dtype=F32) for n in vecs],
        in_specs=[any_] * 10 + [vmem] * 2,
        out_specs=[any_] * 8 + [vmem] * 9,
        scratch_shapes=[buf(*shape) for shape in flat] + [buf(*shape, dtype=F32) for shape in flat]
        + [buf(*w.shape) for w in whole] + [pltpu.SemaphoreType.DMA((20,))],
        compiler_params=pltpu.CompilerParams(vmem_limit_bytes=60 * 2 ** 20),
        cost_estimate=pl.CostEstimate(flops=T * D, bytes_accessed=11 * 2 ** 20, transcendentals=0),
        name="last",
    )(*whole, *grads, sm, late)
    hid, emb, ig, gat, go_, gup, gdn, gpl, gab, gob, ga, sa, gf, sf, gdb, gub, gpb = made
    return (hid, emb, ig, gat, gab, go_, gob, ga, sa, gf, sf, gup, gub, gdn, gdb, gpl, gpb)


def last_kernel(*refs):
    whole_in, grads_in, (sm, late), refs = refs[:3], refs[3:10], refs[10:12], refs[12:]
    whole_out, (at_out, *rest), (gab, *vec_out), refs = refs[:3], refs[3:8], refs[8:17], refs[17:]
    low, wide, held, sems = refs[:7], refs[7:14], refs[14:17], refs[17]
    t = lax.axis_index("tp")
    copies = [pltpu.make_async_copy(a, b, sems.at[i]) for i, (a, b) in enumerate(zip(grads_in, low))]
    loads = [pltpu.make_async_copy(a, b, sems.at[14 + i]) for i, (a, b) in enumerate(zip(whole_in, held))]
    for c in loads + copies:
        c.start()
    n = gab.shape[1]
    gab[...] = sm[6:8, pl.ds(pl.multiple_of(t * n, 128), n)]
    rows = [sm[0:1, :], late[0:1, :], late[1:2, :], sm[3:4, :], sm[4:5, :], sm[5:6, :], sm[pl.ds(8 + t, 1), :], sm[pl.ds(12 + t, 1), :]]
    for ref, value in zip(vec_out, rows):
        ref[...] = value.reshape(ref.shape)
    targets = [at_out.at[0], at_out.at[1], at_out.at[2]] + rest
    stores = []
    for i, c in enumerate(loads):
        c.wait()
        stores.append(pltpu.make_async_copy(held[i], whole_out[i], sems.at[17 + i]))
        stores[-1].start()
    for i, c in enumerate(copies):
        c.wait()
        wide[i][...] = low[i][...].astype(F32)
        stores.append(pltpu.make_async_copy(wide[i], targets[i], sems.at[7 + i]))
        stores[-1].start()
    for c in stores:
        c.wait()


def solution(mesh):
    placed = (
        P("rows", "tp", None), P("rows", None), P(None, None, "tp"), P(None, "tp"), P("tp", None), P(), P(), P(), P(), P(),
        P(None, "tp"), P("tp"), P("tp", None), P(), P(None, "tp"), P("tp"), P("rows", "tp", None), P("rows", None, "tp"),
    )
    return jax.shard_map(
        functools.partial(per_device, mesh.shape["rows"]),
        mesh=mesh,
        in_specs=placed,
        out_specs=(
            P("rows", "tp", None), P("rows", None, "tp"), P("rows", "tp", None), P(None, None, "tp"), P(None, "tp"),
            P("tp", None), P(), P(), P(), P(), P(), P(None, "tp"), P("tp"), P("tp", None), P(), P(None, "tp"), P("tp"),
        ),
        check_vma=False,
    )
```

```python
import functools
import math

import jax
import jax.numpy as jnp
from jax import lax
from jax.experimental import pallas as pl
from jax.experimental.pallas import tpu as pltpu
from jax.sharding import PartitionSpec as P

MESH = pl.DeviceIdType.MESH
HEAD_DIM = 64
HALO = 32
EPS = 1e-5
BF = jnp.bfloat16
F32 = jnp.float32
ROOT = math.sqrt(2.0 / math.pi)
CUBE = 0.044715
NAMES = ("dna", "dnb", "upa", "upb", "o", "q", "k", "v", "pl")
ORDERS = {'dna': ('yxZ', 'hlx'), 'dnb': ('xlyh', 'hlx'), 'upa': ('xylh', 'hlx'), 'upb': ('yxZ', 'hlx'), 'o': ('yxZ', 'lhx'), 'q': ('yxZ', 'xZ'), 'k': ('yxZ', 'lhx'), 'v': ('yxZ', 'lhx'), 'pl': ('lxh', 'xhl')}
PLAN = (
    (),
    (),
    (),
    (),
    (0, 1, 6),
    (2,),
    (),
    (0, 0, 4),
    (),
    (),
    (),
    (1, 1, 5),
    (0,),
    (1,),
    (),
    (),
    (2, 2),
    (),
    (),
    (6,),
    (),
    (2,),
    (3,),
    (),
    (),
    (),
    (),
    (),
    (3, 3),
    (3,),
    (),
    (),
    (),
    (8,),
    (),
    (9,),
    (),
    (7,),
    (8, 9),
    (),
    (),
    (),
    (11, 10),
    (7, 8, 9),
    (),
    (12, 16),
    (),
    (),
    (),
    (),
    (8, 11, 10),
    (),
    (9,),
    (),
    (),
    (12, 8, 16, 11, 15, 9),
    (10, 14),
    (8, 12, 13),
    (16, 11, 15, 9),
    (10, 14, 19, 8, 12, 15, 17),
    (16, 9, 14),
    (12, 11, 13, 10, 16, 15, 18),
    (11, 14, 19),
    (9, 12, 13, 10, 20, 15, 14, 11, 19, 10, 12, 16, 13, 20, 10, 15, 13, 14, 15, 19, 16, 14, 13),
)


def mm(a, b):
    return jnp.dot(a, b, preferred_element_type=F32)


def mm_t(a, b):
    return lax.dot_general(a, b, (((1,), (1,)), ((), ())), preferred_element_type=F32)


def t_mm(a, b):
    return lax.dot_general(a, b, (((0,), (0,)), ((), ())), preferred_element_type=F32)


def normalize(values):
    mean = jnp.mean(values, axis=-1, keepdims=True)
    centred = values - mean
    spread = jnp.mean(centred * centred, axis=-1, keepdims=True)
    factor = lax.rsqrt(spread + EPS)
    return centred * factor, factor


def norm_back(grad, unit, factor, gain):
    scaled = grad * gain
    first = jnp.mean(scaled, axis=-1, keepdims=True)
    second = jnp.mean(scaled * unit, axis=-1, keepdims=True)
    return factor * (scaled - first - unit * second)


def total(values):
    return jnp.sum(values, axis=0, keepdims=True)


def layer_kernel(dims, *refs):
    (groups, RH, LS, D, FF, SEGS) = dims
    W = LS + 2 * HALO
    (x_in, lab_in, wqkv_in, ab_in, wo_in, v0_in, v1_in, v2_in, v3_in, v4_in, wup_in, bup_in, wdn_in, v5_in, wp_in, bp_in, hg_in, eg_in,
     hid_out, emb_out, ig_out, gdn_out, gup_out, go_out, gq_out, gk_out, gv_out, gpl_out, sm_out, late_out,
     x, hg, eg, mask, codes, wqkv, wo, wup, wdn, wp, shared, vec, bup,
     nw, q, k, v, p, at, mid, nf, act, dact, gma, gat, hid,
     halo_l, halo_r, halo_fl, halo_fr,
     gpt, gpr1, gpr2, gps, pt, pr1, pr2, ps, emb,
     smalls, sm_r, late, late_tp, late_rows,
     *tail) = refs
    tail = list(tail)
    sets = {}
    for name in NAMES:
        sets[name] = [tail.pop(0) for _ in range(len(ORDERS[name][0]) + (2 if name == "pl" else 3))]
    if groups > 1:
        r5 = {name: tail.pop(0) for name in NAMES + ("sm", "late")}
    send_sems, recv_sems, local_sems = tail
    T = RH * LS
    BR = 8
    NB = RH // BR
    BT = BR * LS
    H2 = 4 * HEAD_DIM

    r, t = lax.axis_index("rows"), lax.axis_index("tp")
    core, ypos = t % 2, t // 2
    tc = t + 1 - 2 * core
    ty = (t + 2) % 4
    tdiag = 3 - t
    xpos = r % 2
    rx = r + 1 - 2 * xpos
    zpos = (r // 2) % 4
    base = (r // 8) * 8
    zpeers = [base + ((zpos + dz) % 4) * 2 + xpos for dz in (1, 2, 3)]
    quad = r % 4
    rz = r + 2 - 4 * (quad // 2)
    rxz = rz + 1 - 2 * xpos
    zh, zl = zpos // 2, zpos % 2
    z1 = base + (zpos + 1 - 2 * zl) * 2 + xpos
    z2 = base + ((zpos + 2) % 4) * 2 + xpos
    xzpeers = [base + ((zpos + dz) % 4) * 2 + 1 - xpos for dz in (1, 2, 3)]
    gpeers = [((r // 8 + dg) % groups) * 8 + r % 8 for dg in range(1, groups)]

    counter = [0]

    def remote(src, dst, dev):
        i = counter[0]
        counter[0] += 1
        return pltpu.make_async_remote_copy(
            src_ref=src, dst_ref=dst, send_sem=send_sems.at[i], recv_sem=recv_sems.at[i],
            device_id=dev, device_id_type=MESH)

    local_count = [0]

    def local(src, dst):
        i = local_count[0]
        local_count[0] += 1
        c = pltpu.make_async_copy(src, dst, local_sems.at[i])
        c.start()
        return c

    spot, steps = [0], []

    def chain(name, *links):
        steps.append([fn for fn, _ in links])

    def live(*names):
        pass

    def take(i):
        for number in PLAN[i] if i < len(PLAN) else ():
            steps[number].pop(0)()

    def point():
        spot[0] += 1
        take(spot[0] - 1)

    def must(*names):
        point()

    def run(name, count, body, polls=None):
        first = spot[0]
        spot[0] += count

        def step(b, carry):
            body(b)
            for i in range(count):
                if i in (polls or {}) or (first + i < len(PLAN) and PLAN[first + i]):
                    @pl.when(b == i)
                    def _():
                        if i in (polls or {}):
                            polls[i]()
                        take(first + i)
            return carry

        lax.fori_loop(0, count, step, 0)

    def once(name, fn):
        fn()
        point()

    pending = []

    def go(copy):
        copy.start()
        pending.append(copy)
        return copy

    load_x = local(x_in, x)
    load_wp = local(wp_in, wp)
    load_eg = local(eg_in, eg)
    barrier = pltpu.get_barrier_semaphore()
    friends = [(r, tc), (r, ty), (r, tdiag), (rx, t)] + [(zp, t) for zp in zpeers + xzpeers] + [(gp_, t) for gp_ in gpeers]
    for dev in friends:
        pl.semaphore_signal(barrier, inc=1, device_id=dev, device_id_type=MESH)
    pl.semaphore_wait(barrier, len(friends))

    shared[t, 0:2, :] = ab_in[...]
    shared[t, 2:6, :] = bup_in[...]
    bias_moves = [go(remote(shared.at[t], shared.at[t], (r, dev))) for dev in (tc, ty, tdiag)]
    full = {"qkv": wqkv, "wo": wo, "up": wup, "dn": wdn}
    given = {"qkv": wqkv_in, "wo": wo_in, "up": wup_in, "dn": wdn_in}

    def shard(name, s, piece=None):
        ref = full[name]
        if name in ("qkv", "up"):
            rows_ = pl.ds(0, D) if piece is None else pl.ds(piece * (D // 4), D // 4)
            if name == "qkv":
                return ref.at[:, rows_, pl.ds(pl.multiple_of(s * 128, 128), 128)]
            return ref.at[rows_, pl.ds(pl.multiple_of(s * (FF // 4), 128), FF // 4)]
        n = (D if name == "wo" else FF) // 4
        if piece is None:
            return ref.at[pl.ds(s * n, n)]
        return ref.at[pl.ds(s * n + piece * (n // 4), n // 4)]

    def own_piece(name, piece):
        ref = given[name]
        if name == "qkv":
            return ref.at[:, pl.ds(piece * (D // 4), D // 4)]
        n = ref.shape[0] // 4
        return ref.at[pl.ds(piece * n, n)]

    class Gather:
        def __init__(self, name):
            self.name = name
            self.y = remote(own_piece(name, quad), shard(name, t, quad), (r, ty))
            self.c = remote(given[name], shard(name, t), (r, tc))
            mine = shard(name, ty, quad)
            self.x = [remote(mine, mine, (dev, t)) for dev in (rx, rz, rxz)]
            self.f = [remote(mine, mine, (r, tc))]
            for dev in (rx, rz, rxz):
                got = shard(name, ty, dev % 4)
                self.f.append(remote(got, got, (r, tc)))
            chain(name, (self.step1, [self.y]), *[(functools.partial(self.step2, i), [self.x[i]]) for i in range(3)])

        def begin(self):
            go(self.y)
            go(self.c)
            self.loc = local(given[self.name], shard(self.name, t))
            live(self.name)

        def step1(self):
            self.y.wait_recv()
            for c in self.x:
                go(c)
            go(self.f[0])

        def step2(self, i):
            self.x[i].wait_recv()
            go(self.f[i + 1])

        def near(self):
            self.loc.wait()
            self.c.wait_recv()

        def ready(self):
            for c in self.f:
                c.wait_recv()

    w_qkv = Gather("qkv")
    w_o = Gather("wo")
    w_up = Gather("up")
    w_dn = Gather("dn")
    for w in (w_qkv, w_o, w_up):
        w.begin()

    for i, ref in enumerate((v0_in, v1_in, v2_in, v3_in, v4_in, v5_in)):
        vec[i:i + 1, :] = ref[...].reshape(1, D)

    def row(i):
        return vec[i:i + 1, :]

    load_x.wait()

    class Halo:
        def __init__(self, pairs):
            self.left = [remote(a, b, (r, (t + 3) % 4)) for a, b, _, _ in pairs]
            self.right = [remote(c, d, (r, (t + 1) % 4)) for _, _, c, d in pairs]

        def send(self, i):
            pl.when(t > 0)(self.left[i].start)
            pl.when(t < 3)(self.right[i].start)

        def wait(self, i):
            pl.when(t > 0)(self.right[i].wait_recv)
            pl.when(t < 3)(self.left[i].wait_recv)

        def arrivals(self, name):
            for i in range(2):
                chain(name + str(i), (functools.partial(self.wait, i), [self.left[i], self.right[i]]))

        def sent(self):
            for i in range(2):
                pl.when(t > 0)(self.left[i].wait_send)
                pl.when(t < 3)(self.right[i].wait_send)

    HR = RH // 2

    def edges(i, first):
        return nw.at[pl.ds(i * HR, HR), pl.ds(first, HALO)]

    halo = Halo([(edges(i, HALO), edges(i, HALO + LS), edges(i, LS), edges(i, 0)) for i in range(2)])

    halo.arrivals("fore")

    def ln1(b):
        xs = x[pl.ds(b * BT, BT), :].astype(F32)
        unit, _ = normalize(xs)
        out = (unit * row(1) + row(2)).astype(BF)
        nw[pl.ds(b * BR, BR), HALO:HALO + LS, :] = out.reshape(BR, LS, D)

    run("ln1", NB, ln1, {NB // 2 - 1: lambda: halo.send(0), NB - 1: lambda: (halo.send(1), live("fore0", "fore1"))})

    @pl.when(t == 0)
    def _():
        nw[:, 0:HALO, :] = jnp.zeros((RH, HALO, D), BF)

    @pl.when(t == 3)
    def _():
        nw[:, HALO + LS:W, :] = jnp.zeros((RH, HALO, D), BF)

    PH = RH * SEGS // 2
    load_wp.wait()
    load_eg.wait()

    class PoolSum:
        def __init__(self, name, terms, r1, r2, out):
            self.terms, self.r1, self.r2, self.out = terms, r1, r2, out
            mine, theirs = pl.ds(core * PH, PH), pl.ds((1 - core) * PH, PH)
            self.mine = mine
            self.a = remote(terms.at[theirs], r1, (r, tc))
            self.b = remote(terms.at[mine], r2, (r, ty))
            self.c = remote(out.at[mine], out.at[mine], (r, tc))
            chain(name, (self.step2, [self.a]), (self.step3, [self.b]))

        def step1(self):
            go(self.a)

        def step2(self):
            self.a.wait_recv()
            self.terms[self.mine, :] = (self.terms[self.mine, :].astype(F32) + self.r1[...].astype(F32)).astype(BF)
            go(self.b)

        def step3(self):
            self.b.wait_recv()
            self.out[self.mine, :] = (self.terms[self.mine, :].astype(F32) + self.r2[...].astype(F32)).astype(BF)
            go(self.c)

        def ready(self):
            self.c.wait_recv()

    gpool = PoolSum("gpool", gpt, gpr1, gpr2, gps)
    pooled = PoolSum("pooled", pt, pr1, pr2, ps)
    smalls[...] = jnp.zeros(smalls.shape, F32)

    def pool_back():
        smalls[pl.ds(12 + t, 1), :] = total(eg[...].astype(F32))
        gpt[...] = mm_t(eg[...], wp[...]).astype(BF)

    once("pool_back", pool_back)
    gpool.step1()

    load_hg = local(hg_in, hg)
    w_qkv.near()
    live("gpool")
    point()

    labels = lab_in[...]
    SL = labels.shape[1]
    window = pltpu.roll(labels, (SL + HALO - t * LS) % SL, 1)[:, 0:W].astype(F32)
    own_lab = pltpu.roll(labels, (SL - t * LS) % SL, 1)[:, 0:W].astype(F32)
    before = pltpu.roll(labels, (SL + 1 - t * LS) % SL, 1)[:, 0:W].astype(F32)
    codes[...] = jnp.where(own_lab == before, -1.0, own_lab)
    columns = jnp.transpose(own_lab)
    for i in range(RH):
        mask[i * LS:(i + 1) * LS, :] = jnp.where(columns[0:LS, i:i + 1] == window[i:i + 1, :], 0.0, -1e30)

    for copy in bias_moves:
        copy.wait_recv()
    for s in range(4):
        for i in range(2):
            vec[6 + i:7 + i, s * 128:(s + 1) * 128] = shared[s, i:i + 1, :]
        for i in range(4):
            bup[s:s + 1, i * 128:(i + 1) * 128] = shared[s, 2 + i:3 + i, :]

    point()

    near = pl.ds(pl.multiple_of(ypos * H2, H2), H2)
    far = pl.ds(pl.multiple_of((1 - ypos) * H2, H2), H2)

    def project_own(cols, b):
        own = nw[pl.ds(b * BR, BR), HALO:HALO + LS, :].reshape(BT, D)
        q[pl.ds(b * BT, BT), cols] = ((mm(own, wqkv[0, :, cols]) + vec[6:7, cols]) * (HEAD_DIM ** -0.5)).astype(BF)
        ks = mm(own, wqkv[1, :, cols]).astype(BF)
        vs = (mm(own, wqkv[2, :, cols]) + vec[7:8, cols]).astype(BF)
        k[pl.ds(b * BR, BR), HALO:HALO + LS, cols] = ks.reshape(BR, LS, H2)
        v[pl.ds(b * BR, BR), HALO:HALO + LS, cols] = vs.reshape(BR, LS, H2)

    def project_halo(cols, b):
        rows_ = pl.ds(b * BR, BR)
        both = jnp.concatenate([nw[rows_, 0:HALO, :], nw[rows_, HALO + LS:W, :]], axis=0).reshape(BR * 2 * HALO, D)
        ks = mm(both, wqkv[1, :, cols]).astype(BF).reshape(2, BR, HALO, H2)
        vs = (mm(both, wqkv[2, :, cols]) + vec[7:8, cols]).astype(BF).reshape(2, BR, HALO, H2)
        k[rows_, 0:HALO, cols] = ks[0]
        k[rows_, HALO + LS:W, cols] = ks[1]
        v[rows_, 0:HALO, cols] = vs[0]
        v[rows_, HALO + LS:W, cols] = vs[1]

    lane = lax.broadcasted_iota(jnp.int32, (1, H2), 1) // HEAD_DIM
    heads = [(lane == h).astype(F32).astype(BF) for h in range(4)]

    def spread_heads(block):
        return jnp.concatenate([block * heads[h] for h in range(4)], axis=0)

    def merge_heads(stack):
        parts = [stack[h * LS:(h + 1) * LS, :] for h in range(4)]
        out = jnp.where(lane == 0, parts[0], parts[1])
        out = jnp.where(lane == 2, parts[2], out)
        return jnp.where(lane == 3, parts[3], out)

    def attend(half, cols, i):
        rows4 = [i * 4 + n for n in range(4)]
        scores = []
        for n in rows4:
            m1 = mask[pl.ds(n * LS, LS), :]
            qs = spread_heads(q[pl.ds(n * LS, LS), cols])
            scores.append(mm_t(qs, k[n, :, cols]) + jnp.concatenate([m1] * 4, axis=0))
        tops = [jnp.max(sc, axis=-1, keepdims=True) for sc in scores]
        es = [jnp.exp(sc - top) for sc, top in zip(scores, tops)]
        inv = [1.0 / jnp.sum(e, axis=-1, keepdims=True) for e in es]
        ws = [(e * f).astype(BF) for e, f in zip(es, inv)]
        outs = []
        for n, w in zip(rows4, ws):
            p[pl.ds((n * 2 + half) * 4 * LS, 4 * LS), :] = w
            outs.append(mm(w, v[n, :, cols]))
        for n, o in zip(rows4, outs):
            at[pl.ds(n * LS, LS), cols] = merge_heads(o).astype(BF)

    HB = NB // 2
    AB = RH // 8
    run("own_near", NB, lambda b: project_own(near, b))
    w_dn.begin()
    must("fore0")
    run("halo_near", HB, lambda b: project_halo(near, b))
    run("attend", AB, lambda i: attend(ypos, near, i))
    must("fore1")
    run("halo_near", HB, lambda b: project_halo(near, b + HB))
    run("attend", AB, lambda i: attend(ypos, near, i + AB))
    must("qkv")
    w_qkv.ready()
    run("own_far", NB, lambda b: project_own(far, b))
    run("halo_far", NB, lambda b: project_halo(far, b))
    run("attend", 2 * AB, lambda i: attend(1 - ypos, far, i))
    ids = lax.broadcasted_iota(jnp.int32, (SEGS, LS), 0).astype(F32)

    def chosen(n):
        return (ids == codes[pl.ds(n, 1), 0:LS]).astype(F32).astype(BF)

    must("gpool")
    gpool.ready()
    load_hg.wait()

    def place(b):
        rows_ = pl.ds(b * BT, BT)
        put = [t_mm(chosen(b * BR + n), gps[pl.ds((b * BR + n) * SEGS, SEGS), :]) for n in range(BR)]
        g = hg[rows_, :].astype(F32) + jnp.concatenate(put, axis=0)
        low = g.astype(BF)
        hg[rows_, :] = low
        smalls[5:6, :] += total(low.astype(F32))

    run("place", NB, place)

    must("wo", "up")
    for w in (w_o, w_up):
        w.near()
        w.ready()

    FC = FF // 4
    def feed_up(b):
        rows_ = pl.ds(b * BT, BT)
        middle = x[rows_, :].astype(F32) + (mm(at[rows_, :], wo[...]) + row(0))
        mid[rows_, :] = middle
        unit, _ = normalize(middle)
        normed = (unit * row(3) + row(4)).astype(BF)
        nf[rows_, :] = normed
        for j in range(4):
            cols = slice(j * FC, (j + 1) * FC)
            u = mm(normed, wup[:, cols]) + bup[j:j + 1, :]
            u2 = u * u
            th = jnp.tanh(u * (ROOT + (ROOT * CUBE) * u2))
            half_up = 0.5 + 0.5 * th
            a = u * half_up
            act[rows_, cols] = a.astype(BF)
            dact[rows_, cols] = (half_up + (a - a * half_up) * (2.0 * ROOT + (6.0 * CUBE * ROOT) * u2)).astype(BF)

    def feed_down(b):
        rows_ = pl.ds(b * BT, BT)
        low = (mid[rows_, :] + (mm(act[rows_, :], wdn[...]) + row(5))).astype(BF)
        hid[rows_, :] = low
        for n in range(BR):
            first = chosen(b * BR + n)
            pt[pl.ds((b * BR + n) * SEGS, SEGS), :] = mm(first, low[n * LS:(n + 1) * LS, :]).astype(BF)

    run("feed_up", NB, feed_up)
    gb = hg

    mine = {"y": ypos, "h": zh, "l": zl, "x": xpos}
    partner = {"y": (r, ty), "h": (z2, t), "l": (z1, t), "x": (rx, t)}
    own_part = (zh, zl, xpos)

    class Reduce:
        def __init__(self, name, g, r1, bufs, o):
            self.name, self.g, self.r1, self.bufs, self.o = name, g, r1, bufs, o
            axes = "hlx" if r1 is None else "yhlx"
            lead = () if r1 is None else (core,)
            over, gather = ORDERS[name]

            def at(fixed, flip=""):
                return tuple(1 - mine[a] if a == flip else mine[a] if a in fixed else slice(None) for a in axes)

            def peer(dz):
                z = (zpos + dz) % 4
                return (z // 2, z % 2, xpos)

            near_copies = []
            if r1 is not None:
                self.a1 = remote(g.at[1 - core, 1 - ypos], r1.at[1 - ypos], (r, tc))
                self.a2 = remote(g.at[1 - core, ypos], r1.at[ypos], (r, tc))
                near_copies = [self.a1] if over[0] == "y" else [self.a1, self.a2]
            moves, fixed, regions = [], "", []
            for i, d in enumerate(over):
                if d == "Z":
                    tail_at = at(fixed)[:-3] + ()
                    moves.append([remote(g.at[lead + tail_at + peer(dz)], bufs[i].at[dz - 1], (zpeers[dz - 1], t)) for dz in (1, 2, 3)])
                    fixed += "hl"
                else:
                    moves.append([remote(g.at[lead + at(fixed, d)], bufs[i], partner[d])])
                    fixed += d
                regions.append(at(fixed))
            links = [(functools.partial(self.first, lead, at("", over[0]), near_copies, moves[0]), near_copies)]
            for i in range(1, len(over)):
                wait_for = moves[i - 1] + ([self.a2] if r1 is not None and i == 1 and over[0] == "y" else [])
                links.append((functools.partial(self.middle, lead, regions[i - 1], i, wait_for, moves[i]), wait_for))
            gathers, got = [], ""
            for d in gather:
                place_at = tuple(slice(None) if a in got else mine[a] for a in "hlx")
                if d == "Z":
                    gathers.append([remote(o.at[place_at], o.at[place_at], (zpeers[dz - 1], t)) for dz in (1, 2, 3)])
                    got += "hl"
                else:
                    gathers.append([remote(o.at[place_at], o.at[place_at], partner[d])])
                    got += d
            if groups > 1:
                self.m = [remote(o.at[own_part], r5[name].at[i], (gpeers[i], t)) for i in range(groups - 1)]
            links.append((functools.partial(self.last, lead, regions[-1], over[-1] == "Z", moves[-1], gathers[0]), moves[-1]))
            for i in range(1, len(gather)):
                links.append((functools.partial(self.gather, gathers[i - 1], gathers[i]), gathers[i - 1]))
            links.append((functools.partial(self.finish, gathers[-1]), gathers[-1]))
            chain(name, *links)

        def core1(self):
            go(self.a1)

        def core2(self):
            go(self.a2)

        def first(self, lead, region, awaited, moves):
            for c in awaited:
                c.wait_recv()
            if self.r1 is not None:
                self.g[lead + region] = (self.g[lead + region].astype(F32) + self.r1[region].astype(F32)).astype(BF)
            go(moves[0])

        def middle(self, lead, region, i, awaited, moves):
            for c in awaited:
                c.wait_recv()
            acc = self.g[lead + region].astype(F32) + self.bufs[i - 1][...].astype(F32)
            if self.r1 is not None and i == 1:
                acc = acc + self.r1[region].astype(F32)
            self.g[lead + region] = acc.astype(BF)
            for c in moves:
                go(c)

        def last(self, lead, region, direct, awaited, moves):
            acc = self.g[lead + region].astype(F32)
            for i, c in enumerate(awaited):
                c.wait_recv()
                acc = acc + (self.bufs[-1][i] if direct else self.bufs[-1][...]).astype(F32)
            self.o[own_part] = acc.astype(BF)
            if groups > 1:
                for c in self.m:
                    c.start()
                for c in self.m:
                    c.wait()
                acc = self.o[own_part].astype(F32)
                for i in range(groups - 1):
                    acc = acc + r5[self.name][i].astype(F32)
                self.o[own_part] = acc.astype(BF)
            for c in moves:
                go(c)

        def gather(self, awaited, moves):
            for c in awaited:
                c.wait_recv()
            for c in moves:
                go(c)

        def finish(self, awaited):
            for c in awaited:
                c.wait_recv()
            stores.append(local(self.o, final[self.name]))

    HC = D // 2

    def halves(out, i):
        return out.at[:, :, :, :, pl.ds(i * HC, HC)]

    final = {"dna": halves(gdn_out, 0), "dnb": halves(gdn_out, 1), "upa": halves(gup_out, 0), "upb": halves(gup_out, 1),
             "o": go_out, "q": gq_out, "k": gk_out, "v": gv_out, "pl": gpl_out}
    stores = []
    red = {}
    for name in NAMES:
        held = sets[name]
        if name == "pl":
            held = [held[0], None] + held[1:]
        red[name] = Reduce(name, held[0], held[1], held[2:-1], held[-1])

    def split(names, cs, ys, val):
        for i, name in enumerate(names):
            g = sets[name][0]
            g[cs, ys] = val[:, i * HC:(i + 1) * HC].astype(BF).reshape(g.shape[2:])

    def place_of(i):
        return (core + 1 + i // 2) % 2, (ypos + 1 + i) % 2

    def down_grad(i):
        cs, ys = place_of(i)
        val = t_mm(act[:, pl.ds(pl.multiple_of((ys * 2 + cs) * FC, FC), FC)], gb[...])
        split(("dna", "dnb"), cs, ys, val)

    def near_cores(*names):
        return lambda: [red[n].core1() for n in names], lambda: [red[n].core2() for n in names]

    send1, send2 = near_cores("dna", "dnb")
    run("down_grad", 4, down_grad, {0: send1, 1: send2, 2: lambda: live("dnb"), 3: lambda: live("dna")})
    must("dn")
    w_dn.near()
    w_dn.ready()
    run("feed_down", NB, feed_down)
    store_hid = local(hid, hid_out)
    pooled.step1()
    live("pooled")

    def feed_back(b):
        rows_ = pl.ds(b * BT, BT)
        g = gb[rows_, :]
        acc = jnp.zeros((BT, D), F32)
        for j in range(4):
            cols = slice(j * FC, (j + 1) * FC)
            ga = mm_t(g, wdn[cols, :])
            gp = (ga * dact[rows_, cols].astype(F32)).astype(BF)
            dact[rows_, cols] = gp
            smalls[8 + j:9 + j, :] += total(gp.astype(F32))
            acc = acc + mm_t(gp, wup[:, cols])
        unit, factor = normalize(mid[rows_, :])
        smalls[3:4, :] += total(acc * unit)
        smalls[4:5, :] += total(acc)
        gm = g.astype(F32) + norm_back(acc, unit, factor, row(3))
        mid[rows_, :] = gm
        low = gm.astype(BF)
        gma[rows_, :] = low
        smalls[0:1, :] += total(low.astype(F32))
        gat[rows_, :] = mm_t(low, wo[...]).astype(BF)

    run("feed_back", NB, feed_back)
    def up_grad(i):
        cs, ys = place_of(i)
        val = t_mm(nf[...], dact[:, pl.ds(pl.multiple_of((ys * 2 + cs) * FC, FC), FC)])
        split(("upa", "upb"), cs, ys, val)

    send3, send4 = near_cores("upa", "upb")
    run("up_grad", 4, up_grad, {0: send3, 1: send4, 2: lambda: live("upb"), 3: lambda: live("upa")})

    def out_grad():
        val = t_mm(at[...], gma[...]).astype(BF)
        for s in range(4):
            g = sets["o"][0]
            g[s % 2, s // 2] = val[s * (D // 4):(s + 1) * (D // 4), :].reshape(g.shape[2:])
        red["o"].core1()
        red["o"].core2()
        live("o")

    once("out_grad", out_grad)

    must("pooled")
    pooled.ready()

    def embed():
        emb[...] = (mm(ps[...], wp[...]) + bp_in[...].reshape(1, D)).astype(BF)
        sets["pl"][0][...] = t_mm(ps[...], eg[...]).astype(BF).reshape(sets["pl"][0].shape)
        live("pl")

    once("embed", embed)
    store_emb = local(emb, emb_out)

    def attend_back(i):
        work = [(i * 2 + n, half) for n in range(2) for half in range(2)]
        sides = [slice(half * H2, (half + 1) * H2) for _, half in work]
        qss = [spread_heads(q[pl.ds(n * LS, LS), c]) for (n, _), c in zip(work, sides)]
        gss = [spread_heads(gat[pl.ds(n * LS, LS), c]) for (n, _), c in zip(work, sides)]
        ws = [p[pl.ds((n * 2 + half) * 4 * LS, 4 * LS), :] for n, half in work]
        gws = [mm_t(g, v[n, :, c]) for g, (n, _), c in zip(gss, work, sides)]
        wfs = [w.astype(F32) for w in ws]
        prods = [w * g for w, g in zip(wfs, gws)]
        sums = [jnp.sum(pr, axis=-1, keepdims=True) for pr in prods]
        dss = [(pr - w * sm).astype(BF) for pr, w, sm in zip(prods, wfs, sums)]
        dvs = [t_mm(w, g).astype(BF) for w, g in zip(ws, gss)]
        dqs = [mm(ds, k[n, :, c]) for ds, (n, _), c in zip(dss, work, sides)]
        dks = [t_mm(ds, qq).astype(BF) for ds, qq in zip(dss, qss)]
        for (n, _), c, dq, dk, dv in zip(work, sides, dqs, dks, dvs):
            q[pl.ds(n * LS, LS), c] = (merge_heads(dq) * (HEAD_DIM ** -0.5)).astype(BF)
            k[n, :, c] = dk
            v[n, :, c] = dv

    run("attend_back", RH // 2, attend_back)

    back = Halo([tuple(ref.at[pl.ds(i * HR, HR)] for ref in (halo_l, halo_fr, halo_r, halo_fl)) for i in range(2)])
    back.arrivals("back")

    def norm_grad(b):
        keys = pl.ds(b * BR, BR)
        dqs = q[pl.ds(b * BT, BT), :]
        dks, dvs = k[keys].reshape(BR * W, D), v[keys].reshape(BR * W, D)
        smalls[6:7, :] += total(dqs.astype(F32))
        smalls[7:8, :] += total(dvs.astype(F32))
        win = (mm_t(dks, wqkv[1]) + mm_t(dvs, wqkv[2])).reshape(BR, W, D)
        own = win[:, HALO:HALO + LS, :].reshape(BT, D) + mm_t(dqs, wqkv[0])
        gat[pl.ds(b * BT, BT), :] = own.astype(BF)
        halo_l[keys] = win[:, 0:HALO, :].astype(BF)
        halo_r[keys] = win[:, HALO + LS:W, :].astype(BF)

    def put_at(g, val):
        low = val.astype(BF)
        for s in range(4):
            g[s % 2, s // 2] = low[:, s * 128:(s + 1) * 128].reshape(g.shape[2:])

    def put_value():
        put_at(sets["v"][0], t_mm(nw[...].reshape(RH * W, D), v[...].reshape(RH * W, D)))
        red["v"].core1()
        red["v"].core2()
        live("v")

    def put_key():
        put_at(sets["k"][0], t_mm(nw[...].reshape(RH * W, D), k[...].reshape(RH * W, D)))
        red["k"].core1()
        red["k"].core2()
        live("k")

    def put_query():
        put_at(sets["q"][0], t_mm(nw[:, HALO:HALO + LS, :].reshape(T, D), q[...]))
        red["q"].core1()
        red["q"].core2()
        live("q")

    once("put_v", put_value)
    once("put_k", put_key)
    once("put_q", put_query)
    run("norm_grad", NB, norm_grad, {HB - 1: lambda: back.send(0), NB - 1: lambda: (back.send(1), live("back0", "back1"))})

    @pl.when(t == 0)
    def _():
        halo_fl[...] = jnp.zeros(halo_fl.shape, BF)

    @pl.when(t == 3)
    def _():
        halo_fr[...] = jnp.zeros(halo_fr.shape, BF)

    class Small:
        name = "sm"

        def __init__(self):
            self.copies = [[remote(smalls, sm_r.at[0], (r, tc))], [remote(smalls, sm_r.at[1], (r, ty))],
                           [remote(smalls, sm_r.at[2], (rx, t))],
                           [remote(smalls, sm_r.at[2 + dz], (zpeers[dz - 1], t)) for dz in (1, 2, 3)]]
            chain("sm", *[(functools.partial(self.step, i), self.copies[i]) for i in range(4)])

        def send(self, i):
            for c in self.copies[i]:
                c.start()

        def step(self, i):
            for c in self.copies[i]:
                c.wait()
            if i < 3:
                smalls[...] += sm_r[i]
                self.send(i + 1)
            else:
                smalls[...] += sm_r[3] + sm_r[4] + sm_r[5]
                across(smalls, "sm")
                stores.append(local(smalls, sm_out))

    class Late:
        name = "late"

        def __init__(self):
            self.a = [remote(late, late_tp.at[i], (r, dev)) for i, dev in enumerate((tc, ty, tdiag))]
            self.b = [remote(late, late_rows.at[i], (dev, t)) for i, dev in enumerate([rx] + zpeers + xzpeers)]
            chain("late", (self.over_tp, self.a), (self.over_rows, self.b))

        def over_tp(self):
            for c in self.a:
                c.wait()
            late[...] += late_tp[0] + late_tp[1] + late_tp[2]
            for c in self.b:
                c.start()

        def over_rows(self):
            for c in self.b:
                c.wait()
            for i in range(7):
                late[...] += late_rows[i]
            across(late, "late")
            stores.append(local(late, late_out))

    def across(ref, name):
        moves = [remote(ref, r5[name].at[i], (gpeers[i], t)) for i in range(groups - 1)]
        for c in moves:
            c.start()
        for c in moves:
            c.wait()
        for i in range(groups - 1):
            ref[...] += r5[name][i]

    small, lates = Small(), Late()
    small.send(0)
    live("sm")
    late[...] = jnp.zeros(late.shape, F32)

    def ln1_back(b):
        rows_ = pl.ds(b * BT, BT)
        grp = pl.ds(b * BR, BR)
        g = gat[rows_, :].astype(F32).reshape(BR, LS, D)
        g = jnp.concatenate([g[:, 0:HALO, :] + halo_fl[grp].astype(F32), g[:, HALO:LS, :] + halo_fr[grp].astype(F32)], axis=1)
        g = g.reshape(BT, D)
        unit, factor = normalize(x[rows_, :].astype(F32))
        late[0:1, :] += total(g * unit)
        late[1:2, :] += total(g)
        nf[rows_, :] = (mid[rows_, :] + norm_back(g, unit, factor, row(1))).astype(BF)

    must("back0")
    run("ln1_back", HB, ln1_back)
    must("back1")
    run("ln1_back", HB, lambda b: ln1_back(b + HB))
    store_ig = local(nf, ig_out)
    for c in lates.a:
        c.start()
    live("late")
    must(*NAMES, "sm", "late")
    for c in pending:
        c.wait_send()
    halo.sent()
    back.sent()
    for c in stores + [store_hid, store_emb, store_ig]:
        c.wait()


def per_device(rows_size, layer_input, segment_labels, attend_weight, attend_bias, out_weight, out_bias, gain_attention,
               shift_attention, gain_feed, shift_feed, up_weight, up_bias, down_weight, down_bias, pool_weight, pool_bias,
               hidden_grad, embedding_grad):
    RH, LS, D = layer_input.shape
    SEGS = embedding_grad.shape[1]
    OC = pool_weight.shape[1]
    FS = up_weight.shape[1]
    FF = FS * 4
    W = LS + 2 * HALO
    T = RH * LS
    NB = RH // 8
    groups = rows_size // 8
    t = lax.axis_index("tp")
    part = (D // 8, D // 4)
    chunk = {"dna": (FS // 8, D // 2), "dnb": (FS // 8, D // 2), "upa": (D // 8, FS // 2), "upb": (D // 8, FS // 2), "o": (D // 32, D), "q": part, "k": part, "v": part, "pl": (D // 8, OC)}
    any_, vmem = pl.BlockSpec(memory_space=pl.ANY), pl.BlockSpec(memory_space=pltpu.VMEM)

    def buf(*shape, dtype=BF):
        return pltpu.VMEM(shape, dtype)

    scratch = [
        buf(T, D), buf(T, D), buf(RH * SEGS, OC), buf(T, W, dtype=F32), buf(RH, W, dtype=F32),
        buf(3, D, D), buf(D, D), buf(D, FF), buf(FF, D), buf(D, OC), buf(4, 8, 128, dtype=F32), buf(8, D, dtype=F32), buf(4, FS, dtype=F32),
        buf(RH, W, D), buf(T, D), buf(RH, W, D), buf(RH, W, D), buf(RH * 2 * 4 * LS, W), buf(T, D), buf(T, D, dtype=F32),
        buf(T, D), buf(T, FF), buf(T, FF), buf(T, D), buf(T, D), buf(T, D),
        buf(RH, HALO, D), buf(RH, HALO, D), buf(RH, HALO, D), buf(RH, HALO, D),
    ]
    for _ in range(2):
        scratch += [buf(RH * SEGS, D), buf(RH * SEGS // 2, D), buf(RH * SEGS // 2, D), buf(RH * SEGS, D)]
    scratch += [buf(RH * SEGS, OC), buf(16, D, dtype=F32), buf(6, 16, D, dtype=F32), buf(2, D, dtype=F32), buf(3, 2, D, dtype=F32), buf(7, 2, D, dtype=F32)]
    for name in NAMES:
        c, over = chunk[name], ORDERS[name][0]
        left = 3 if name == "pl" else 4
        scratch += [buf(*[2] * 3, *c)] if name == "pl" else [buf(2, *[2] * 4, *c), buf(*[2] * 4, *c)]
        for i, d in enumerate(over):
            scratch.append(buf(3, *c) if d == "Z" else buf(*[2] * (left - 1 - i), *c))
        scratch.append(buf(2, 2, 2, *c))
    if groups > 1:
        scratch += [buf(groups - 1, *chunk[name]) for name in NAMES]
        scratch += [buf(groups - 1, 16, D, dtype=F32), buf(groups - 1, 2, D, dtype=F32)]
    n_remote = 4 * 9 + 3 + 8 + 6 + 9 * 11 + 6 + 10 + 11 * (groups - 1)
    scratch += [pltpu.SemaphoreType.DMA((n_remote,)), pltpu.SemaphoreType.DMA((n_remote,)), pltpu.SemaphoreType.DMA((24,))]

    def out(*shape, dtype=BF):
        return jax.ShapeDtypeStruct(shape, dtype)

    flops = 30 * T * D * FF
    hid, emb, ig, gdn, gup, go_, gq, gk, gv, gpl, sm, late = pl.pallas_call(
        functools.partial(layer_kernel, (groups, RH, LS, D, FF, SEGS)),
        out_shape=[out(T, D), out(RH * SEGS, OC), out(T, D)]
        + [out(2, 2, 2, FS // 8, D), out(2, 2, 2, D // 8, FS)] + [out(2, 2, 2, *chunk[name]) for name in ("o", "q", "k", "v", "pl")]
        + [out(16, D, dtype=F32), out(2, D, dtype=F32)],
        in_specs=[any_, vmem, any_, vmem, any_] + [vmem] * 5 + [any_, vmem, any_, vmem, any_, vmem, any_, any_],
        out_specs=[any_] * 12,
        scratch_shapes=scratch,
        compiler_params=pltpu.CompilerParams(collective_id=0, has_side_effects=True, vmem_limit_bytes=63 * 2 ** 20),
        cost_estimate=pl.CostEstimate(flops=flops, bytes_accessed=20 * 2 ** 20, transcendentals=T * FF),
        name="layer",
    )(layer_input.reshape(T, D), segment_labels, attend_weight, attend_bias, out_weight, out_bias, gain_attention,
      shift_attention, gain_feed, shift_feed, up_weight, up_bias.reshape(4, FS // 4), down_weight, down_bias,
      pool_weight, pool_bias, hidden_grad.reshape(T, D), embedding_grad.reshape(RH * SEGS, OC))

    grads = [gq, gk, gv, go_, gup, gdn, gpl]
    flat = [(D, D // 4)] * 3 + [(D // 4, D), (D, FS), (FS, D), (D, OC)]
    grads = [g.reshape(shape) for g, shape in zip(grads, flat)]
    whole = [hid.reshape(RH, LS, D), emb.reshape(RH, SEGS, OC), ig.reshape(RH, LS, D)]
    vecs = [D] * 6 + [FS, OC]
    made = pl.pallas_call(
        last_kernel,
        out_shape=[out(*w.shape) for w in whole] + [out(3, D, D // 4, dtype=F32)] + [out(*shape, dtype=F32) for shape in flat[3:]]
        + [out(2, D // 4, dtype=F32)] + [out(n, dtype=F32) for n in vecs],
        in_specs=[any_] * 10 + [vmem] * 2,
        out_specs=[any_] * 8 + [vmem] * 9,
        scratch_shapes=[buf(*shape) for shape in flat] + [buf(*shape, dtype=F32) for shape in flat]
        + [buf(*w.shape) for w in whole] + [pltpu.SemaphoreType.DMA((20,))],
        compiler_params=pltpu.CompilerParams(vmem_limit_bytes=60 * 2 ** 20),
        cost_estimate=pl.CostEstimate(flops=T * D, bytes_accessed=11 * 2 ** 20, transcendentals=0),
        name="last",
    )(*whole, *grads, sm, late)
    hid, emb, ig, gat, go_, gup, gdn, gpl, gab, gob, ga, sa, gf, sf, gdb, gub, gpb = made
    return (hid, emb, ig, gat, gab, go_, gob, ga, sa, gf, sf, gup, gub, gdn, gdb, gpl, gpb)


def last_kernel(*refs):
    whole_in, grads_in, (sm, late), refs = refs[:3], refs[3:10], refs[10:12], refs[12:]
    whole_out, (at_out, *rest), (gab, *vec_out), refs = refs[:3], refs[3:8], refs[8:17], refs[17:]
    low, wide, held, sems = refs[:7], refs[7:14], refs[14:17], refs[17]
    t = lax.axis_index("tp")
    copies = [pltpu.make_async_copy(a, b, sems.at[i]) for i, (a, b) in enumerate(zip(grads_in, low))]
    loads = [pltpu.make_async_copy(a, b, sems.at[14 + i]) for i, (a, b) in enumerate(zip(whole_in, held))]
    for c in loads + copies:
        c.start()
    n = gab.shape[1]
    gab[...] = sm[6:8, pl.ds(pl.multiple_of(t * n, 128), n)]
    rows = [sm[0:1, :], late[0:1, :], late[1:2, :], sm[3:4, :], sm[4:5, :], sm[5:6, :], sm[pl.ds(8 + t, 1), :], sm[pl.ds(12 + t, 1), :]]
    for ref, value in zip(vec_out, rows):
        ref[...] = value.reshape(ref.shape)
    targets = [at_out.at[0], at_out.at[1], at_out.at[2]] + rest
    stores = []
    for i, c in enumerate(loads):
        c.wait()
        stores.append(pltpu.make_async_copy(held[i], whole_out[i], sems.at[17 + i]))
        stores[-1].start()
    for i, c in enumerate(copies):
        c.wait()
        wide[i][...] = low[i][...].astype(F32)
        stores.append(pltpu.make_async_copy(wide[i], targets[i], sems.at[7 + i]))
        stores[-1].start()
    for c in stores:
        c.wait()


def solution(mesh):
    placed = (
        P("rows", "tp", None), P("rows", None), P(None, None, "tp"), P(None, "tp"), P("tp", None), P(), P(), P(), P(), P(),
        P(None, "tp"), P("tp"), P("tp", None), P(), P(None, "tp"), P("tp"), P("rows", "tp", None), P("rows", None, "tp"),
    )
    return jax.shard_map(
        functools.partial(per_device, mesh.shape["rows"]),
        mesh=mesh,
        in_specs=placed,
        out_specs=(
            P("rows", "tp", None), P("rows", None, "tp"), P("rows", "tp", None), P(None, None, "tp"), P(None, "tp"),
            P("tp", None), P(), P(), P(), P(), P(), P(None, "tp"), P("tp"), P("tp", None), P(), P(None, "tp"), P("tp"),
        ),
        check_vma=False,
    )
```

```python
import functools
import math

import jax
import jax.numpy as jnp
from jax import lax
from jax.experimental import pallas as pl
from jax.experimental.pallas import tpu as pltpu
from jax.sharding import PartitionSpec as P

MESH = pl.DeviceIdType.MESH
HEAD_DIM = 64
HALO = 32
EPS = 1e-5
BF = jnp.bfloat16
F32 = jnp.float32
ROOT = math.sqrt(2.0 / math.pi)
CUBE = 0.044715
NAMES = ("dna", "dnb", "upa", "upb", "o", "q", "k", "v", "pl")
ORDERS = {
    "dna": ("lxhy", "hlx"),
    "dnb": ("xlhy", "hlx"),
    "upa": ("xyZ", "hlx"),
    "upb": ("ylxh", "hxl"),
    "o": ("xylh", "Zx"),
    "q": ("yxZ", "xZ"),
    "k": ("yxZ", "xhl"),
    "v": ("xlyh", "Zx"),
    "pl": ("lxh", "hlx"),
}
PLAN = (
    (),
    (),
    (),
    (),
    (6, 0),
    (1,),
    (),
    (4,),
    (),
    (),
    (0, 0),
    (2, 1, 1, 0, 5),
    (1,),
    (),
    (),
    (),
    (2, 2),
    (),
    (),
    (),
    (6, 2),
    (),
    (),
    (3,),
    (),
    (),
    (),
    (),
    (3, 3),
    (),
    (3,),
    (),
    (),
    (),
    (),
    (8, 9),
    (),
    (7,),
    (8, 9),
    (),
    (),
    (),
    (11, 10),
    (7, 8, 17, 9),
    (),
    (16, 12),
    (),
    (),
    (),
    (),
    (8,),
    (10, 11, 17),
    (),
    (9,),
    (8, 17, 12, 16),
    (10, 9, 15),
    (14, 11, 8, 12),
    (13, 16, 17),
    (15, 14),
    (10, 8, 11, 12, 9, 19),
    (),
    (),
    (14, 16, 15, 13, 10, 11, 9, 12, 20),
    (15, 13, 14),
    (8, 10, 16, 9, 18, 14, 11, 12, 15, 10, 13, 16, 11, 18, 12, 13, 14, 15, 11, 16, 13, 14, 15),
)


def mm(a, b):
    return jnp.dot(a, b, preferred_element_type=F32)


def mm_t(a, b):
    return lax.dot_general(a, b, (((1,), (1,)), ((), ())), preferred_element_type=F32)


def t_mm(a, b):
    return lax.dot_general(a, b, (((0,), (0,)), ((), ())), preferred_element_type=F32)


def normalize(values):
    mean = jnp.mean(values, axis=-1, keepdims=True)
    centred = values - mean
    spread = jnp.mean(centred * centred, axis=-1, keepdims=True)
    factor = lax.rsqrt(spread + EPS)
    return centred * factor, factor


def norm_back(grad, unit, factor, gain):
    scaled = grad * gain
    first = jnp.mean(scaled, axis=-1, keepdims=True)
    second = jnp.mean(scaled * unit, axis=-1, keepdims=True)
    return factor * (scaled - first - unit * second)


def total(values):
    return jnp.sum(values, axis=0, keepdims=True)


def layer_kernel(dims, *refs):
    (groups, RH, LS, D, FF, SEGS) = dims
    W = LS + 2 * HALO
    (x_in, lab_in, wqkv_in, ab_in, wo_in, v0_in, v1_in, v2_in, v3_in, v4_in, wup_in, bup_in, wdn_in, v5_in, wp_in, bp_in, hg_in, eg_in,
     hid_out, emb_out, ig_out, gdn_out, gup_out, go_out, gq_out, gk_out, gv_out, gpl_out, sm_out, late_out,
     lab, ab, bup_own, bp, vec_own, x, hg, eg, mask, codes, wqkv, wo, wup, wdn, wp, shared, vec, bup,
     nw, q, k, v, p, at, mid, nf, act, dact, gma, gat, hid,
     halo_l, halo_r, halo_fl, halo_fr,
     gpt, gpr1, gpr2, gps, pt, pr1, pr2, ps, emb,
     smalls, sm_r, late, late_tp, late_rows,
     *tail) = refs
    tail = list(tail)
    sets = {}
    for name in NAMES:
        sets[name] = [tail.pop(0) for _ in range(len(ORDERS[name][0]) + (2 if name == "pl" else 3))]
    if groups > 1:
        r5 = {name: tail.pop(0) for name in NAMES + ("sm", "late")}
    send_sems, recv_sems, local_sems = tail
    T = RH * LS
    BR = 8
    NB = RH // BR
    BT = BR * LS
    H2 = 4 * HEAD_DIM

    r, t = lax.axis_index("rows"), lax.axis_index("tp")
    core, ypos = t % 2, t // 2
    tc = t + 1 - 2 * core
    ty = (t + 2) % 4
    tdiag = 3 - t
    xpos = r % 2
    rx = r + 1 - 2 * xpos
    zpos = (r // 2) % 4
    base = (r // 8) * 8
    zpeers = [base + ((zpos + dz) % 4) * 2 + xpos for dz in (1, 2, 3)]
    quad = r % 4
    rz = r + 2 - 4 * (quad // 2)
    rxz = rz + 1 - 2 * xpos
    zh, zl = zpos // 2, zpos % 2
    z1 = base + (zpos + 1 - 2 * zl) * 2 + xpos
    z2 = base + ((zpos + 2) % 4) * 2 + xpos
    xzpeers = [base + ((zpos + dz) % 4) * 2 + 1 - xpos for dz in (1, 2, 3)]
    gpeers = [((r // 8 + dg) % groups) * 8 + r % 8 for dg in range(1, groups)]

    counter = [0]

    def remote(src, dst, dev):
        i = counter[0]
        counter[0] += 1
        return pltpu.make_async_remote_copy(
            src_ref=src, dst_ref=dst, send_sem=send_sems.at[i], recv_sem=recv_sems.at[i],
            device_id=dev, device_id_type=MESH)

    local_count = [0]

    def later(src, dst):
        i = local_count[0]
        local_count[0] += 1
        return pltpu.make_async_copy(src, dst, local_sems.at[i])

    def local(src, dst):
        c = later(src, dst)
        c.start()
        return c

    def store(copy):
        copy.start()
        stores.append(copy)

    spot, steps = [0], []

    def chain(name, *links):
        steps.append([fn for fn, _ in links])

    def live(*names):
        pass

    def take(i):
        for number in PLAN[i] if i < len(PLAN) else ():
            steps[number].pop(0)()

    def point():
        spot[0] += 1
        take(spot[0] - 1)

    def must(*names):
        point()

    def run(name, count, body, polls=None):
        first = spot[0]
        spot[0] += count

        def step(b, carry):
            body(b)
            for i in range(count):
                if i in (polls or {}) or (first + i < len(PLAN) and PLAN[first + i]):
                    @pl.when(b == i)
                    def _():
                        if i in (polls or {}):
                            polls[i]()
                        take(first + i)
            return carry

        lax.fori_loop(0, count, step, 0)

    def once(name, fn):
        fn()
        point()

    pending = []

    def go(copy):
        copy.start()
        pending.append(copy)
        return copy

    load_own = [local(ab_in, ab), local(bup_in, bup_own)]
    load_x = local(x_in, x)
    load_vec = [local(ref, vec_own.at[i]) for i, ref in enumerate((v0_in, v1_in, v2_in, v3_in, v4_in, v5_in))]
    load_lab = [local(lab_in, lab), local(bp_in, bp)]
    load_wp = local(wp_in, wp)
    load_eg = local(eg_in, eg)
    barrier = pltpu.get_barrier_semaphore()
    friends = [(r, tc), (r, ty), (r, tdiag), (rx, t)] + [(zp, t) for zp in zpeers + xzpeers] + [(gp_, t) for gp_ in gpeers]
    for dev in friends:
        pl.semaphore_signal(barrier, inc=1, device_id=dev, device_id_type=MESH)
    pl.semaphore_wait(barrier, len(friends))

    for c in load_own:
        c.wait()
    shared[t, 0:2, :] = ab[...]
    shared[t, 2:6, :] = bup_own[...]
    bias_moves = [go(remote(shared.at[t], shared.at[t], (r, dev))) for dev in (tc, ty, tdiag)]
    full = {"qkv": wqkv, "wo": wo, "up": wup, "dn": wdn}
    given = {"qkv": wqkv_in, "wo": wo_in, "up": wup_in, "dn": wdn_in}

    def shard(name, s, piece=None):
        ref = full[name]
        if name in ("qkv", "up"):
            rows_ = pl.ds(0, D) if piece is None else pl.ds(piece * (D // 4), D // 4)
            if name == "qkv":
                return ref.at[:, rows_, pl.ds(pl.multiple_of(s * 128, 128), 128)]
            return ref.at[rows_, pl.ds(pl.multiple_of(s * (FF // 4), 128), FF // 4)]
        n = (D if name == "wo" else FF) // 4
        if piece is None:
            return ref.at[pl.ds(s * n, n)]
        return ref.at[pl.ds(s * n + piece * (n // 4), n // 4)]

    def own_piece(name, piece):
        ref = given[name]
        if name == "qkv":
            return ref.at[:, pl.ds(piece * (D // 4), D // 4)]
        n = ref.shape[0] // 4
        return ref.at[pl.ds(piece * n, n)]

    class Gather:
        def __init__(self, name):
            self.name = name
            self.y = remote(own_piece(name, quad), shard(name, t, quad), (r, ty))
            self.c = remote(given[name], shard(name, t), (r, tc))
            self.loc = later(given[name], shard(name, t))
            mine = shard(name, ty, quad)
            self.x = [remote(mine, mine, (dev, t)) for dev in (rx, rz, rxz)]
            self.f = [remote(mine, mine, (r, tc))]
            for dev in (rx, rz, rxz):
                got = shard(name, ty, dev % 4)
                self.f.append(remote(got, got, (r, tc)))
            chain(name, (self.step1, [self.y]), *[(functools.partial(self.step2, i), [self.x[i]]) for i in range(3)])

        def begin(self):
            go(self.y)
            go(self.c)
            self.loc.start()
            live(self.name)

        def step1(self):
            self.y.wait_recv()
            for c in self.x:
                go(c)
            go(self.f[0])

        def step2(self, i):
            self.x[i].wait_recv()
            go(self.f[i + 1])

        def near(self):
            self.loc.wait()
            self.c.wait_recv()

        def ready(self):
            for c in self.f:
                c.wait_recv()

    w_qkv = Gather("qkv")
    w_o = Gather("wo")
    w_up = Gather("up")
    w_dn = Gather("dn")
    for w in (w_qkv, w_o):
        w.begin()

    for c in load_vec + load_lab:
        c.wait()
    vec[0:6, :] = vec_own[...]

    def row(i):
        return vec[i:i + 1, :]

    load_x.wait()

    class Halo:
        def __init__(self, pairs):
            self.left = [remote(a, b, (r, (t + 3) % 4)) for a, b, _, _ in pairs]
            self.right = [remote(c, d, (r, (t + 1) % 4)) for _, _, c, d in pairs]

        def send(self, i):
            pl.when(t > 0)(self.left[i].start)
            pl.when(t < 3)(self.right[i].start)

        def wait(self, i):
            pl.when(t > 0)(self.right[i].wait_recv)
            pl.when(t < 3)(self.left[i].wait_recv)

        def arrivals(self, name):
            for i in range(2):
                chain(name + str(i), (functools.partial(self.wait, i), [self.left[i], self.right[i]]))

        def sent(self):
            for i in range(2):
                pl.when(t > 0)(self.left[i].wait_send)
                pl.when(t < 3)(self.right[i].wait_send)

    HR = RH // 2

    def edges(i, first):
        return nw.at[pl.ds(i * HR, HR), pl.ds(first, HALO)]

    halo = Halo([(edges(i, HALO), edges(i, HALO + LS), edges(i, LS), edges(i, 0)) for i in range(2)])

    halo.arrivals("fore")

    def ln1(b):
        xs = x[pl.ds(b * BT, BT), :].astype(F32)
        unit, _ = normalize(xs)
        out = (unit * row(1) + row(2)).astype(BF)
        nw[pl.ds(b * BR, BR), HALO:HALO + LS, :] = out.reshape(BR, LS, D)

    run("ln1", NB, ln1, {NB // 2 - 1: lambda: (halo.send(0), w_up.begin()), NB - 1: lambda: (halo.send(1), live("fore0", "fore1"))})

    @pl.when(t == 0)
    def _():
        nw[:, 0:HALO, :] = jnp.zeros((RH, HALO, D), BF)

    @pl.when(t == 3)
    def _():
        nw[:, HALO + LS:W, :] = jnp.zeros((RH, HALO, D), BF)

    PH = RH * SEGS // 2
    load_wp.wait()
    load_eg.wait()

    class PoolSum:
        def __init__(self, name, terms, r1, r2, out):
            self.terms, self.r1, self.r2, self.out = terms, r1, r2, out
            mine, theirs = pl.ds(core * PH, PH), pl.ds((1 - core) * PH, PH)
            self.mine = mine
            self.a = remote(terms.at[theirs], r1, (r, tc))
            self.b = remote(terms.at[mine], r2, (r, ty))
            self.c = remote(out.at[mine], out.at[mine], (r, tc))
            chain(name, (self.step2, [self.a]), (self.step3, [self.b]))

        def step1(self):
            go(self.a)

        def step2(self):
            self.a.wait_recv()
            self.terms[self.mine, :] = (self.terms[self.mine, :].astype(F32) + self.r1[...].astype(F32)).astype(BF)
            go(self.b)

        def step3(self):
            self.b.wait_recv()
            self.out[self.mine, :] = (self.terms[self.mine, :].astype(F32) + self.r2[...].astype(F32)).astype(BF)
            go(self.c)

        def ready(self):
            self.c.wait_recv()

    gpool = PoolSum("gpool", gpt, gpr1, gpr2, gps)
    pooled = PoolSum("pooled", pt, pr1, pr2, ps)
    smalls[...] = jnp.zeros(smalls.shape, F32)

    def pool_back():
        smalls[pl.ds(12 + t, 1), :] = total(eg[...].astype(F32))
        gpt[...] = mm_t(eg[...], wp[...]).astype(BF)

    once("pool_back", pool_back)
    gpool.step1()

    load_hg = local(hg_in, hg)
    w_qkv.near()
    live("gpool")
    point()

    labels = lab[...]
    SL = labels.shape[1]
    window = pltpu.roll(labels, (SL + HALO - t * LS) % SL, 1)[:, 0:W].astype(F32)
    own_lab = pltpu.roll(labels, (SL - t * LS) % SL, 1)[:, 0:W].astype(F32)
    before = pltpu.roll(labels, (SL + 1 - t * LS) % SL, 1)[:, 0:W].astype(F32)
    codes[...] = jnp.where(own_lab == before, -1.0, own_lab)
    columns = jnp.transpose(own_lab)
    for i in range(RH):
        mask[i * LS:(i + 1) * LS, :] = jnp.where(columns[0:LS, i:i + 1] == window[i:i + 1, :], 0.0, -1e30)

    for copy in bias_moves:
        copy.wait_recv()
    for s in range(4):
        for i in range(2):
            vec[6 + i:7 + i, s * 128:(s + 1) * 128] = shared[s, i:i + 1, :]
        for i in range(4):
            bup[s:s + 1, i * 128:(i + 1) * 128] = shared[s, 2 + i:3 + i, :]

    point()

    near = pl.ds(pl.multiple_of(ypos * H2, H2), H2)
    far = pl.ds(pl.multiple_of((1 - ypos) * H2, H2), H2)

    def project_own(cols, b):
        own = nw[pl.ds(b * BR, BR), HALO:HALO + LS, :].reshape(BT, D)
        q[pl.ds(b * BT, BT), cols] = ((mm(own, wqkv[0, :, cols]) + vec[6:7, cols]) * (HEAD_DIM ** -0.5)).astype(BF)
        ks = mm(own, wqkv[1, :, cols]).astype(BF)
        vs = (mm(own, wqkv[2, :, cols]) + vec[7:8, cols]).astype(BF)
        k[pl.ds(b * BR, BR), HALO:HALO + LS, cols] = ks.reshape(BR, LS, H2)
        v[pl.ds(b * BR, BR), HALO:HALO + LS, cols] = vs.reshape(BR, LS, H2)

    def project_halo(cols, b):
        rows_ = pl.ds(b * BR, BR)
        both = jnp.concatenate([nw[rows_, 0:HALO, :], nw[rows_, HALO + LS:W, :]], axis=0).reshape(BR * 2 * HALO, D)
        ks = mm(both, wqkv[1, :, cols]).astype(BF).reshape(2, BR, HALO, H2)
        vs = (mm(both, wqkv[2, :, cols]) + vec[7:8, cols]).astype(BF).reshape(2, BR, HALO, H2)
        k[rows_, 0:HALO, cols] = ks[0]
        k[rows_, HALO + LS:W, cols] = ks[1]
        v[rows_, 0:HALO, cols] = vs[0]
        v[rows_, HALO + LS:W, cols] = vs[1]

    lane = lax.broadcasted_iota(jnp.int32, (1, H2), 1) // HEAD_DIM
    heads = [(lane == h).astype(F32).astype(BF) for h in range(4)]

    def spread_heads(block):
        return jnp.concatenate([block * heads[h] for h in range(4)], axis=0)

    def merge_heads(stack):
        parts = [stack[h * LS:(h + 1) * LS, :] for h in range(4)]
        out = jnp.where(lane == 0, parts[0], parts[1])
        out = jnp.where(lane == 2, parts[2], out)
        return jnp.where(lane == 3, parts[3], out)

    def attend(half, cols, i):
        rows4 = [i * 4 + n for n in range(4)]
        scores = []
        for n in rows4:
            m1 = mask[pl.ds(n * LS, LS), :]
            qs = spread_heads(q[pl.ds(n * LS, LS), cols])
            scores.append(mm_t(qs, k[n, :, cols]) + jnp.concatenate([m1] * 4, axis=0))
        tops = [jnp.max(sc, axis=-1, keepdims=True) for sc in scores]
        es = [jnp.exp(sc - top) for sc, top in zip(scores, tops)]
        inv = [1.0 / jnp.sum(e, axis=-1, keepdims=True) for e in es]
        ws = [(e * f).astype(BF) for e, f in zip(es, inv)]
        outs = []
        for n, w in zip(rows4, ws):
            p[pl.ds((n * 2 + half) * 4 * LS, 4 * LS), :] = w
            outs.append(mm(w, v[n, :, cols]))
        for n, o in zip(rows4, outs):
            at[pl.ds(n * LS, LS), cols] = merge_heads(o).astype(BF)

    HB = NB // 2
    AB = RH // 8
    run("own_near", NB, lambda b: project_own(near, b))
    w_dn.begin()
    must("fore0")
    run("halo_near", HB, lambda b: project_halo(near, b))
    run("attend", AB, lambda i: attend(ypos, near, i))
    must("fore1")
    run("halo_near", HB, lambda b: project_halo(near, b + HB))
    run("attend", AB, lambda i: attend(ypos, near, i + AB))
    must("qkv")
    w_qkv.ready()
    run("own_far", NB, lambda b: project_own(far, b))
    run("halo_far", NB, lambda b: project_halo(far, b))
    run("attend", 2 * AB, lambda i: attend(1 - ypos, far, i))
    ids = lax.broadcasted_iota(jnp.int32, (SEGS, LS), 0).astype(F32)

    def chosen(n):
        return (ids == codes[pl.ds(n, 1), 0:LS]).astype(F32).astype(BF)

    must("gpool")
    gpool.ready()
    load_hg.wait()

    def place(b):
        rows_ = pl.ds(b * BT, BT)
        put = [t_mm(chosen(b * BR + n), gps[pl.ds((b * BR + n) * SEGS, SEGS), :]) for n in range(BR)]
        g = hg[rows_, :].astype(F32) + jnp.concatenate(put, axis=0)
        low = g.astype(BF)
        hg[rows_, :] = low
        smalls[5:6, :] += total(low.astype(F32))

    run("place", NB, place)

    must("wo", "up")
    for w in (w_o, w_up):
        w.near()
        w.ready()

    FC = FF // 4
    def feed_up(b):
        rows_ = pl.ds(b * BT, BT)
        middle = x[rows_, :].astype(F32) + (mm(at[rows_, :], wo[...]) + row(0))
        mid[rows_, :] = middle
        unit, _ = normalize(middle)
        normed = (unit * row(3) + row(4)).astype(BF)
        nf[rows_, :] = normed
        for j in range(4):
            cols = slice(j * FC, (j + 1) * FC)
            u = mm(normed, wup[:, cols]) + bup[j:j + 1, :]
            u2 = u * u
            th = jnp.tanh(u * (ROOT + (ROOT * CUBE) * u2))
            half_up = 0.5 + 0.5 * th
            a = u * half_up
            act[rows_, cols] = a.astype(BF)
            dact[rows_, cols] = (half_up + (a - a * half_up) * (2.0 * ROOT + (6.0 * CUBE * ROOT) * u2)).astype(BF)

    def feed_down(b):
        rows_ = pl.ds(b * BT, BT)
        low = (mid[rows_, :] + (mm(act[rows_, :], wdn[...]) + row(5))).astype(BF)
        hid[rows_, :] = low
        for n in range(BR):
            first = chosen(b * BR + n)
            pt[pl.ds((b * BR + n) * SEGS, SEGS), :] = mm(first, low[n * LS:(n + 1) * LS, :]).astype(BF)

    run("feed_up", NB, feed_up)
    gb = hg

    mine = {"y": ypos, "h": zh, "l": zl, "x": xpos}
    partner = {"y": (r, ty), "h": (z2, t), "l": (z1, t), "x": (rx, t)}
    own_part = (zh, zl, xpos)

    class Reduce:
        def __init__(self, name, g, r1, bufs, o):
            self.name, self.g, self.r1, self.bufs, self.o = name, g, r1, bufs, o
            axes = "hlx" if r1 is None else "yhlx"
            lead = () if r1 is None else (core,)
            over, gather = ORDERS[name]

            def at(fixed, flip=""):
                return tuple(1 - mine[a] if a == flip else mine[a] if a in fixed else slice(None) for a in axes)

            def peer(dz):
                z = (zpos + dz) % 4
                return (z // 2, z % 2, xpos)

            near_copies = []
            if r1 is not None:
                self.a1 = remote(g.at[1 - core, 1 - ypos], r1.at[1 - ypos], (r, tc))
                self.a2 = remote(g.at[1 - core, ypos], r1.at[ypos], (r, tc))
                near_copies = [self.a1] if over[0] == "y" else [self.a1, self.a2]
            moves, fixed, regions = [], "", []
            for i, d in enumerate(over):
                if d == "Z":
                    tail_at = at(fixed)[:-3] + ()
                    moves.append([remote(g.at[lead + tail_at + peer(dz)], bufs[i].at[dz - 1], (zpeers[dz - 1], t)) for dz in (1, 2, 3)])
                    fixed += "hl"
                else:
                    moves.append([remote(g.at[lead + at(fixed, d)], bufs[i], partner[d])])
                    fixed += d
                regions.append(at(fixed))
            links = [(functools.partial(self.first, lead, at("", over[0]), near_copies, moves[0]), near_copies)]
            for i in range(1, len(over)):
                wait_for = moves[i - 1] + ([self.a2] if r1 is not None and i == 1 and over[0] == "y" else [])
                links.append((functools.partial(self.middle, lead, regions[i - 1], i, wait_for, moves[i]), wait_for))
            gathers, got = [], ""
            for d in gather:
                place_at = tuple(slice(None) if a in got else mine[a] for a in "hlx")
                if d == "Z":
                    gathers.append([remote(o.at[place_at], o.at[place_at], (zpeers[dz - 1], t)) for dz in (1, 2, 3)])
                    got += "hl"
                else:
                    gathers.append([remote(o.at[place_at], o.at[place_at], partner[d])])
                    got += d
            if groups > 1:
                self.m = [remote(o.at[own_part], r5[name].at[i], (gpeers[i], t)) for i in range(groups - 1)]
            links.append((functools.partial(self.last, lead, regions[-1], over[-1] == "Z", moves[-1], gathers[0]), moves[-1]))
            for i in range(1, len(gather)):
                links.append((functools.partial(self.gather, gathers[i - 1], gathers[i]), gathers[i - 1]))
            links.append((functools.partial(self.finish, gathers[-1]), gathers[-1]))
            self.save = later(o, final[name])
            chain(name, *links)

        def core1(self):
            go(self.a1)

        def core2(self):
            go(self.a2)

        def first(self, lead, region, awaited, moves):
            for c in awaited:
                c.wait_recv()
            if self.r1 is not None:
                self.g[lead + region] = (self.g[lead + region].astype(F32) + self.r1[region].astype(F32)).astype(BF)
            go(moves[0])

        def middle(self, lead, region, i, awaited, moves):
            for c in awaited:
                c.wait_recv()
            acc = self.g[lead + region].astype(F32) + self.bufs[i - 1][...].astype(F32)
            if self.r1 is not None and i == 1:
                acc = acc + self.r1[region].astype(F32)
            self.g[lead + region] = acc.astype(BF)
            for c in moves:
                go(c)

        def last(self, lead, region, direct, awaited, moves):
            acc = self.g[lead + region].astype(F32)
            for i, c in enumerate(awaited):
                c.wait_recv()
                acc = acc + (self.bufs[-1][i] if direct else self.bufs[-1][...]).astype(F32)
            self.o[own_part] = acc.astype(BF)
            if groups > 1:
                for c in self.m:
                    c.start()
                for c in self.m:
                    c.wait()
                acc = self.o[own_part].astype(F32)
                for i in range(groups - 1):
                    acc = acc + r5[self.name][i].astype(F32)
                self.o[own_part] = acc.astype(BF)
            for c in moves:
                go(c)

        def gather(self, awaited, moves):
            for c in awaited:
                c.wait_recv()
            for c in moves:
                go(c)

        def finish(self, awaited):
            for c in awaited:
                c.wait_recv()
            store(self.save)

    HC = D // 2

    def halves(out, i):
        return out.at[:, :, :, :, pl.ds(i * HC, HC)]

    final = {"dna": halves(gdn_out, 0), "dnb": halves(gdn_out, 1), "upa": halves(gup_out, 0), "upb": halves(gup_out, 1),
             "o": go_out, "q": gq_out, "k": gk_out, "v": gv_out, "pl": gpl_out}
    stores = []
    red = {}
    for name in NAMES:
        held = sets[name]
        if name == "pl":
            held = [held[0], None] + held[1:]
        red[name] = Reduce(name, held[0], held[1], held[2:-1], held[-1])

    def split(names, cs, ys, val):
        for i, name in enumerate(names):
            g = sets[name][0]
            g[cs, ys] = val[:, i * HC:(i + 1) * HC].astype(BF).reshape(g.shape[2:])

    def place_of(i):
        return (core + 1 + i // 2) % 2, (ypos + 1 + i) % 2

    def down_grad(i):
        cs, ys = place_of(i)
        val = t_mm(act[:, pl.ds(pl.multiple_of((ys * 2 + cs) * FC, FC), FC)], gb[...])
        split(("dna", "dnb"), cs, ys, val)

    def near_cores(*names):
        return lambda: [red[n].core1() for n in names], lambda: [red[n].core2() for n in names]

    send1, send2 = near_cores("dna", "dnb")
    run("down_grad", 4, down_grad, {0: send1, 1: send2, 2: lambda: live("dnb"), 3: lambda: live("dna")})
    must("dn")
    w_dn.near()
    w_dn.ready()
    run("feed_down", NB, feed_down)
    store_hid = local(hid, hid_out)
    pooled.step1()
    live("pooled")

    def feed_back(b):
        rows_ = pl.ds(b * BT, BT)
        g = gb[rows_, :]
        acc = jnp.zeros((BT, D), F32)
        for j in range(4):
            cols = slice(j * FC, (j + 1) * FC)
            ga = mm_t(g, wdn[cols, :])
            gp = (ga * dact[rows_, cols].astype(F32)).astype(BF)
            dact[rows_, cols] = gp
            smalls[8 + j:9 + j, :] += total(gp.astype(F32))
            acc = acc + mm_t(gp, wup[:, cols])
        unit, factor = normalize(mid[rows_, :])
        smalls[3:4, :] += total(acc * unit)
        smalls[4:5, :] += total(acc)
        gm = g.astype(F32) + norm_back(acc, unit, factor, row(3))
        mid[rows_, :] = gm
        low = gm.astype(BF)
        gma[rows_, :] = low
        smalls[0:1, :] += total(low.astype(F32))
        gat[rows_, :] = mm_t(low, wo[...]).astype(BF)

    run("feed_back", NB, feed_back)
    def up_grad(i):
        cs, ys = place_of(i)
        val = t_mm(nf[...], dact[:, pl.ds(pl.multiple_of((ys * 2 + cs) * FC, FC), FC)])
        split(("upa", "upb"), cs, ys, val)

    send3, send4 = near_cores("upa", "upb")
    run("up_grad", 4, up_grad, {0: send3, 1: send4, 2: lambda: live("upb"), 3: lambda: live("upa")})

    def out_grad():
        val = t_mm(at[...], gma[...]).astype(BF)
        for s in range(4):
            g = sets["o"][0]
            g[s % 2, s // 2] = val[s * (D // 4):(s + 1) * (D // 4), :].reshape(g.shape[2:])
        red["o"].core1()
        red["o"].core2()
        live("o")

    late[...] = jnp.zeros(late.shape, F32)

    class Small:
        name = "sm"

        def __init__(self):
            self.save = later(smalls, sm_out)
            self.copies = [[remote(smalls, sm_r.at[0], (r, tc))], [remote(smalls, sm_r.at[1], (r, ty))],
                           [remote(smalls, sm_r.at[2], (rx, t))],
                           [remote(smalls, sm_r.at[2 + dz], (zpeers[dz - 1], t)) for dz in (1, 2, 3)]]
            chain("sm", *[(functools.partial(self.step, i), self.copies[i]) for i in range(4)])

        def send(self, i):
            for c in self.copies[i]:
                c.start()

        def step(self, i):
            for c in self.copies[i]:
                c.wait()
            if i < 3:
                smalls[...] += sm_r[i]
                self.send(i + 1)
            else:
                smalls[...] += sm_r[3] + sm_r[4] + sm_r[5]
                across(smalls, "sm")
                store(self.save)

    class Late:
        name = "late"

        def __init__(self):
            self.save = later(late, late_out)
            self.a = [remote(late, late_tp.at[i], (r, dev)) for i, dev in enumerate((tc, ty, tdiag))]
            self.b = [remote(late, late_rows.at[i], (dev, t)) for i, dev in enumerate([rx] + zpeers + xzpeers)]
            chain("late", (self.over_tp, self.a), (self.over_rows, self.b))

        def over_tp(self):
            for c in self.a:
                c.wait()
            late[...] += late_tp[0] + late_tp[1] + late_tp[2]
            for c in self.b:
                c.start()

        def over_rows(self):
            for c in self.b:
                c.wait()
            for i in range(7):
                late[...] += late_rows[i]
            across(late, "late")
            store(self.save)

    def across(ref, name):
        moves = [remote(ref, r5[name].at[i], (gpeers[i], t)) for i in range(groups - 1)]
        for c in moves:
            c.start()
        for c in moves:
            c.wait()
        for i in range(groups - 1):
            ref[...] += r5[name][i]

    small, lates = Small(), Late()
    small.send(0)
    live("sm")
    once("out_grad", out_grad)

    must("pooled")
    pooled.ready()

    def embed():
        sets["pl"][0][...] = t_mm(ps[...], eg[...]).astype(BF).reshape(sets["pl"][0].shape)
        live("pl")

    once("embed", embed)

    def attend_back(i):
        work = [(i * 2 + n, half) for n in range(2) for half in range(2)]
        sides = [slice(half * H2, (half + 1) * H2) for _, half in work]
        qss = [spread_heads(q[pl.ds(n * LS, LS), c]) for (n, _), c in zip(work, sides)]
        gss = [spread_heads(gat[pl.ds(n * LS, LS), c]) for (n, _), c in zip(work, sides)]
        ws = [p[pl.ds((n * 2 + half) * 4 * LS, 4 * LS), :] for n, half in work]
        gws = [mm_t(g, v[n, :, c]) for g, (n, _), c in zip(gss, work, sides)]
        wfs = [w.astype(F32) for w in ws]
        prods = [w * g for w, g in zip(wfs, gws)]
        sums = [jnp.sum(pr, axis=-1, keepdims=True) for pr in prods]
        dss = [(pr - w * sm).astype(BF) for pr, w, sm in zip(prods, wfs, sums)]
        dvs = [t_mm(w, g).astype(BF) for w, g in zip(ws, gss)]
        dqs = [mm(ds, k[n, :, c]) for ds, (n, _), c in zip(dss, work, sides)]
        dks = [t_mm(ds, qq).astype(BF) for ds, qq in zip(dss, qss)]
        for (n, _), c, dq, dk, dv in zip(work, sides, dqs, dks, dvs):
            q[pl.ds(n * LS, LS), c] = (merge_heads(dq) * (HEAD_DIM ** -0.5)).astype(BF)
            k[n, :, c] = dk
            v[n, :, c] = dv

    run("attend_back", RH // 2, attend_back)

    back = Halo([tuple(ref.at[pl.ds(i * HR, HR)] for ref in (halo_l, halo_fr, halo_r, halo_fl)) for i in range(2)])
    back.arrivals("back")

    def norm_grad(b):
        keys = pl.ds(b * BR, BR)
        dqs = q[pl.ds(b * BT, BT), :]
        dks, dvs = k[keys].reshape(BR * W, D), v[keys].reshape(BR * W, D)
        late[2:3, :] += total(dqs.astype(F32))
        late[3:4, :] += total(dvs.astype(F32))
        win = (mm_t(dks, wqkv[1]) + mm_t(dvs, wqkv[2])).reshape(BR, W, D)
        own = win[:, HALO:HALO + LS, :].reshape(BT, D) + mm_t(dqs, wqkv[0])
        gat[pl.ds(b * BT, BT), :] = own.astype(BF)
        halo_l[keys] = win[:, 0:HALO, :].astype(BF)
        halo_r[keys] = win[:, HALO + LS:W, :].astype(BF)

    def put_at(g, val):
        low = val.astype(BF)
        for s in range(4):
            g[s % 2, s // 2] = low[:, s * 128:(s + 1) * 128].reshape(g.shape[2:])

    def put_value():
        put_at(sets["v"][0], t_mm(nw[...].reshape(RH * W, D), v[...].reshape(RH * W, D)))
        red["v"].core1()
        red["v"].core2()
        live("v")

    def put_key():
        put_at(sets["k"][0], t_mm(nw[...].reshape(RH * W, D), k[...].reshape(RH * W, D)))
        red["k"].core1()
        red["k"].core2()
        live("k")

    def put_query():
        put_at(sets["q"][0], t_mm(nw[:, HALO:HALO + LS, :].reshape(T, D), q[...]))
        red["q"].core1()
        red["q"].core2()
        live("q")

    once("put_v", put_value)
    once("put_k", put_key)
    once("put_q", put_query)
    run("norm_grad", NB, norm_grad, {HB - 1: lambda: back.send(0), NB - 1: lambda: (back.send(1), live("back0", "back1"))})

    @pl.when(t == 0)
    def _():
        halo_fl[...] = jnp.zeros(halo_fl.shape, BF)

    @pl.when(t == 3)
    def _():
        halo_fr[...] = jnp.zeros(halo_fr.shape, BF)


    def ln1_back(b):
        rows_ = pl.ds(b * BT, BT)
        grp = pl.ds(b * BR, BR)
        g = gat[rows_, :].astype(F32).reshape(BR, LS, D)
        g = jnp.concatenate([g[:, 0:HALO, :] + halo_fl[grp].astype(F32), g[:, HALO:LS, :] + halo_fr[grp].astype(F32)], axis=1)
        g = g.reshape(BT, D)
        unit, factor = normalize(x[rows_, :].astype(F32))
        late[0:1, :] += total(g * unit)
        late[1:2, :] += total(g)
        nf[rows_, :] = (mid[rows_, :] + norm_back(g, unit, factor, row(1))).astype(BF)

    must("back0")
    run("ln1_back", HB, ln1_back)
    def embed_out():
        emb[...] = (mm(ps[...], wp[...]) + bp[...].reshape(1, D)).astype(BF)

    once("embed_out", embed_out)
    store_emb = local(emb, emb_out)
    must("back1")
    run("ln1_back", HB, lambda b: ln1_back(b + HB))
    store_ig = local(nf, ig_out)
    for c in lates.a:
        c.start()
    live("late")
    must(*NAMES, "sm", "late")
    for c in pending:
        c.wait_send()
    halo.sent()
    back.sent()
    for c in stores + [store_hid, store_emb, store_ig]:
        c.wait()


def per_device(rows_size, layer_input, segment_labels, attend_weight, attend_bias, out_weight, out_bias, gain_attention,
               shift_attention, gain_feed, shift_feed, up_weight, up_bias, down_weight, down_bias, pool_weight, pool_bias,
               hidden_grad, embedding_grad):
    RH, LS, D = layer_input.shape
    SEGS = embedding_grad.shape[1]
    OC = pool_weight.shape[1]
    FS = up_weight.shape[1]
    FF = FS * 4
    W = LS + 2 * HALO
    T = RH * LS
    NB = RH // 8
    groups = rows_size // 8
    t = lax.axis_index("tp")
    part = (D // 8, D // 4)
    chunk = {"dna": (FS // 8, D // 2), "dnb": (FS // 8, D // 2), "upa": (D // 8, FS // 2), "upb": (D // 8, FS // 2), "o": (D // 32, D), "q": part, "k": part, "v": part, "pl": (D // 8, OC)}
    any_, vmem = pl.BlockSpec(memory_space=pl.ANY), pl.BlockSpec(memory_space=pltpu.VMEM)

    def buf(*shape, dtype=BF):
        return pltpu.VMEM(shape, dtype)

    scratch = [
        pltpu.VMEM(segment_labels.shape, jnp.int32), buf(2, D // 4, dtype=F32), buf(4, FS // 4, dtype=F32), buf(OC, dtype=F32), buf(6, D, dtype=F32),
        buf(T, D), buf(T, D), buf(RH * SEGS, OC), buf(T, W, dtype=F32), buf(RH, W, dtype=F32),
        buf(3, D, D), buf(D, D), buf(D, FF), buf(FF, D), buf(D, OC), buf(4, 8, 128, dtype=F32), buf(8, D, dtype=F32), buf(4, FS, dtype=F32),
        buf(RH, W, D), buf(T, D), buf(RH, W, D), buf(RH, W, D), buf(RH * 2 * 4 * LS, W), buf(T, D), buf(T, D, dtype=F32),
        buf(T, D), buf(T, FF), buf(T, FF), buf(T, D), buf(T, D), buf(T, D),
        buf(RH, HALO, D), buf(RH, HALO, D), buf(RH, HALO, D), buf(RH, HALO, D),
    ]
    for _ in range(2):
        scratch += [buf(RH * SEGS, D), buf(RH * SEGS // 2, D), buf(RH * SEGS // 2, D), buf(RH * SEGS, D)]
    scratch += [buf(RH * SEGS, OC), buf(16, D, dtype=F32), buf(6, 16, D, dtype=F32), buf(4, D, dtype=F32), buf(3, 4, D, dtype=F32), buf(7, 4, D, dtype=F32)]
    for name in NAMES:
        c, over = chunk[name], ORDERS[name][0]
        left = 3 if name == "pl" else 4
        scratch += [buf(*[2] * 3, *c)] if name == "pl" else [buf(2, *[2] * 4, *c), buf(*[2] * 4, *c)]
        for i, d in enumerate(over):
            scratch.append(buf(3, *c) if d == "Z" else buf(*[2] * (left - 1 - i), *c))
        scratch.append(buf(2, 2, 2, *c))
    if groups > 1:
        scratch += [buf(groups - 1, *chunk[name]) for name in NAMES]
        scratch += [buf(groups - 1, 16, D, dtype=F32), buf(groups - 1, 4, D, dtype=F32)]
    n_remote = 4 * 9 + 3 + 8 + 6 + 9 * 11 + 6 + 10 + 11 * (groups - 1)
    scratch += [pltpu.SemaphoreType.DMA((n_remote,)), pltpu.SemaphoreType.DMA((n_remote,)), pltpu.SemaphoreType.DMA((48,))]

    def out(*shape, dtype=BF):
        return jax.ShapeDtypeStruct(shape, dtype)

    flops = 30 * T * D * FF
    hid, emb, ig, gdn, gup, go_, gq, gk, gv, gpl, sm, late = pl.pallas_call(
        functools.partial(layer_kernel, (groups, RH, LS, D, FF, SEGS)),
        out_shape=[out(T, D), out(RH * SEGS, OC), out(T, D)]
        + [out(2, 2, 2, FS // 8, D), out(2, 2, 2, D // 8, FS)] + [out(2, 2, 2, *chunk[name]) for name in ("o", "q", "k", "v", "pl")]
        + [out(16, D, dtype=F32), out(4, D, dtype=F32)],
        in_specs=[any_] * 18,
        out_specs=[any_] * 12,
        scratch_shapes=scratch,
        compiler_params=pltpu.CompilerParams(collective_id=0, has_side_effects=True, vmem_limit_bytes=63 * 2 ** 20),
        cost_estimate=pl.CostEstimate(flops=flops, bytes_accessed=20 * 2 ** 20, transcendentals=T * FF),
        name="layer",
    )(layer_input.reshape(T, D), segment_labels, attend_weight, attend_bias, out_weight, out_bias, gain_attention,
      shift_attention, gain_feed, shift_feed, up_weight, up_bias.reshape(4, FS // 4), down_weight, down_bias,
      pool_weight, pool_bias, hidden_grad.reshape(T, D), embedding_grad.reshape(RH * SEGS, OC))

    grads = [gq, gk, gv, go_, gup, gdn, gpl]
    flat = [(D, D // 4)] * 3 + [(D // 4, D), (D, FS), (FS, D), (D, OC)]
    grads = [g.reshape(shape) for g, shape in zip(grads, flat)]
    whole = [hid.reshape(RH, LS, D), emb.reshape(RH, SEGS, OC), ig.reshape(RH, LS, D)]
    vecs = [D] * 6 + [FS, OC]
    made = pl.pallas_call(
        last_kernel,
        out_shape=[out(*w.shape) for w in whole] + [out(3, D, D // 4, dtype=F32)] + [out(*shape, dtype=F32) for shape in flat[3:]]
        + [out(2, D // 4, dtype=F32)] + [out(n, dtype=F32) for n in vecs],
        in_specs=[any_] * 12,
        out_specs=[any_] * 17,
        scratch_shapes=[buf(*shape) for shape in flat] + [buf(*shape, dtype=F32) for shape in flat]
        + [buf(*w.shape) for w in whole] + [buf(16, D, dtype=F32), buf(4, D, dtype=F32), pltpu.SemaphoreType.DMA((31,))],
        compiler_params=pltpu.CompilerParams(vmem_limit_bytes=60 * 2 ** 20),
        cost_estimate=pl.CostEstimate(flops=T * D, bytes_accessed=11 * 2 ** 20, transcendentals=0),
        name="last",
    )(*whole, *grads, sm, late)
    hid, emb, ig, gat, go_, gup, gdn, gpl, gab, gob, ga, sa, gf, sf, gdb, gub, gpb = made
    return (hid, emb, ig, gat, gab, go_, gob, ga, sa, gf, sf, gup, gub, gdn, gdb, gpl, gpb)


def last_kernel(*refs):
    whole_in, grads_in, small_in, refs = refs[:3], refs[3:10], refs[10:12], refs[12:]
    whole_out, (at_out, *rest), (gab, *vec_out), refs = refs[:3], refs[3:8], refs[8:17], refs[17:]
    low, wide, held, (sm, late, sems) = refs[:7], refs[7:14], refs[14:17], refs[17:]
    t = lax.axis_index("tp")
    number = [0]

    def copy(src, dst):
        c = pltpu.make_async_copy(src, dst, sems.at[number[0]])
        number[0] += 1
        c.start()
        return c

    copies = [copy(a, b) for a, b in zip(grads_in, low)]
    small = [copy(a, b) for a, b in zip(small_in, (sm, late))]
    loads = [copy(a, b) for a, b in zip(whole_in, held)]
    targets = [at_out.at[0], at_out.at[1], at_out.at[2]] + rest
    stores = []
    for i in (4, 5, 6, 3, 0, 1, 2):
        copies[i].wait()
        wide[i][...] = low[i][...].astype(F32)
        stores.append(copy(wide[i], targets[i]))
    for c in small:
        c.wait()
    n = gab.shape[1]
    stores.append(copy(late.at[2:4, pl.ds(pl.multiple_of(t * n, 128), n)], gab))
    rows = [sm.at[0], late.at[0], late.at[1], sm.at[3], sm.at[4], sm.at[5], sm.at[8 + t], sm.at[12 + t]]
    stores += [copy(a, b) for a, b in zip(rows, vec_out)]
    for i, c in enumerate(loads):
        c.wait()
        stores.append(copy(held[i], whole_out[i]))
    for c in stores:
        c.wait()


def solution(mesh):
    placed = (
        P("rows", "tp", None), P("rows", None), P(None, None, "tp"), P(None, "tp"), P("tp", None), P(), P(), P(), P(), P(),
        P(None, "tp"), P("tp"), P("tp", None), P(), P(None, "tp"), P("tp"), P("rows", "tp", None), P("rows", None, "tp"),
    )
    return jax.shard_map(
        functools.partial(per_device, mesh.shape["rows"]),
        mesh=mesh,
        in_specs=placed,
        out_specs=(
            P("rows", "tp", None), P("rows", None, "tp"), P("rows", "tp", None), P(None, None, "tp"), P(None, "tp"),
            P("tp", None), P(), P(), P(), P(), P(), P(None, "tp"), P("tp"), P("tp", None), P(), P(None, "tp"), P("tp"),
        ),
        check_vma=False,
    )
```

```python
import functools
import math

import jax
import jax.numpy as jnp
from jax import lax
from jax.experimental import pallas as pl
from jax.experimental.pallas import tpu as pltpu
from jax.sharding import PartitionSpec as P

MESH = pl.DeviceIdType.MESH
HEAD_DIM = 64
HALO = 32
EPS = 1e-5
BF = jnp.bfloat16
F32 = jnp.float32
ROOT = math.sqrt(2.0 / math.pi)
CUBE = 0.044715
NAMES = ("dna", "dnb", "upa", "upb", "o", "q", "k", "v", "pl")
ORDERS = {
    "dna": ("lxhy", "hlx"),
    "dnb": ("xlhy", "hlx"),
    "upa": ("xyZ", "hlx"),
    "upb": ("ylxh", "hxl"),
    "o": ("xylh", "Zx"),
    "q": ("yxZ", "xZ"),
    "k": ("yxZ", "xhl"),
    "v": ("xlyh", "Zx"),
    "pl": ("lxh", "hlx"),
}
PLAN = (
    (),
    (),
    (),
    (),
    (6, 0),
    (1,),
    (),
    (4,),
    (),
    (),
    (0, 0),
    (2, 1, 1, 0, 5),
    (1,),
    (),
    (),
    (),
    (2, 2),
    (),
    (),
    (),
    (6, 2),
    (),
    (),
    (3,),
    (),
    (),
    (),
    (),
    (3, 3),
    (),
    (3,),
    (),
    (),
    (),
    (),
    (8, 9),
    (),
    (7,),
    (8, 9),
    (),
    (),
    (),
    (11, 10),
    (7, 8, 17, 9),
    (),
    (16, 12),
    (),
    (),
    (),
    (),
    (8,),
    (10, 11, 17),
    (),
    (9,),
    (8, 17, 12, 16),
    (10, 9, 15),
    (14, 11, 8, 12),
    (13, 16, 17),
    (15, 14),
    (10, 8, 11, 12, 9, 19),
    (),
    (),
    (14, 16, 15, 13, 10, 11, 9, 12, 20),
    (15, 13, 14),
    (8, 10, 16, 9, 18, 14, 11, 12, 15, 10, 13, 16, 11, 18, 12, 13, 14, 15, 11, 16, 13, 14, 15),
)


def mm(a, b):
    return jnp.dot(a, b, preferred_element_type=F32)


def mm_t(a, b):
    return lax.dot_general(a, b, (((1,), (1,)), ((), ())), preferred_element_type=F32)


def t_mm(a, b):
    return lax.dot_general(a, b, (((0,), (0,)), ((), ())), preferred_element_type=F32)


def normalize(values):
    mean = jnp.mean(values, axis=-1, keepdims=True)
    centred = values - mean
    spread = jnp.mean(centred * centred, axis=-1, keepdims=True)
    factor = lax.rsqrt(spread + EPS)
    return centred * factor, factor


def norm_back(grad, unit, factor, gain):
    scaled = grad * gain
    first = jnp.mean(scaled, axis=-1, keepdims=True)
    second = jnp.mean(scaled * unit, axis=-1, keepdims=True)
    return factor * (scaled - first - unit * second)


def total(values):
    return jnp.sum(values, axis=0, keepdims=True)


def layer_kernel(dims, *refs):
    (groups, RH, LS, D, FF, SEGS) = dims
    W = LS + 2 * HALO
    (x_in, lab_in, wqkv_in, ab_in, wo_in, v0_in, v1_in, v2_in, v3_in, v4_in, wup_in, bup_in, wdn_in, v5_in, wp_in, bp_in, hg_in, eg_in,
     hid_out, emb_out, ig_out, gdn_out, gup_out, go_out, gq_out, gk_out, gv_out, gpl_out, sm_out, late_out,
     lab, ab, bup_own, bp, vec_own, x, hg, eg, mask, codes, wqkv, wo, wup, wdn, wp, shared, vec, bup,
     nw, q, k, v, p, at, mid, nf, act, dact, gma, gat, hid,
     halo_l, halo_r, halo_fl, halo_fr,
     gpt, gpr1, gpr2, gps, pt, pr1, pr2, ps, emb,
     smalls, sm_r, late, late_tp, late_rows,
     *tail) = refs
    tail = list(tail)
    sets = {}
    for name in NAMES:
        sets[name] = [tail.pop(0) for _ in range(len(ORDERS[name][0]) + (2 if name == "pl" else 3))]
    if groups > 1:
        r5 = {name: tail.pop(0) for name in NAMES + ("sm", "late")}
    send_sems, recv_sems, local_sems = tail
    T = RH * LS
    BR = 8
    NB = RH // BR
    BT = BR * LS
    H2 = 4 * HEAD_DIM

    r, t = lax.axis_index("rows"), lax.axis_index("tp")
    core, ypos = t % 2, t // 2
    tc = t + 1 - 2 * core
    ty = (t + 2) % 4
    tdiag = 3 - t
    xpos = r % 2
    rx = r + 1 - 2 * xpos
    zpos = (r // 2) % 4
    base = (r // 8) * 8
    zpeers = [base + ((zpos + dz) % 4) * 2 + xpos for dz in (1, 2, 3)]
    quad = r % 4
    rz = r + 2 - 4 * (quad // 2)
    rxz = rz + 1 - 2 * xpos
    zh, zl = zpos // 2, zpos % 2
    z1 = base + (zpos + 1 - 2 * zl) * 2 + xpos
    z2 = base + ((zpos + 2) % 4) * 2 + xpos
    xzpeers = [base + ((zpos + dz) % 4) * 2 + 1 - xpos for dz in (1, 2, 3)]
    gpeers = [((r // 8 + dg) % groups) * 8 + r % 8 for dg in range(1, groups)]

    counter = [0]

    def remote(src, dst, dev):
        i = counter[0]
        counter[0] += 1
        return pltpu.make_async_remote_copy(
            src_ref=src, dst_ref=dst, send_sem=send_sems.at[i], recv_sem=recv_sems.at[i],
            device_id=dev, device_id_type=MESH)

    local_count = [0]

    def later(src, dst):
        i = local_count[0]
        local_count[0] += 1
        return pltpu.make_async_copy(src, dst, local_sems.at[i])

    def local(src, dst):
        c = later(src, dst)
        c.start()
        return c

    def store(copy):
        copy.start()
        stores.append(copy)

    spot, steps = [0], []

    def chain(name, *links):
        steps.append([fn for fn, _ in links])

    def live(*names):
        pass

    def take(i):
        for number in PLAN[i] if i < len(PLAN) else ():
            steps[number].pop(0)()

    def point():
        spot[0] += 1
        take(spot[0] - 1)

    def must(*names):
        point()

    def run(name, count, body, polls=None):
        first = spot[0]
        spot[0] += count

        def step(b, carry):
            body(b)
            for i in range(count):
                if i in (polls or {}) or (first + i < len(PLAN) and PLAN[first + i]):
                    @pl.when(b == i)
                    def _():
                        if i in (polls or {}):
                            polls[i]()
                        take(first + i)
            return carry

        lax.fori_loop(0, count, step, 0)

    def once(name, fn):
        fn()
        point()

    pending = []

    def go(copy):
        copy.start()
        pending.append(copy)
        return copy

    load_own = [local(ab_in, ab), local(bup_in, bup_own)]
    load_x = local(x_in, x)
    load_vec = [local(ref, vec_own.at[i]) for i, ref in enumerate((v0_in, v1_in, v2_in, v3_in, v4_in, v5_in))]
    load_lab = [local(lab_in, lab), local(bp_in, bp)]
    load_wp = local(wp_in, wp)
    load_eg = local(eg_in, eg)
    barrier = pltpu.get_barrier_semaphore()
    friends = [(r, tc), (r, ty), (r, tdiag), (rx, t)] + [(zp, t) for zp in zpeers + xzpeers] + [(gp_, t) for gp_ in gpeers]
    for dev in friends:
        pl.semaphore_signal(barrier, inc=1, device_id=dev, device_id_type=MESH)
    pl.semaphore_wait(barrier, len(friends))

    for c in load_own:
        c.wait()
    shared[t, 0:2, :] = ab[...]
    shared[t, 2:6, :] = bup_own[...]
    bias_moves = [go(remote(shared.at[t], shared.at[t], (r, dev))) for dev in (tc, ty, tdiag)]
    full = {"qkv": wqkv, "wo": wo, "up": wup, "dn": wdn}
    given = {"qkv": wqkv_in, "wo": wo_in, "up": wup_in, "dn": wdn_in}

    def shard(name, s, piece=None):
        ref = full[name]
        if name in ("qkv", "up"):
            rows_ = pl.ds(0, D) if piece is None else pl.ds(piece * (D // 4), D // 4)
            if name == "qkv":
                return ref.at[:, rows_, pl.ds(pl.multiple_of(s * 128, 128), 128)]
            return ref.at[rows_, pl.ds(pl.multiple_of(s * (FF // 4), 128), FF // 4)]
        n = (D if name == "wo" else FF) // 4
        if piece is None:
            return ref.at[pl.ds(s * n, n)]
        return ref.at[pl.ds(s * n + piece * (n // 4), n // 4)]

    def own_piece(name, piece):
        ref = given[name]
        if name == "qkv":
            return ref.at[:, pl.ds(piece * (D // 4), D // 4)]
        n = ref.shape[0] // 4
        return ref.at[pl.ds(piece * n, n)]

    class Gather:
        def __init__(self, name):
            self.name = name
            self.y = remote(own_piece(name, quad), shard(name, t, quad), (r, ty))
            self.c = remote(given[name], shard(name, t), (r, tc))
            self.loc = later(given[name], shard(name, t))
            mine = shard(name, ty, quad)
            self.x = [remote(mine, mine, (dev, t)) for dev in (rx, rz, rxz)]
            self.f = [remote(mine, mine, (r, tc))]
            for dev in (rx, rz, rxz):
                got = shard(name, ty, dev % 4)
                self.f.append(remote(got, got, (r, tc)))
            chain(name, (self.step1, [self.y]), *[(functools.partial(self.step2, i), [self.x[i]]) for i in range(3)])

        def begin(self):
            go(self.y)
            go(self.c)
            self.loc.start()
            live(self.name)

        def step1(self):
            self.y.wait_recv()
            for c in self.x:
                go(c)
            go(self.f[0])

        def step2(self, i):
            self.x[i].wait_recv()
            go(self.f[i + 1])

        def near(self):
            self.loc.wait()
            self.c.wait_recv()

        def ready(self):
            for c in self.f:
                c.wait_recv()

    w_qkv = Gather("qkv")
    w_o = Gather("wo")
    w_up = Gather("up")
    w_dn = Gather("dn")
    for w in (w_qkv, w_o):
        w.begin()

    for c in load_vec + load_lab:
        c.wait()
    vec[0:6, :] = vec_own[...]

    def row(i):
        return vec[i:i + 1, :]

    load_x.wait()

    class Halo:
        def __init__(self, pairs):
            self.left = [remote(a, b, (r, (t + 3) % 4)) for a, b, _, _ in pairs]
            self.right = [remote(c, d, (r, (t + 1) % 4)) for _, _, c, d in pairs]

        def send(self, i):
            pl.when(t > 0)(self.left[i].start)
            pl.when(t < 3)(self.right[i].start)

        def wait(self, i):
            pl.when(t > 0)(self.right[i].wait_recv)
            pl.when(t < 3)(self.left[i].wait_recv)

        def arrivals(self, name):
            for i in range(2):
                chain(name + str(i), (functools.partial(self.wait, i), [self.left[i], self.right[i]]))

        def sent(self):
            for i in range(2):
                pl.when(t > 0)(self.left[i].wait_send)
                pl.when(t < 3)(self.right[i].wait_send)

    HR = RH // 2

    def edges(i, first):
        return nw.at[pl.ds(i * HR, HR), pl.ds(first, HALO)]

    halo = Halo([(edges(i, HALO), edges(i, HALO + LS), edges(i, LS), edges(i, 0)) for i in range(2)])

    halo.arrivals("fore")

    def ln1(b):
        xs = x[pl.ds(b * BT, BT), :].astype(F32)
        unit, _ = normalize(xs)
        out = (unit * row(1) + row(2)).astype(BF)
        nw[pl.ds(b * BR, BR), HALO:HALO + LS, :] = out.reshape(BR, LS, D)

    run("ln1", NB, ln1, {NB // 2 - 1: lambda: (halo.send(0), w_up.begin()), NB - 1: lambda: (halo.send(1), live("fore0", "fore1"))})

    @pl.when(t == 0)
    def _():
        nw[:, 0:HALO, :] = jnp.zeros((RH, HALO, D), BF)

    @pl.when(t == 3)
    def _():
        nw[:, HALO + LS:W, :] = jnp.zeros((RH, HALO, D), BF)

    PH = RH * SEGS // 2
    load_wp.wait()
    load_eg.wait()

    class PoolSum:
        def __init__(self, name, terms, r1, r2, out):
            self.terms, self.r1, self.r2, self.out = terms, r1, r2, out
            mine, theirs = pl.ds(core * PH, PH), pl.ds((1 - core) * PH, PH)
            self.mine = mine
            self.a = remote(terms.at[theirs], r1, (r, tc))
            self.b = remote(terms.at[mine], r2, (r, ty))
            self.c = remote(out.at[mine], out.at[mine], (r, tc))
            chain(name, (self.step2, [self.a]), (self.step3, [self.b]))

        def step1(self):
            go(self.a)

        def step2(self):
            self.a.wait_recv()
            self.terms[self.mine, :] = (self.terms[self.mine, :].astype(F32) + self.r1[...].astype(F32)).astype(BF)
            go(self.b)

        def step3(self):
            self.b.wait_recv()
            self.out[self.mine, :] = (self.terms[self.mine, :].astype(F32) + self.r2[...].astype(F32)).astype(BF)
            go(self.c)

        def ready(self):
            self.c.wait_recv()

    gpool = PoolSum("gpool", gpt, gpr1, gpr2, gps)
    pooled = PoolSum("pooled", pt, pr1, pr2, ps)
    smalls[...] = jnp.zeros(smalls.shape, F32)

    def pool_back():
        smalls[pl.ds(12 + t, 1), :] = total(eg[...].astype(F32))
        gpt[...] = mm_t(eg[...], wp[...]).astype(BF)

    once("pool_back", pool_back)
    gpool.step1()

    load_hg = local(hg_in, hg)
    w_qkv.near()
    live("gpool")
    point()

    labels = lab[...]
    SL = labels.shape[1]
    window = pltpu.roll(labels, (SL + HALO - t * LS) % SL, 1)[:, 0:W].astype(F32)
    own_lab = pltpu.roll(labels, (SL - t * LS) % SL, 1)[:, 0:W].astype(F32)
    before = pltpu.roll(labels, (SL + 1 - t * LS) % SL, 1)[:, 0:W].astype(F32)
    codes[...] = jnp.where(own_lab == before, -1.0, own_lab)
    columns = jnp.transpose(own_lab)
    for i in range(RH):
        mask[i * LS:(i + 1) * LS, :] = jnp.where(columns[0:LS, i:i + 1] == window[i:i + 1, :], 0.0, -1e30)

    for copy in bias_moves:
        copy.wait_recv()
    for s in range(4):
        for i in range(2):
            vec[6 + i:7 + i, s * 128:(s + 1) * 128] = shared[s, i:i + 1, :]
        for i in range(4):
            bup[s:s + 1, i * 128:(i + 1) * 128] = shared[s, 2 + i:3 + i, :]

    point()

    near = pl.ds(pl.multiple_of(ypos * H2, H2), H2)
    far = pl.ds(pl.multiple_of((1 - ypos) * H2, H2), H2)

    def project_own(cols, b):
        own = nw[pl.ds(b * BR, BR), HALO:HALO + LS, :].reshape(BT, D)
        q[pl.ds(b * BT, BT), cols] = ((mm(own, wqkv[0, :, cols]) + vec[6:7, cols]) * (HEAD_DIM ** -0.5)).astype(BF)
        ks = mm(own, wqkv[1, :, cols]).astype(BF)
        vs = (mm(own, wqkv[2, :, cols]) + vec[7:8, cols]).astype(BF)
        k[pl.ds(b * BR, BR), HALO:HALO + LS, cols] = ks.reshape(BR, LS, H2)
        v[pl.ds(b * BR, BR), HALO:HALO + LS, cols] = vs.reshape(BR, LS, H2)

    def project_halo(cols, b):
        rows_ = pl.ds(b * BR, BR)
        both = jnp.concatenate([nw[rows_, 0:HALO, :], nw[rows_, HALO + LS:W, :]], axis=0).reshape(BR * 2 * HALO, D)
        ks = mm(both, wqkv[1, :, cols]).astype(BF).reshape(2, BR, HALO, H2)
        vs = (mm(both, wqkv[2, :, cols]) + vec[7:8, cols]).astype(BF).reshape(2, BR, HALO, H2)
        k[rows_, 0:HALO, cols] = ks[0]
        k[rows_, HALO + LS:W, cols] = ks[1]
        v[rows_, 0:HALO, cols] = vs[0]
        v[rows_, HALO + LS:W, cols] = vs[1]

    lane = lax.broadcasted_iota(jnp.int32, (1, H2), 1) // HEAD_DIM
    heads = [(lane == h).astype(F32).astype(BF) for h in range(4)]

    def spread_heads(block):
        return jnp.concatenate([block * heads[h] for h in range(4)], axis=0)

    def merge_heads(stack):
        parts = [stack[h * LS:(h + 1) * LS, :] for h in range(4)]
        out = jnp.where(lane == 0, parts[0], parts[1])
        out = jnp.where(lane == 2, parts[2], out)
        return jnp.where(lane == 3, parts[3], out)

    def attend(half, cols, i):
        rows4 = [i * 4 + n for n in range(4)]
        scores = []
        for n in rows4:
            m1 = mask[pl.ds(n * LS, LS), :]
            qs = spread_heads(q[pl.ds(n * LS, LS), cols])
            scores.append(mm_t(qs, k[n, :, cols]) + jnp.concatenate([m1] * 4, axis=0))
        tops = [jnp.max(sc, axis=-1, keepdims=True) for sc in scores]
        es = [jnp.exp(sc - top) for sc, top in zip(scores, tops)]
        inv = [1.0 / jnp.sum(e, axis=-1, keepdims=True) for e in es]
        ws = [(e * f).astype(BF) for e, f in zip(es, inv)]
        outs = []
        for n, w in zip(rows4, ws):
            p[pl.ds((n * 2 + half) * 4 * LS, 4 * LS), :] = w
            outs.append(mm(w, v[n, :, cols]))
        for n, o in zip(rows4, outs):
            at[pl.ds(n * LS, LS), cols] = merge_heads(o).astype(BF)

    HB = NB // 2
    AB = RH // 8
    run("own_near", NB, lambda b: project_own(near, b))
    w_dn.begin()
    must("fore0")
    run("halo_near", HB, lambda b: project_halo(near, b))
    run("attend", AB, lambda i: attend(ypos, near, i))
    must("fore1")
    run("halo_near", HB, lambda b: project_halo(near, b + HB))
    run("attend", AB, lambda i: attend(ypos, near, i + AB))
    must("qkv")
    w_qkv.ready()
    run("own_far", NB, lambda b: project_own(far, b))
    run("halo_far", NB, lambda b: project_halo(far, b))
    run("attend", 2 * AB, lambda i: attend(1 - ypos, far, i))
    ids = lax.broadcasted_iota(jnp.int32, (SEGS, LS), 0).astype(F32)

    def chosen(n):
        return (ids == codes[pl.ds(n, 1), 0:LS]).astype(F32).astype(BF)

    must("gpool")
    gpool.ready()
    load_hg.wait()

    def place(b):
        rows_ = pl.ds(b * BT, BT)
        put = [t_mm(chosen(b * BR + n), gps[pl.ds((b * BR + n) * SEGS, SEGS), :]) for n in range(BR)]
        g = hg[rows_, :].astype(F32) + jnp.concatenate(put, axis=0)
        low = g.astype(BF)
        hg[rows_, :] = low
        smalls[5:6, :] += total(low.astype(F32))

    run("place", NB, place)

    must("wo", "up")
    for w in (w_o, w_up):
        w.near()
        w.ready()

    FC = FF // 4
    def feed_up(b):
        rows_ = pl.ds(b * BT, BT)
        middle = x[rows_, :].astype(F32) + (mm(at[rows_, :], wo[...]) + row(0))
        mid[rows_, :] = middle
        unit, _ = normalize(middle)
        normed = (unit * row(3) + row(4)).astype(BF)
        nf[rows_, :] = normed
        for j in range(4):
            cols = slice(j * FC, (j + 1) * FC)
            u = mm(normed, wup[:, cols]) + bup[j:j + 1, :]
            u2 = u * u
            th = jnp.tanh(u * (ROOT + (ROOT * CUBE) * u2))
            half_up = 0.5 + 0.5 * th
            a = u * half_up
            act[rows_, cols] = a.astype(BF)
            dact[rows_, cols] = (half_up + (a - a * half_up) * (2.0 * ROOT + (6.0 * CUBE * ROOT) * u2)).astype(BF)

    def feed_down(b):
        rows_ = pl.ds(b * BT, BT)
        low = (mid[rows_, :] + (mm(act[rows_, :], wdn[...]) + row(5))).astype(BF)
        hid[rows_, :] = low
        for n in range(BR):
            first = chosen(b * BR + n)
            pt[pl.ds((b * BR + n) * SEGS, SEGS), :] = mm(first, low[n * LS:(n + 1) * LS, :]).astype(BF)

    run("feed_up", NB, feed_up)
    gb = hg

    mine = {"y": ypos, "h": zh, "l": zl, "x": xpos}
    partner = {"y": (r, ty), "h": (z2, t), "l": (z1, t), "x": (rx, t)}
    own_part = (zh, zl, xpos)

    class Reduce:
        def __init__(self, name, g, r1, bufs, o):
            self.name, self.g, self.r1, self.bufs, self.o = name, g, r1, bufs, o
            axes = "hlx" if r1 is None else "yhlx"
            lead = () if r1 is None else (core,)
            over, gather = ORDERS[name]

            def at(fixed, flip=""):
                return tuple(1 - mine[a] if a == flip else mine[a] if a in fixed else slice(None) for a in axes)

            def peer(dz):
                z = (zpos + dz) % 4
                return (z // 2, z % 2, xpos)

            near_copies = []
            if r1 is not None:
                self.a1 = remote(g.at[1 - core, 1 - ypos], r1.at[1 - ypos], (r, tc))
                self.a2 = remote(g.at[1 - core, ypos], r1.at[ypos], (r, tc))
                near_copies = [self.a1] if over[0] == "y" else [self.a1, self.a2]
            moves, fixed, regions = [], "", []
            for i, d in enumerate(over):
                if d == "Z":
                    tail_at = at(fixed)[:-3] + ()
                    moves.append([remote(g.at[lead + tail_at + peer(dz)], bufs[i].at[dz - 1], (zpeers[dz - 1], t)) for dz in (1, 2, 3)])
                    fixed += "hl"
                else:
                    moves.append([remote(g.at[lead + at(fixed, d)], bufs[i], partner[d])])
                    fixed += d
                regions.append(at(fixed))
            links = [(functools.partial(self.first, lead, at("", over[0]), near_copies, moves[0]), near_copies)]
            for i in range(1, len(over)):
                wait_for = moves[i - 1] + ([self.a2] if r1 is not None and i == 1 and over[0] == "y" else [])
                links.append((functools.partial(self.middle, lead, regions[i - 1], i, wait_for, moves[i]), wait_for))
            gathers, got = [], ""
            for d in gather:
                place_at = tuple(slice(None) if a in got else mine[a] for a in "hlx")
                if d == "Z":
                    gathers.append([remote(o.at[place_at], o.at[place_at], (zpeers[dz - 1], t)) for dz in (1, 2, 3)])
                    got += "hl"
                else:
                    gathers.append([remote(o.at[place_at], o.at[place_at], partner[d])])
                    got += d
            if groups > 1:
                self.m = [remote(o.at[own_part], r5[name].at[i], (gpeers[i], t)) for i in range(groups - 1)]
            links.append((functools.partial(self.last, lead, regions[-1], over[-1] == "Z", moves[-1], gathers[0]), moves[-1]))
            for i in range(1, len(gather)):
                links.append((functools.partial(self.gather, gathers[i - 1], gathers[i]), gathers[i - 1]))
            links.append((functools.partial(self.finish, gathers[-1]), gathers[-1]))
            self.save = later(o, final[name])
            chain(name, *links)

        def core1(self):
            go(self.a1)

        def core2(self):
            go(self.a2)

        def first(self, lead, region, awaited, moves):
            for c in awaited:
                c.wait_recv()
            if self.r1 is not None:
                self.g[lead + region] = (self.g[lead + region].astype(F32) + self.r1[region].astype(F32)).astype(BF)
            go(moves[0])

        def middle(self, lead, region, i, awaited, moves):
            for c in awaited:
                c.wait_recv()
            acc = self.g[lead + region].astype(F32) + self.bufs[i - 1][...].astype(F32)
            if self.r1 is not None and i == 1:
                acc = acc + self.r1[region].astype(F32)
            self.g[lead + region] = acc.astype(BF)
            for c in moves:
                go(c)

        def last(self, lead, region, direct, awaited, moves):
            acc = self.g[lead + region].astype(F32)
            for i, c in enumerate(awaited):
                c.wait_recv()
                acc = acc + (self.bufs[-1][i] if direct else self.bufs[-1][...]).astype(F32)
            self.o[own_part] = acc.astype(BF)
            if groups > 1:
                for c in self.m:
                    c.start()
                for c in self.m:
                    c.wait()
                acc = self.o[own_part].astype(F32)
                for i in range(groups - 1):
                    acc = acc + r5[self.name][i].astype(F32)
                self.o[own_part] = acc.astype(BF)
            for c in moves:
                go(c)

        def gather(self, awaited, moves):
            for c in awaited:
                c.wait_recv()
            for c in moves:
                go(c)

        def finish(self, awaited):
            for c in awaited:
                c.wait_recv()
            store(self.save)

    HC = D // 2

    def halves(out, i):
        return out.at[:, :, :, :, pl.ds(i * HC, HC)]

    final = {"dna": halves(gdn_out, 0), "dnb": halves(gdn_out, 1), "upa": halves(gup_out, 0), "upb": halves(gup_out, 1),
             "o": go_out, "q": gq_out, "k": gk_out, "v": gv_out, "pl": gpl_out}
    stores = []
    red = {}
    for name in NAMES:
        held = sets[name]
        if name == "pl":
            held = [held[0], None] + held[1:]
        red[name] = Reduce(name, held[0], held[1], held[2:-1], held[-1])

    def split(names, cs, ys, val):
        for i, name in enumerate(names):
            g = sets[name][0]
            g[cs, ys] = val[:, i * HC:(i + 1) * HC].astype(BF).reshape(g.shape[2:])

    def place_of(i):
        return (core + 1 + i // 2) % 2, (ypos + 1 + i) % 2

    def down_grad(i):
        cs, ys = place_of(i)
        val = t_mm(act[:, pl.ds(pl.multiple_of((ys * 2 + cs) * FC, FC), FC)], gb[...])
        split(("dna", "dnb"), cs, ys, val)

    def near_cores(*names):
        return lambda: [red[n].core1() for n in names], lambda: [red[n].core2() for n in names]

    send1, send2 = near_cores("dna", "dnb")
    run("down_grad", 4, down_grad, {0: send1, 1: send2, 2: lambda: live("dnb"), 3: lambda: live("dna")})
    must("dn")
    w_dn.near()
    w_dn.ready()
    run("feed_down", NB, feed_down)
    store_hid = local(hid, hid_out)
    pooled.step1()
    live("pooled")

    def feed_back(b):
        rows_ = pl.ds(b * BT, BT)
        g = gb[rows_, :]
        acc = jnp.zeros((BT, D), F32)
        for j in range(4):
            cols = slice(j * FC, (j + 1) * FC)
            ga = mm_t(g, wdn[cols, :])
            gp = (ga * dact[rows_, cols].astype(F32)).astype(BF)
            dact[rows_, cols] = gp
            smalls[8 + j:9 + j, :] += total(gp.astype(F32))
            acc = acc + mm_t(gp, wup[:, cols])
        unit, factor = normalize(mid[rows_, :])
        smalls[3:4, :] += total(acc * unit)
        smalls[4:5, :] += total(acc)
        gm = g.astype(F32) + norm_back(acc, unit, factor, row(3))
        mid[rows_, :] = gm
        low = gm.astype(BF)
        gma[rows_, :] = low
        smalls[0:1, :] += total(low.astype(F32))
        gat[rows_, :] = mm_t(low, wo[...]).astype(BF)

    run("feed_back", NB, feed_back)
    def up_grad(i):
        cs, ys = place_of(i)
        val = t_mm(nf[...], dact[:, pl.ds(pl.multiple_of((ys * 2 + cs) * FC, FC), FC)])
        split(("upa", "upb"), cs, ys, val)

    send3, send4 = near_cores("upa", "upb")
    run("up_grad", 4, up_grad, {0: send3, 1: send4, 2: lambda: live("upb"), 3: lambda: live("upa")})

    def out_grad():
        val = t_mm(at[...], gma[...]).astype(BF)
        for s in range(4):
            g = sets["o"][0]
            g[s % 2, s // 2] = val[s * (D // 4):(s + 1) * (D // 4), :].reshape(g.shape[2:])
        red["o"].core1()
        red["o"].core2()
        live("o")

    late[...] = jnp.zeros(late.shape, F32)

    class Small:
        name = "sm"

        def __init__(self):
            self.save = later(smalls, sm_out)
            self.copies = [[remote(smalls, sm_r.at[0], (r, tc))], [remote(smalls, sm_r.at[1], (r, ty))],
                           [remote(smalls, sm_r.at[2], (rx, t))],
                           [remote(smalls, sm_r.at[2 + dz], (zpeers[dz - 1], t)) for dz in (1, 2, 3)]]
            chain("sm", *[(functools.partial(self.step, i), self.copies[i]) for i in range(4)])

        def send(self, i):
            for c in self.copies[i]:
                c.start()

        def step(self, i):
            for c in self.copies[i]:
                c.wait()
            if i < 3:
                smalls[...] += sm_r[i]
                self.send(i + 1)
            else:
                smalls[...] += sm_r[3] + sm_r[4] + sm_r[5]
                across(smalls, "sm")
                store(self.save)

    class Late:
        name = "late"

        def __init__(self):
            self.save = later(late, late_out)
            self.a = [remote(late, late_tp.at[i], (r, dev)) for i, dev in enumerate((tc, ty, tdiag))]
            self.b = [remote(late, late_rows.at[i], (dev, t)) for i, dev in enumerate([rx] + zpeers + xzpeers)]
            chain("late", (self.over_tp, self.a), (self.over_rows, self.b))

        def over_tp(self):
            for c in self.a:
                c.wait()
            late[...] += late_tp[0] + late_tp[1] + late_tp[2]
            for c in self.b:
                c.start()

        def over_rows(self):
            for c in self.b:
                c.wait()
            for i in range(7):
                late[...] += late_rows[i]
            across(late, "late")
            store(self.save)

    def across(ref, name):
        moves = [remote(ref, r5[name].at[i], (gpeers[i], t)) for i in range(groups - 1)]
        for c in moves:
            c.start()
        for c in moves:
            c.wait()
        for i in range(groups - 1):
            ref[...] += r5[name][i]

    small, lates = Small(), Late()
    small.send(0)
    live("sm")
    once("out_grad", out_grad)

    must("pooled")
    pooled.ready()

    def embed():
        sets["pl"][0][...] = t_mm(ps[...], eg[...]).astype(BF).reshape(sets["pl"][0].shape)
        live("pl")

    once("embed", embed)

    def attend_back(i):
        work = [(i * 2 + n, half) for n in range(2) for half in range(2)]
        sides = [slice(half * H2, (half + 1) * H2) for _, half in work]
        qss = [spread_heads(q[pl.ds(n * LS, LS), c]) for (n, _), c in zip(work, sides)]
        gss = [spread_heads(gat[pl.ds(n * LS, LS), c]) for (n, _), c in zip(work, sides)]
        ws = [p[pl.ds((n * 2 + half) * 4 * LS, 4 * LS), :] for n, half in work]
        gws = [mm_t(g, v[n, :, c]) for g, (n, _), c in zip(gss, work, sides)]
        wfs = [w.astype(F32) for w in ws]
        prods = [w * g for w, g in zip(wfs, gws)]
        sums = [jnp.sum(pr, axis=-1, keepdims=True) for pr in prods]
        dss = [(pr - w * sm).astype(BF) for pr, w, sm in zip(prods, wfs, sums)]
        dvs = [t_mm(w, g).astype(BF) for w, g in zip(ws, gss)]
        dqs = [mm(ds, k[n, :, c]) for ds, (n, _), c in zip(dss, work, sides)]
        dks = [t_mm(ds, qq).astype(BF) for ds, qq in zip(dss, qss)]
        for (n, _), c, dq, dk, dv in zip(work, sides, dqs, dks, dvs):
            q[pl.ds(n * LS, LS), c] = (merge_heads(dq) * (HEAD_DIM ** -0.5)).astype(BF)
            k[n, :, c] = dk
            v[n, :, c] = dv

    run("attend_back", RH // 2, attend_back)

    back = Halo([tuple(ref.at[pl.ds(i * HR, HR)] for ref in (halo_l, halo_fr, halo_r, halo_fl)) for i in range(2)])
    back.arrivals("back")

    def norm_grad(b):
        keys = pl.ds(b * BR, BR)
        dqs = q[pl.ds(b * BT, BT), :]
        dks, dvs = k[keys].reshape(BR * W, D), v[keys].reshape(BR * W, D)
        late[2:3, :] += total(dqs.astype(F32))
        late[3:4, :] += total(dvs.astype(F32))
        win = (mm_t(dks, wqkv[1]) + mm_t(dvs, wqkv[2])).reshape(BR, W, D)
        own = win[:, HALO:HALO + LS, :].reshape(BT, D) + mm_t(dqs, wqkv[0])
        gat[pl.ds(b * BT, BT), :] = own.astype(BF)
        halo_l[keys] = win[:, 0:HALO, :].astype(BF)
        halo_r[keys] = win[:, HALO + LS:W, :].astype(BF)

    def put_at(g, val):
        low = val.astype(BF)
        for s in range(4):
            g[s % 2, s // 2] = low[:, s * 128:(s + 1) * 128].reshape(g.shape[2:])

    def put_value():
        put_at(sets["v"][0], t_mm(nw[...].reshape(RH * W, D), v[...].reshape(RH * W, D)))
        red["v"].core1()
        red["v"].core2()
        live("v")

    def put_key():
        put_at(sets["k"][0], t_mm(nw[...].reshape(RH * W, D), k[...].reshape(RH * W, D)))
        red["k"].core1()
        red["k"].core2()
        live("k")

    def put_query():
        put_at(sets["q"][0], t_mm(nw[:, HALO:HALO + LS, :].reshape(T, D), q[...]))
        red["q"].core1()
        red["q"].core2()
        live("q")

    once("put_v", put_value)
    once("put_k", put_key)
    once("put_q", put_query)
    run("norm_grad", NB, norm_grad, {HB - 1: lambda: back.send(0), NB - 1: lambda: (back.send(1), live("back0", "back1"))})

    @pl.when(t == 0)
    def _():
        halo_fl[...] = jnp.zeros(halo_fl.shape, BF)

    @pl.when(t == 3)
    def _():
        halo_fr[...] = jnp.zeros(halo_fr.shape, BF)


    def ln1_back(b):
        rows_ = pl.ds(b * BT, BT)
        grp = pl.ds(b * BR, BR)
        g = gat[rows_, :].astype(F32).reshape(BR, LS, D)
        g = jnp.concatenate([g[:, 0:HALO, :] + halo_fl[grp].astype(F32), g[:, HALO:LS, :] + halo_fr[grp].astype(F32)], axis=1)
        g = g.reshape(BT, D)
        unit, factor = normalize(x[rows_, :].astype(F32))
        late[0:1, :] += total(g * unit)
        late[1:2, :] += total(g)
        nf[rows_, :] = (mid[rows_, :] + norm_back(g, unit, factor, row(1))).astype(BF)

    must("back0")
    run("ln1_back", HB, ln1_back)
    def embed_out():
        emb[...] = (mm(ps[...], wp[...]) + bp[...].reshape(1, D)).astype(BF)

    once("embed_out", embed_out)
    store_emb = local(emb, emb_out)
    must("back1")
    run("ln1_back", HB, lambda b: ln1_back(b + HB))
    store_ig = local(nf, ig_out)
    for c in lates.a:
        c.start()
    live("late")
    must(*NAMES, "sm", "late")
    for c in pending:
        c.wait_send()
    halo.sent()
    back.sent()
    for c in stores + [store_hid, store_emb, store_ig]:
        c.wait()


def per_device(rows_size, layer_input, segment_labels, attend_weight, attend_bias, out_weight, out_bias, gain_attention,
               shift_attention, gain_feed, shift_feed, up_weight, up_bias, down_weight, down_bias, pool_weight, pool_bias,
               hidden_grad, embedding_grad):
    RH, LS, D = layer_input.shape
    SEGS = embedding_grad.shape[1]
    OC = pool_weight.shape[1]
    FS = up_weight.shape[1]
    FF = FS * 4
    W = LS + 2 * HALO
    T = RH * LS
    NB = RH // 8
    groups = rows_size // 8
    t = lax.axis_index("tp")
    part = (D // 8, D // 4)
    chunk = {"dna": (FS // 8, D // 2), "dnb": (FS // 8, D // 2), "upa": (D // 8, FS // 2), "upb": (D // 8, FS // 2), "o": (D // 32, D), "q": part, "k": part, "v": part, "pl": (D // 8, OC)}
    any_, vmem = pl.BlockSpec(memory_space=pl.ANY), pl.BlockSpec(memory_space=pltpu.VMEM)

    def buf(*shape, dtype=BF):
        return pltpu.VMEM(shape, dtype)

    scratch = [
        pltpu.VMEM(segment_labels.shape, jnp.int32), buf(2, D // 4, dtype=F32), buf(4, FS // 4, dtype=F32), buf(OC, dtype=F32), buf(6, D, dtype=F32),
        buf(T, D), buf(T, D), buf(RH * SEGS, OC), buf(T, W, dtype=F32), buf(RH, W, dtype=F32),
        buf(3, D, D), buf(D, D), buf(D, FF), buf(FF, D), buf(D, OC), buf(4, 8, 128, dtype=F32), buf(8, D, dtype=F32), buf(4, FS, dtype=F32),
        buf(RH, W, D), buf(T, D), buf(RH, W, D), buf(RH, W, D), buf(RH * 2 * 4 * LS, W), buf(T, D), buf(T, D, dtype=F32),
        buf(T, D), buf(T, FF), buf(T, FF), buf(T, D), buf(T, D), buf(T, D),
        buf(RH, HALO, D), buf(RH, HALO, D), buf(RH, HALO, D), buf(RH, HALO, D),
    ]
    for _ in range(2):
        scratch += [buf(RH * SEGS, D), buf(RH * SEGS // 2, D), buf(RH * SEGS // 2, D), buf(RH * SEGS, D)]
    scratch += [buf(RH * SEGS, OC), buf(16, D, dtype=F32), buf(6, 16, D, dtype=F32), buf(4, D, dtype=F32), buf(3, 4, D, dtype=F32), buf(7, 4, D, dtype=F32)]
    for name in NAMES:
        c, over = chunk[name], ORDERS[name][0]
        left = 3 if name == "pl" else 4
        scratch += [buf(*[2] * 3, *c)] if name == "pl" else [buf(2, *[2] * 4, *c), buf(*[2] * 4, *c)]
        for i, d in enumerate(over):
            scratch.append(buf(3, *c) if d == "Z" else buf(*[2] * (left - 1 - i), *c))
        scratch.append(buf(2, 2, 2, *c))
    if groups > 1:
        scratch += [buf(groups - 1, *chunk[name]) for name in NAMES]
        scratch += [buf(groups - 1, 16, D, dtype=F32), buf(groups - 1, 4, D, dtype=F32)]
    n_remote = 4 * 9 + 3 + 8 + 6 + 9 * 11 + 6 + 10 + 11 * (groups - 1)
    scratch += [pltpu.SemaphoreType.DMA((n_remote,)), pltpu.SemaphoreType.DMA((n_remote,)), pltpu.SemaphoreType.DMA((48,))]

    def out(*shape, dtype=BF):
        return jax.ShapeDtypeStruct(shape, dtype)

    flops = 30 * T * D * FF
    hid, emb, ig, gdn, gup, go_, gq, gk, gv, gpl, sm, late = pl.pallas_call(
        functools.partial(layer_kernel, (groups, RH, LS, D, FF, SEGS)),
        out_shape=[out(T, D), out(RH * SEGS, OC), out(T, D)]
        + [out(2, 2, 2, FS // 8, D), out(2, 2, 2, D // 8, FS)] + [out(2, 2, 2, *chunk[name]) for name in ("o", "q", "k", "v", "pl")]
        + [out(16, D, dtype=F32), out(4, D, dtype=F32)],
        in_specs=[any_] * 18,
        out_specs=[any_] * 12,
        scratch_shapes=scratch,
        compiler_params=pltpu.CompilerParams(collective_id=0, has_side_effects=True, vmem_limit_bytes=63 * 2 ** 20),
        cost_estimate=pl.CostEstimate(flops=flops, bytes_accessed=20 * 2 ** 20, transcendentals=T * FF),
        name="layer",
    )(layer_input.reshape(T, D), segment_labels, attend_weight, attend_bias, out_weight, out_bias, gain_attention,
      shift_attention, gain_feed, shift_feed, up_weight, up_bias.reshape(4, FS // 4), down_weight, down_bias,
      pool_weight, pool_bias, hidden_grad.reshape(T, D), embedding_grad.reshape(RH * SEGS, OC))

    grads = [gq, gk, gv, go_, gup, gdn, gpl]
    flat = [(D, D // 4)] * 3 + [(D // 4, D), (D, FS), (FS, D), (D, OC)]
    grads = [g.reshape(shape) for g, shape in zip(grads, flat)]
    whole = [hid.reshape(RH, LS, D), emb.reshape(RH, SEGS, OC), ig.reshape(RH, LS, D)]
    vecs = [D] * 6 + [FS, OC]
    made = pl.pallas_call(
        last_kernel,
        out_shape=[out(*w.shape) for w in whole] + [out(3, D, D // 4, dtype=F32)] + [out(*shape, dtype=F32) for shape in flat[3:]]
        + [out(2, D // 4, dtype=F32)] + [out(n, dtype=F32) for n in vecs],
        in_specs=[any_] * 12,
        out_specs=[any_] * 17,
        scratch_shapes=[buf(*shape) for shape in flat] + [buf(*shape, dtype=F32) for shape in flat]
        + [buf(*w.shape) for w in whole] + [buf(16, D, dtype=F32), buf(4, D, dtype=F32), pltpu.SemaphoreType.DMA((31,))],
        compiler_params=pltpu.CompilerParams(vmem_limit_bytes=60 * 2 ** 20),
        cost_estimate=pl.CostEstimate(flops=T * D, bytes_accessed=11 * 2 ** 20, transcendentals=0),
        name="last",
    )(*whole, *grads, sm, late)
    hid, emb, ig, gat, go_, gup, gdn, gpl, gab, gob, ga, sa, gf, sf, gdb, gub, gpb = made
    return (hid, emb, ig, gat, gab, go_, gob, ga, sa, gf, sf, gup, gub, gdn, gdb, gpl, gpb)


def last_kernel(*refs):
    whole_in, grads_in, small_in, refs = refs[:3], refs[3:10], refs[10:12], refs[12:]
    whole_out, (at_out, *rest), (gab, *vec_out), refs = refs[:3], refs[3:8], refs[8:17], refs[17:]
    low, wide, held, (sm, late, sems) = refs[:7], refs[7:14], refs[14:17], refs[17:]
    t = lax.axis_index("tp")
    number = [0]

    def copy(src, dst):
        c = pltpu.make_async_copy(src, dst, sems.at[number[0]])
        number[0] += 1
        c.start()
        return c

    loads = [copy(a, b) for a, b in zip(whole_in, held)]
    copies = [copy(a, b) for a, b in zip(grads_in, low)]
    small = [copy(a, b) for a, b in zip(small_in, (sm, late))]
    targets = [at_out.at[0], at_out.at[1], at_out.at[2]] + rest
    stores = []
    for i, c in enumerate(loads):
        c.wait()
        stores.append(copy(held[i], whole_out[i]))
    for i in (4, 5, 6, 3, 0, 1, 2):
        copies[i].wait()
        wide[i][...] = low[i][...].astype(F32)
        stores.append(copy(wide[i], targets[i]))
    for c in small:
        c.wait()
    n = gab.shape[1]
    stores.append(copy(late.at[2:4, pl.ds(pl.multiple_of(t * n, 128), n)], gab))
    rows = [sm.at[0], late.at[0], late.at[1], sm.at[3], sm.at[4], sm.at[5], sm.at[8 + t], sm.at[12 + t]]
    stores += [copy(a, b) for a, b in zip(rows, vec_out)]
    for c in stores:
        c.wait()


def solution(mesh):
    placed = (
        P("rows", "tp", None), P("rows", None), P(None, None, "tp"), P(None, "tp"), P("tp", None), P(), P(), P(), P(), P(),
        P(None, "tp"), P("tp"), P("tp", None), P(), P(None, "tp"), P("tp"), P("rows", "tp", None), P("rows", None, "tp"),
    )
    return jax.shard_map(
        functools.partial(per_device, mesh.shape["rows"]),
        mesh=mesh,
        in_specs=placed,
        out_specs=(
            P("rows", "tp", None), P("rows", None, "tp"), P("rows", "tp", None), P(None, None, "tp"), P(None, "tp"),
            P("tp", None), P(), P(), P(), P(), P(), P(None, "tp"), P("tp"), P("tp", None), P(), P(None, "tp"), P("tp"),
        ),
        check_vma=False,
    )
```
